512 devices in a mesh: tm: 32 (over z, core), row: 16 (over y, x).
Axes of the slice: x: 4, y: 4, z: 16, core: 2. Of those that a mesh axis runs over, the one named last changes fastest.
Arguments:
- covariance: float32 [32, 1024, 1024], P('tm', 'row'), as said below
- precision: float32 [32, 1024, 1024], P('tm', 'row'), as said below
- band_weight: float32 [32, 5, 1024], P('tm'), may hold values from -0.5 to 0.5
- band_offset: int32 [32, 5], P('tm'), may hold values from -64 to 64, as said below
- prior_mean: float32 [32, 1024], P('tm', 'row'), may hold values from -6 to 6
- innovation: float32 [32, 128], P('tm'), may hold values from -6 to 6
- seen_sites: int32 [32, 128], P('tm'), may hold values from 0 to 511, as said below
Outputs:
- smoother_gain: float32 [32, 1024, 1024], P('tm', 'row')
- smoother_shift: float32 [32, 1024], P('tm', 'row')
- smoother_spread: float32 [32, 1024, 1024], P('tm', 'row')
The draws below stay inside these ranges and needn't reach their ends.
Inputs may be any that keep to these rules, and one draw needn't show every extreme that they name: `covariance`: each block's matrix is symmetric. `precision`: each block's matrix is symmetric. `band_offset`: the offsets of one block are distinct, and one of them has magnitude 64. `seen_sites`: the sites of one step are distinct.
All inputs are finite; a program needn't handle non-finite values.
Results may differ from the reference program's by a relative error of at most 0.0003.
Values sent between devices are 32-bit elements; how exact they have to be, the bound alone decides.
No kernel may reach another device: no remote copies, remote signals or barrier semaphores. Data moves between devices by JAX's collectives and lax.ppermute only.
A program may use at most 64 MiB of HBM per device.

```python
import math
import jax
import jax.numpy as jnp
from jax import lax

SITES = 512
STATE = 1024
NBAND = 5
REACH = 64
OBS = 128
TBLOCKS = 32


def symmetric_draw(key, lowest, highest, mixing):
    first_key, second_key = jax.random.split(key, 2)
    raw_entries = jax.random.uniform(first_key, (TBLOCKS, STATE, STATE), jnp.float32, -1.0, 1.0)
    mixed = (raw_entries + jnp.swapaxes(raw_entries, 1, 2)) * (mixing / math.sqrt(STATE))
    diagonal = jax.random.uniform(second_key, (TBLOCKS, STATE), jnp.float32, lowest, highest)
    matrix = mixed + diagonal[:, :, None] * jnp.eye(STATE, dtype=jnp.float32)[None, :, :]
    return matrix


def draw_covariance(key, part):
    key = jax.random.fold_in(key, 11)
    return symmetric_draw(key, 0.5, 1.0, 0.25)


def draw_precision(key, part):
    key = jax.random.fold_in(key, 12)
    return symmetric_draw(key, 0.5, 1.0, 0.25)


def shuffle_row(row_key, values):
    return jax.random.permutation(row_key, values)


def draw_band_offset(key, part):
    key = jax.random.fold_in(key, 13)
    sign_key, pick_key, order_key = jax.random.split(key, 3)
    signs = jax.random.randint(sign_key, (TBLOCKS,), 0, 2).astype(jnp.int32)
    choices_pool = jnp.arange(2 * REACH, dtype=jnp.int32)[None, :] - REACH + signs[:, None]
    picked = jax.vmap(shuffle_row)(jax.random.split(pick_key, TBLOCKS), choices_pool)[:, :NBAND - 1]
    extreme = REACH * (1 - 2 * signs)
    joined = jnp.concatenate([extreme[:, None], picked], axis=1)
    orders = jax.vmap(shuffle_row)(jax.random.split(order_key, TBLOCKS), jnp.broadcast_to(jnp.arange(NBAND, dtype=jnp.int32), (TBLOCKS, NBAND)))
    return jnp.take_along_axis(joined, orders, axis=1).astype(jnp.int32)


def draw_seen_sites(key, part):
    key = jax.random.fold_in(key, 14)
    every_site = jnp.broadcast_to(jnp.arange(SITES, dtype=jnp.int32), (TBLOCKS, SITES))
    shuffled = jax.vmap(shuffle_row)(jax.random.split(key, TBLOCKS), every_site)
    return shuffled[:, :OBS].astype(jnp.int32)


def block_scale(stream_key, dims, pieces, low, high):
    level, own = 1.0, jax.random.fold_in(stream_key, 6)
    for position, parts in pieces:
        heights = jnp.exp(jax.random.uniform(jax.random.fold_in(own, position), (parts,), jnp.float32, low / len(pieces), high / len(pieces)))
        level = level * jnp.repeat(heights, dims[position] // parts).reshape([-1 if axis == position else 1 for axis in range(len(dims))])
    return level


def centred(key, shape, scale, bound, cuts=(), kind=jnp.bfloat16):
    loudness = block_scale(key, shape, cuts, -0.22, 0.18) if cuts else 1.0
    values = jax.random.normal(key, shape, jnp.float32) * scale * loudness
    return jnp.minimum(jnp.maximum(values, -bound), bound).astype(kind)


def setup_inputs(seed: int = 0) -> dict:
    key_list = jax.random.split(jax.random.key(seed), 8)
    return {
        "covariance": draw_covariance(jax.random.fold_in(key_list[7], 71), 0),
        "precision": draw_precision(jax.random.fold_in(key_list[7], 71), 0),
        "band_weight": jnp.clip(jax.random.uniform(key_list[2], (TBLOCKS, NBAND, STATE), jnp.float32, -0.5, 0.5) * block_scale(key_list[2], (TBLOCKS, NBAND, STATE), ((0, 32),), -0.4, 0.0), -0.5, 0.5),
        "band_offset": draw_band_offset(jax.random.fold_in(key_list[7], 71), 0),
        "prior_mean": centred(key_list[4], (TBLOCKS, STATE), 1.0, 6.0, ((0, 32), (1, 16)), jnp.float32),
        "innovation": centred(key_list[5], (TBLOCKS, OBS), 1.0, 6.0, ((0, 32),), jnp.float32),
        "seen_sites": draw_seen_sites(jax.random.fold_in(key_list[7], 71), 0),
    }


HIGHEST = lax.Precision.HIGHEST


def product(left, right):
    return jnp.dot(left, right, precision=HIGHEST, preferred_element_type=jnp.float32)


def against(left, right):
    return lax.dot_general(left, right, (((1,), (1,)), ((), ())), precision=HIGHEST, preferred_element_type=jnp.float32)


def band_columns(matrix, weights, offsets):
    columns = matrix.shape[1]
    padded = jnp.pad(matrix, ((0, 0), (REACH, REACH)))
    summed = jnp.zeros(matrix.shape, jnp.float32)
    for band_index in range(NBAND):
        start_at = (offsets[band_index] + REACH).astype(jnp.int32)
        sliced = lax.dynamic_slice_in_dim(padded, start_at, columns, 1)
        summed = summed + weights[band_index][None, :] * sliced
    return summed


def band_vector(vector, weights, offsets):
    padded = jnp.pad(vector, (REACH, REACH))
    summed = jnp.zeros(vector.shape, jnp.float32)
    for band_index in range(NBAND):
        start_at = (offsets[band_index] + REACH).astype(jnp.int32)
        summed = summed + weights[band_index] * lax.dynamic_slice_in_dim(padded, start_at, STATE, 0)
    return summed


def element(inputs):
    matrix, inverse, weights, offsets, mean_block, innov_block, site_block = inputs
    crossed = band_columns(matrix, weights, offsets)
    gain = product(crossed, inverse)
    spread = matrix - against(crossed, gain)
    matches = (site_block[:, None] == jnp.arange(STATE, dtype=jnp.int32)[None, :]).astype(jnp.float32)
    pulled = product(innov_block, matches)
    filtered = mean_block + product(matrix, pulled)
    forward = band_vector(filtered, weights, offsets)
    shift = filtered - product(gain, forward)
    return gain, shift, spread


def combine(first_gain, first_shift, first_spread, later_gain, later_shift, later_spread):
    merged_gain = product(first_gain, later_gain)
    merged_shift = product(first_gain, later_shift) + first_shift
    merged_spread = against(product(first_gain, later_spread), first_gain) + first_spread
    return merged_gain, merged_shift, merged_spread


def reference(covariance, precision, band_weight, band_offset, prior_mean, innovation, seen_sites):
    gains, shifts, spreads = lax.map(element, (covariance, precision, band_weight, band_offset, prior_mean, innovation, seen_sites))
    for stride in (1, 2):
        def level(block):
            later = jnp.minimum(block + stride, TBLOCKS - 1)
            merged = combine(gains[block], shifts[block], spreads[block], gains[later], shifts[later], spreads[later])
            inside = block + stride < TBLOCKS
            return (jnp.where(inside, merged[0], gains[block]),
                    jnp.where(inside, merged[1], shifts[block]),
                    jnp.where(inside, merged[2], spreads[block]))
        gains, shifts, spreads = lax.map(level, jnp.arange(TBLOCKS, dtype=jnp.int32))
    return gains, shifts, spreads
```

```python
import jax
import jax.numpy as jnp
from jax import lax
from jax.sharding import Mesh, PartitionSpec as P

NBAND = 5
REACH = 64
SIDE = 4

HIGHEST = lax.Precision.HIGHEST
HIGH = lax.Precision.HIGH


def shifted(block, distance):
    count = lax.axis_size("tm")
    return lax.ppermute(block, "tm", [(i + distance, i) for i in range(count - distance)])


def swap(message, axis):
    return lax.all_to_all(message, axis, 0, 0)


def spread_out(message, axis):
    return swap(jnp.broadcast_to(message[None], (SIDE,) + message.shape), axis)


def times(left, right):
    return jnp.dot(left, right, precision=HIGH, preferred_element_type=jnp.float32)


def against(left, right):
    return lax.dot_general(
        left, right, (((1,), (1,)), ((), ())), precision=HIGH, preferred_element_type=jnp.float32
    )


def matvec(matrix, vector):
    return jnp.sum(matrix * vector[None, :], axis=1)


def band_columns(matrix, weights, offsets):
    columns = matrix.shape[-1]
    padded = jnp.pad(matrix, ((0, 0), (REACH, REACH)))
    summed = jnp.zeros(matrix.shape, jnp.float32)
    for band_index in range(NBAND):
        start_at = offsets[band_index] + REACH
        sliced = lax.dynamic_slice_in_dim(padded, start_at, columns, 1)
        summed = summed + weights[band_index][None, :] * sliced
    return summed


def swap_order(array):
    rest = array.shape[1:]
    rows = array.shape[0]
    parts = array.reshape((SIDE, SIDE, rows // (SIDE * SIDE)) + rest)
    return jnp.swapaxes(parts, 0, 1).reshape((rows,) + rest)


def swap_lanes(array):
    rows, columns = array.shape
    parts = array.reshape(rows, SIDE, SIDE, columns // (SIDE * SIDE))
    return jnp.swapaxes(parts, 1, 2).reshape(rows, columns)


def side_by_side(blocks):
    return jnp.concatenate([blocks[i] for i in range(SIDE)], axis=1)


def with_row(block, vector):
    return jnp.concatenate([block, jnp.pad(vector[None, :], ((0, 7), (0, 0)))], axis=0)


def body(covariance, precision, band_weight, band_offset, prior_mean, innovation, seen_sites):
    own = covariance[0]
    inverse = precision[0]
    weights = band_weight[0]
    offsets = band_offset[0]
    rows, columns = own.shape
    panel = SIDE * rows
    at_y = lax.axis_index("y")
    at_x = lax.axis_index("x")
    at_t = lax.axis_index("tm")
    count_t = lax.axis_size("tm")

    crossed = band_columns(own, weights, offsets)
    matches = seen_sites[0][:, None] == jnp.arange(columns, dtype=jnp.int32)[None, :]
    pulled = jnp.sum(jnp.where(matches, innovation[0][:, None], 0.0), axis=0)
    filtered = prior_mean[0] + matvec(own, pulled)

    pieces = own.reshape(rows, SIDE, SIDE, rows).transpose(2, 0, 1, 3).reshape(SIDE, rows, panel)
    message = jnp.concatenate(
        [jnp.broadcast_to(crossed[None], (SIDE, rows, columns)), pieces], axis=2
    )
    got = swap(message, "x").reshape(panel, columns + panel)
    crossed_panel = got[:, :columns]
    own_block = got[:, columns:]
    padded = jnp.pad(filtered, (0, columns - rows))
    got = spread_out(with_row(inverse, padded), "y")
    inverse_panel = got[:, :rows].reshape(panel, columns)
    filtered_mine = got[:, rows, :rows].reshape(panel)
    gain = against(crossed_panel, inverse_panel)

    crossed_mine = lax.all_gather(swap_lanes(crossed), "y", axis=0, tiled=True)
    gain_tall = lax.all_gather(gain, "y", axis=0, tiled=True)
    gain_later = shifted(gain, 1)

    got = spread_out(with_row(gain, filtered_mine), "x")
    gain_wide = side_by_side(got[:, :panel])
    filtered_all = swap_order(got[:, panel].reshape(columns))
    rimmed = jnp.pad(filtered_all, (REACH, REACH))
    forward = jnp.zeros((columns,), jnp.float32)
    for band_index in range(NBAND):
        start_at = offsets[band_index] + REACH
        forward = forward + weights[band_index] * lax.dynamic_slice_in_dim(
            rimmed, start_at, columns, 0
        )
    shift = lax.dynamic_slice_in_dim(filtered_all, at_y * panel, panel, 0) - matvec(
        gain_wide, swap_order(forward)
    )
    spread = own_block - against(gain_wide, crossed_mine)

    later = jnp.concatenate([gain_later, shifted(with_row(spread, shift), 1)], axis=0)
    got = spread_out(later, "y")
    later_gain = swap_order(got[:, :panel].reshape(columns, panel))
    later_spread = swap_order(got[:, panel : 2 * panel].reshape(columns, panel))
    later_shift = swap_order(got[:, 2 * panel].reshape(columns))
    inside = at_t + 1 < count_t
    gain_2 = jnp.where(inside, times(gain_wide, later_gain), gain)
    turned = jnp.where(inside, times(gain_wide, later_spread), 0.0)
    shift_2 = shift + jnp.where(inside, matvec(gain_wide, later_shift), 0.0)
    gain_2_later = shifted(gain_2, 2)
    part = against(swap_order(gain_tall), turned).reshape(SIDE, panel, panel)
    message = jnp.concatenate(
        [part, jnp.broadcast_to(gain_2[None], (SIDE, panel, panel))], axis=1
    )
    got = swap(message, "x")
    spread_2 = spread + jnp.sum(got[:, :panel], axis=0).T
    gain_2_wide = side_by_side(got[:, panel:])

    tall = lax.all_gather(jnp.concatenate([gain_2, gain_2_later], axis=0), "y", axis=0)
    got = spread_out(shifted(with_row(spread_2, shift_2), 2), "y")
    later_spread = swap_order(got[:, :panel].reshape(columns, panel))
    later_shift = swap_order(got[:, panel].reshape(columns))
    inside = at_t + 2 < count_t
    gain_2_tall = tall[:, :panel].reshape(columns, panel)
    later_gain = swap_order(tall[:, panel:].reshape(columns, panel))
    turned = jnp.where(inside, times(gain_2_wide, later_spread), 0.0)
    gain_4 = jnp.where(inside, times(gain_2_wide, later_gain), gain_2)
    shift_4 = shift_2 + jnp.where(inside, matvec(gain_2_wide, later_shift), 0.0)
    part = against(turned, gain_2_tall).reshape(SIDE, rows, columns)
    message = jnp.concatenate(
        [part, gain_4.reshape(SIDE, rows, panel), spread_2.reshape(SIDE, rows, panel)], axis=2
    )
    got = swap(message, "x")
    placed = swap_lanes(jnp.concatenate([got[i, :, columns : columns + panel] for i in range(SIDE)], axis=1))
    kept = swap_lanes(jnp.concatenate([got[i, :, columns + panel :] for i in range(SIDE)], axis=1))
    final_spread = jnp.sum(got[:, :, :columns], axis=0) + kept
    final_shift = lax.dynamic_slice_in_dim(shift_4, at_x * rows, rows, 0)
    return placed[None], final_shift[None], final_spread[None]


def solution(mesh):
    count = mesh.devices.shape[0]
    grid = Mesh(mesh.devices.reshape(count, SIDE, SIDE), ("tm", "y", "x"))
    row = ("y", "x")
    in_specs = (
        P("tm", row, None),
        P("tm", row, None),
        P("tm", None, None),
        P("tm", None),
        P("tm", row),
        P("tm", None),
        P("tm", None),
    )
    out_specs = (P("tm", row, None), P("tm", row), P("tm", row, None))
    return jax.shard_map(body, mesh=grid, in_specs=in_specs, out_specs=out_specs, check_vma=False)
```

```python
import jax
import jax.numpy as jnp
from jax import lax
from jax.experimental import pallas as pl
from jax.experimental.pallas import tpu as pltpu
from jax.sharding import Mesh, PartitionSpec as P

NBAND = 5
SIDE = 4

HIGHEST = lax.Precision.HIGHEST
F32 = jnp.float32


def dot(left, right):
    return jnp.dot(left, right, precision=HIGHEST, preferred_element_type=F32)


def dot_t(left, right):
    return lax.dot_general(
        left, right, (((1,), (1,)), ((), ())), precision=HIGHEST, preferred_element_type=F32
    )


def vector_times(row, matrix):
    return dot_t(jnp.broadcast_to(row, (8, row.shape[1])), matrix)[0:1]


def swap_lanes(array):
    width = array.shape[1] // (SIDE * SIDE)
    low = lax.broadcasted_iota(jnp.int32, (array.shape[0], 2 * width), 1) < width
    blocks = []
    for b in range(SIDE):
        for half in range(SIDE // 2):
            ends = []
            for side in range(2):
                at = (2 * half + side) * SIDE + b
                block = array[:, (at // 2) * 2 * width : (at // 2 + 1) * 2 * width]
                if at % 2 != side:
                    block = pltpu.roll(block, width, 1)
                ends.append(block)
            blocks.append(jnp.where(low, ends[0], ends[1]))
    return jnp.concatenate(blocks, axis=1)


def bands(array, weights, offset_at):
    columns = array.shape[1]
    lane = lax.broadcasted_iota(jnp.int32, (1, columns), 1)
    total = jnp.zeros(array.shape, F32)
    for b in range(NBAND):
        offset = offset_at(b)
        source = lane + offset
        weight = jnp.where((source >= 0) & (source < columns), weights[b : b + 1], 0.0)
        total = total + weight * pltpu.roll(array, lax.rem(columns - offset, columns), 1)
    return total


def bands_row(row, weights, offset_at):
    return bands(jnp.broadcast_to(row, (8, row.shape[1])), weights, offset_at)[0:1]


def wide(ref, rows):
    return jnp.concatenate([ref[i, 0:rows, :] for i in range(SIDE)], axis=1)


def place_tall(pieces, firsts, at_y, out_ref, row0=0):
    chunk = 64
    for piece, step in zip(pieces, firsts):
        source = lax.rem(at_y + SIDE - step, SIDE)
        for b in range(SIDE):
            out_ref[pl.ds(pl.multiple_of(b * SIDE * chunk + source * chunk, chunk), chunk), :] = piece[
                row0 + b * chunk : row0 + (b + 1) * chunk, :
            ]


STEPS = (0, 1, 3, 2)


def prepare(offsets, own, inverse, weights, prior, innovation, sites, x_out, y_out):
    rows, columns = own.shape
    panel = SIDE * rows
    matrix = own[...]
    crossed = bands(matrix, weights[...], lambda b: offsets[0, b])
    state = lax.broadcasted_iota(jnp.int32, (columns, sites.shape[1]), 0)
    matches = (state == sites[...]).astype(F32)
    pulled = vector_times(innovation[...], matches)
    filtered = prior[...] + vector_times(pulled, matrix)
    own_swapped = swap_lanes(matrix)
    crossed_swapped = swap_lanes(crossed)
    for i in range(SIDE):
        x_out[i, :, 0:columns] = crossed
        x_out[i, :, columns : columns + panel] = own_swapped[:, i * panel : (i + 1) * panel]
        x_out[i, :, columns + panel :] = crossed_swapped[:, i * panel : (i + 1) * panel]
    y_out[0:rows, :] = inverse[...]
    y_out[rows:, :] = jnp.zeros((8, columns), F32)
    y_out[rows : rows + 1, 0:rows] = filtered


def first_gain(where, x_in, p0, p1, p2, p3, gain_out, x_out, inverse):
    rows = x_in.shape[1]
    columns = p0.shape[1]
    at_y = where[0]
    filtered = [None] * SIDE
    for piece, step in zip((p0, p1, p2, p3), STEPS):
        source = lax.rem(at_y + SIDE - step, SIDE)
        inverse[pl.ds(pl.multiple_of(source * rows, rows), rows), :] = piece[0:rows, :]
        inverse[pl.ds(pl.multiple_of(SIDE * rows + 8 * source, 8), 8), :] = piece[rows:, :]
    crossed = jnp.concatenate([x_in[i, :, 0:columns] for i in range(SIDE)], axis=0)
    gain = dot_t(crossed, inverse[0 : SIDE * rows, :])
    gain_out[...] = gain
    tail = jnp.concatenate(
        [inverse[SIDE * rows + 8 * i : SIDE * rows + 8 * i + 1, 0:rows] for i in range(SIDE)], axis=1
    )
    tail = jnp.broadcast_to(tail, (8, SIDE * rows))
    for i in range(SIDE):
        x_out[i, 0 : SIDE * rows, :] = gain
        x_out[i, SIDE * rows :, :] = tail


def second_gain(
    where, offsets, weights, gain, x_in, e0, e1, e2, e3, c0, c1, c2, c3,
    gain_out, x_out, shift_out, c_out, tall,
):
    panel = gain.shape[0]
    rows = panel // SIDE
    at_y = where[0]
    gain_wide = wide(x_in, panel)
    filtered = jnp.concatenate([x_in[i, panel : panel + 1, :] for i in range(SIDE)], axis=1)
    natural = swap_lanes(jnp.broadcast_to(filtered, (8, filtered.shape[1])))
    forward = swap_lanes(bands(natural, weights[...], lambda b: offsets[0, b]))
    mine = jnp.zeros((1, panel), F32)
    for i in range(SIDE):
        mine = mine + jnp.where(at_y == i, natural[0:1, i * panel : (i + 1) * panel], 0.0)
    shift_out[...] = jnp.broadcast_to(mine - vector_times(forward[0:1], gain_wide), (8, panel))
    place_tall((e0, e1, e2, e3), STEPS, at_y, tall)
    gain_2 = jnp.where(where[2] == 1, dot(gain_wide, tall[...]), gain[...])
    gain_out[...] = gain_2
    for i in range(SIDE):
        x_out[i] = gain_2
    for piece, step in zip((c0, c1, c2, c3), STEPS):
        source = lax.rem(at_y + SIDE - step, SIDE)
        c_out[pl.ds(pl.multiple_of(source * rows, rows), rows), :] = piece[...]
    c_out[panel : panel + NBAND, :] = weights[...]
    c_out[panel + NBAND : panel + NBAND + 1, :] = filtered
    c_out[panel + NBAND + 1 : panel + NBAND + 2, :] = forward[0:1]
    lane = lax.broadcasted_iota(jnp.int32, (1, c_out.shape[1]), 1)
    held = jnp.zeros((1, c_out.shape[1]), jnp.int32)
    for b in range(NBAND):
        held = jnp.where(lane == b, offsets[0, b], held)
    c_out[panel + NBAND + 2 : panel + NBAND + 3, :] = held.astype(F32)


def first_spread(
    where, offsets, c_in, gain_in, gain_2_in, first_in, e0, e1, e2, e3, shift,
    part_out, shift_out, tall,
):
    panel = e0.shape[0]
    columns = c_in.shape[1]
    rows = panel // SIDE
    at_y = where[0]
    later = c_in[0:panel, :]
    crossed = bands(later, c_in[panel : panel + NBAND, :], lambda b: offsets[b])
    gain_wide = wide(gain_in, panel)
    gain_2_wide = wide(gain_2_in, panel)
    turned = dot_t(gain_wide, swap_lanes(later)) - dot_t(gain_2_wide, swap_lanes(crossed))
    filtered = c_in[panel + NBAND : panel + NBAND + 1, :]
    forward = c_in[panel + NBAND + 1 : panel + NBAND + 2, :]
    moved = vector_times(filtered, gain_wide) - vector_times(forward, gain_2_wide)
    inside = where[2] == 1
    shift_out[...] = shift[...] + jnp.where(inside, moved, 0.0)
    mine = jnp.concatenate([first_in[i, :, columns + panel :] for i in range(SIDE)], axis=0)
    turned = jnp.where(inside, turned, 0.0) - mine
    place_tall((e0, e1, e2, e3), STEPS, at_y, tall)
    for i in range(SIDE):
        part_out[i] = dot_t(tall[i * panel : (i + 1) * panel, :], turned)


def join_spread(parts, first_in, shift, out):
    panel = parts.shape[1]
    columns = first_in.shape[2] - 2 * panel
    total = (parts[0] + parts[1]) + (parts[2] + parts[3])
    mine = jnp.concatenate(
        [first_in[i, :, columns : columns + panel] for i in range(SIDE)], axis=0
    )
    out[0:panel, :] = mine + total.T
    out[panel:, :] = shift[...]


def second_spread(
    where, gain_2, gain_2_in, spread, y_in, a0, a1, a2, a3, x_out, shift_out, tall, later_tall,
):
    panel = gain_2.shape[0]
    rows = panel // SIDE
    columns = SIDE * panel
    at_y = where[0]
    inside = where[3] == 1
    gain_2_wide = wide(gain_2_in, panel)
    for i in range(SIDE):
        for b in range(SIDE):
            tall[b * panel + i * rows : b * panel + (i + 1) * rows, :] = y_in[
                i, b * rows : (b + 1) * rows, :
            ]
    turned = jnp.where(inside, dot(gain_2_wide, tall[...]), 0.0)
    shifts = jnp.concatenate([y_in[i, panel : panel + 8, :] for i in range(SIDE)], axis=1)
    moved = vector_times(swap_lanes(shifts)[0:1], gain_2_wide)
    shift_out[...] = spread[panel:, :] + jnp.where(inside, moved, 0.0)
    place_tall((a0, a1, a2, a3), STEPS, at_y, later_tall, panel)
    gain_4 = jnp.where(inside, dot(gain_2_wide, later_tall[...]), gain_2[...])
    for i in range(SIDE):
        x_out[i, :, columns : columns + panel] = gain_4[i * rows : (i + 1) * rows]
        x_out[i, :, columns + panel :] = spread[i * rows : (i + 1) * rows, :]
    for piece, step in zip((a0, a1, a2, a3), STEPS):
        source = lax.rem(at_y + SIDE - step, SIDE)
        tall[pl.ds(pl.multiple_of(source * panel, panel), panel), :] = piece[0:panel, :]
    part = dot_t(turned, tall[...])
    for i in range(SIDE):
        x_out[i, :, 0:columns] = part[i * rows : (i + 1) * rows]


def finish(x_in, gain_out, spread_out):
    rows, columns = gain_out.shape
    panel = SIDE * rows
    gain_out[...] = swap_lanes(
        jnp.concatenate([x_in[i, :, columns : columns + panel] for i in range(SIDE)], axis=1)
    )
    kept = swap_lanes(jnp.concatenate([x_in[i, :, columns + panel :] for i in range(SIDE)], axis=1))
    total = (x_in[0, :, 0:columns] + x_in[1, :, 0:columns]) + (
        x_in[2, :, 0:columns] + x_in[3, :, 0:columns]
    )
    spread_out[...] = total + kept


VMEM = pl.BlockSpec(memory_space=pltpu.VMEM)
SMEM = pl.BlockSpec(memory_space=pltpu.SMEM)


def call(kernel, scalars, arrays, outs, scratch=(), flops=0):
    shapes = [jax.ShapeDtypeStruct(s, F32) for s in outs]
    size = sum(a.size for a in arrays) + sum(s.size for s in shapes)
    return pl.pallas_call(
        kernel,
        out_shape=shapes,
        in_specs=[SMEM] * len(scalars) + [VMEM] * len(arrays),
        out_specs=[VMEM] * len(outs),
        scratch_shapes=[pltpu.VMEM(s, F32) for s in scratch],
        compiler_params=pltpu.CompilerParams(vmem_limit_bytes=40 * 2**20),
        cost_estimate=pl.CostEstimate(flops=flops, bytes_accessed=4 * size, transcendentals=0),
    )(*scalars, *arrays)


def shifted(block, distance):
    count = lax.axis_size("tm")
    return lax.ppermute(block, "tm", [(i + distance, i) for i in range(count - distance)])


def swap(message, axis):
    return lax.all_to_all(message, axis, 0, 0)


def ring(block, axis):
    pieces = [block]
    for step in STEPS[1:]:
        pieces.append(lax.ppermute(block, axis, [(i, (i + step) % SIDE) for i in range(SIDE)]))
    return pieces


def ring_shifted(block, distance):
    count = lax.axis_size("tm")
    pieces = []
    for step in STEPS:
        route = [
            ((i + distance) * SIDE + j, i * SIDE + (j + step) % SIDE)
            for i in range(count - distance)
            for j in range(SIDE)
        ]
        pieces.append(lax.ppermute(block, ("tm", "y"), route))
    return pieces


def body(covariance, precision, band_weight, band_offset, prior_mean, innovation, seen_sites):
    own = covariance[0]
    inverse = precision[0]
    weights = band_weight[0]
    rows, columns = own.shape
    panel = SIDE * rows
    at_t = lax.axis_index("tm")
    count_t = lax.axis_size("tm")
    at_x = lax.axis_index("x")
    where = jnp.stack(
        [
            lax.axis_index("y").astype(jnp.int32),
            at_x.astype(jnp.int32),
            (at_t + 1 < count_t).astype(jnp.int32),
            (at_t + 2 < count_t).astype(jnp.int32),
        ]
    )
    unit = 2 * panel * panel * columns

    x_message, y_message = call(
        prepare,
        (band_offset,),
        (own, inverse, weights, prior_mean, innovation, seen_sites),
        ((SIDE, rows, columns + 2 * panel), (rows + 8, columns)),
    )
    first_in = swap(x_message, "x")
    inverse_pieces = ring(y_message, "y")
    own_pieces = ring(own, "y")
    gain, x_message = call(
        first_gain,
        (where,),
        (first_in, *inverse_pieces),
        ((panel, panel), (SIDE, panel + 8, panel)),
        ((panel + 32, columns),),
        unit,
    )
    gain_in = swap(x_message, "x")
    later_pieces = ring_shifted(gain, 1)
    gain_2, x_message, shift, c_message = call(
        second_gain,
        (where, band_offset),
        (weights, gain, gain_in, *later_pieces, *own_pieces),
        ((panel, panel), (SIDE, panel, panel), (8, panel), (panel + 8, columns)),
        ((columns, panel),),
        unit,
    )
    gain_2_in = swap(x_message, "x")
    gain_pieces = ring(gain, "y")
    gain_2_later = shifted(gain_2, 2)
    c_in = shifted(c_message, 1)
    next_offsets = c_in[panel + NBAND + 2, 0:8].astype(jnp.int32)
    part, shift_2 = call(
        first_spread,
        (where, next_offsets),
        (c_in, gain_in, gain_2_in, first_in, *gain_pieces, shift),
        ((SIDE, panel, panel), (8, panel)),
        ((columns, panel),),
        3 * unit,
    )
    parts = swap(part, "x")
    gain_2_pieces = ring(jnp.concatenate([gain_2, gain_2_later], axis=0), "y")
    (spread_2,) = call(join_spread, (), (parts, first_in, shift_2), ((panel + 8, panel),))
    later = shifted(spread_2, 2)
    y_in = swap(jnp.broadcast_to(later[None], (SIDE, panel + 8, panel)), "y")
    x_message, shift_4 = call(
        second_spread,
        (where,),
        (gain_2, gain_2_in, spread_2, y_in, *gain_2_pieces),
        ((SIDE, rows, columns + 2 * panel), (8, panel)),
        ((columns, panel), (columns, panel)),
        3 * unit,
    )
    last_in = swap(x_message, "x")
    final_gain, final_spread = call(finish, (), (last_in,), ((rows, columns), (rows, columns)))
    final_shift = lax.dynamic_slice_in_dim(shift_4[0], at_x * rows, rows, 0)
    return final_gain[None], final_shift[None], final_spread[None]


def solution(mesh):
    count = mesh.devices.shape[0]
    grid = Mesh(mesh.devices.reshape(count, SIDE, SIDE), ("tm", "y", "x"))
    row = ("y", "x")
    in_specs = (
        P("tm", row, None),
        P("tm", row, None),
        P("tm", None, None),
        P("tm", None),
        P("tm", row),
        P("tm", None),
        P("tm", None),
    )
    out_specs = (P("tm", row, None), P("tm", row), P("tm", row, None))
    return jax.shard_map(body, mesh=grid, in_specs=in_specs, out_specs=out_specs, check_vma=False)
```

```python
import math

import jax
import jax.numpy as jnp
from jax import lax
from jax.experimental import pallas as pl
from jax.experimental.pallas import tpu as pltpu
from jax.sharding import Mesh, PartitionSpec as P

NBAND = 5
SIDE = 4

HIGHEST = lax.Precision.HIGHEST
F32 = jnp.float32


def halves(array):
    high = array.astype(jnp.bfloat16)
    return high, (array - high.astype(F32)).astype(jnp.bfloat16)


def three(left, right, contract):
    def one(first, second):
        return lax.dot_general(first, second, (contract, ((), ())), preferred_element_type=F32)

    left_high, left_low = left
    right_high, right_low = right
    return one(left_high, right_high) + (one(left_high, right_low) + one(left_low, right_high))


def dot(left, right):
    return three(halves(left), halves(right), ((1,), (0,)))


def dot_t(left, right):
    return three(halves(left), halves(right), ((1,), (1,)))


def exact_dot_t(left, right):
    return lax.dot_general(
        left, right, (((1,), (1,)), ((), ())), precision=HIGHEST, preferred_element_type=F32
    )


def vector_times(row, matrix):
    return exact_dot_t(jnp.broadcast_to(row, (8, row.shape[1])), matrix)[0:1]


def swap_lanes(array):
    width = array.shape[1] // (SIDE * SIDE)
    low = lax.broadcasted_iota(jnp.int32, (array.shape[0], 2 * width), 1) < width
    blocks = []
    for b in range(SIDE):
        for half in range(SIDE // 2):
            ends = []
            for side in range(2):
                at = (2 * half + side) * SIDE + b
                block = array[:, (at // 2) * 2 * width : (at // 2 + 1) * 2 * width]
                if at % 2 != side:
                    block = pltpu.roll(block, width, 1)
                ends.append(block)
            blocks.append(jnp.where(low, ends[0], ends[1]))
    return jnp.concatenate(blocks, axis=1)


def bands(array, weights, offset_at):
    columns = array.shape[1]
    lane = lax.broadcasted_iota(jnp.int32, (1, columns), 1)
    total = jnp.zeros(array.shape, F32)
    for b in range(NBAND):
        offset = offset_at(b)
        source = lane + offset
        weight = jnp.where((source >= 0) & (source < columns), weights[b : b + 1], 0.0)
        total = total + weight * pltpu.roll(array, lax.rem(columns - offset, columns), 1)
    return total


def bands_row(row, weights, offset_at):
    return bands(jnp.broadcast_to(row, (8, row.shape[1])), weights, offset_at)[0:1]


def wide(ref, rows):
    return jnp.concatenate([ref[i, 0:rows, :] for i in range(SIDE)], axis=1)


def place_tall(pieces, firsts, at_y, out_ref, row0=0):
    chunk = 64
    for piece, step in zip(pieces, firsts):
        source = lax.rem(at_y + SIDE - step, SIDE)
        for b in range(SIDE):
            out_ref[pl.ds(pl.multiple_of(b * SIDE * chunk + source * chunk, chunk), chunk), :] = piece[
                row0 + b * chunk : row0 + (b + 1) * chunk, :
            ]


STEPS = (0, 1, 3, 2)


def prepare(offsets, own, inverse, weights, prior, innovation, sites, x_out, y_out):
    rows, columns = own.shape
    panel = SIDE * rows
    matrix = own[...]
    crossed = bands(matrix, weights[...], lambda b: offsets[0, b])
    state = lax.broadcasted_iota(jnp.int32, (columns, sites.shape[1]), 0)
    matches = (state == sites[...]).astype(F32)
    pulled = vector_times(innovation[...], matches)
    filtered = prior[...] + vector_times(pulled, matrix)
    own_swapped = swap_lanes(matrix)
    crossed_swapped = swap_lanes(crossed)
    for i in range(SIDE):
        x_out[i, :, 0:columns] = crossed
        x_out[i, :, columns : columns + panel] = own_swapped[:, i * panel : (i + 1) * panel]
        x_out[i, :, columns + panel :] = crossed_swapped[:, i * panel : (i + 1) * panel]
    y_out[0:rows, :] = inverse[...]
    y_out[rows:, :] = jnp.zeros((8, columns), F32)
    y_out[rows : rows + 1, 0:rows] = filtered


def first_gain(where, x_in, p0, p1, p2, p3, gain_out, x_out, inverse):
    rows = x_in.shape[1]
    columns = p0.shape[1]
    at_y = where[0]
    filtered = [None] * SIDE
    for piece, step in zip((p0, p1, p2, p3), STEPS):
        source = lax.rem(at_y + SIDE - step, SIDE)
        inverse[pl.ds(pl.multiple_of(source * rows, rows), rows), :] = piece[0:rows, :]
        inverse[pl.ds(pl.multiple_of(SIDE * rows + 8 * source, 8), 8), :] = piece[rows:, :]
    crossed = jnp.concatenate([x_in[i, :, 0:columns] for i in range(SIDE)], axis=0)
    gain = dot_t(crossed, inverse[0 : SIDE * rows, :])
    gain_out[...] = gain
    tail = jnp.concatenate(
        [inverse[SIDE * rows + 8 * i : SIDE * rows + 8 * i + 1, 0:rows] for i in range(SIDE)], axis=1
    )
    tail = jnp.broadcast_to(tail, (8, SIDE * rows))
    for i in range(SIDE):
        x_out[i, 0 : SIDE * rows, :] = gain
        x_out[i, SIDE * rows :, :] = tail


def second_gain(
    where, offsets, weights, gain, x_in, e0, e1, e2, e3, own_panel,
    gain_out, x_out, shift_out, c_out, tall,
):
    panel = gain.shape[0]
    at_y = where[0]
    gain_wide = wide(x_in, panel)
    filtered = jnp.concatenate([x_in[i, panel : panel + 1, :] for i in range(SIDE)], axis=1)
    natural = swap_lanes(jnp.broadcast_to(filtered, (8, filtered.shape[1])))
    forward = swap_lanes(bands(natural, weights[...], lambda b: offsets[0, b]))
    mine = jnp.zeros((1, panel), F32)
    for i in range(SIDE):
        mine = mine + jnp.where(at_y == i, natural[0:1, i * panel : (i + 1) * panel], 0.0)
    shift_out[...] = jnp.broadcast_to(mine - vector_times(forward[0:1], gain_wide), (8, panel))
    place_tall((e0, e1, e2, e3), STEPS, at_y, tall)
    gain_2 = jnp.where(where[2] == 1, dot(gain_wide, tall[...]), gain[...])
    gain_out[...] = gain_2
    for i in range(SIDE):
        x_out[i] = gain_2
    c_out[0:panel, :] = own_panel[...]
    c_out[panel : panel + NBAND, :] = weights[...]
    c_out[panel + NBAND : panel + NBAND + 1, :] = filtered
    c_out[panel + NBAND + 1 : panel + NBAND + 2, :] = forward[0:1]
    lane = lax.broadcasted_iota(jnp.int32, (1, c_out.shape[1]), 1)
    held = jnp.zeros((1, c_out.shape[1]), jnp.int32)
    for b in range(NBAND):
        held = jnp.where(lane == b, offsets[0, b], held)
    c_out[panel + NBAND + 2 : panel + NBAND + 3, :] = held.astype(F32)


def first_spread(
    where, offsets, c_in, gain_in, gain_2_in, first_in, e0, e1, e2, e3, shift,
    part_out, shift_out, tall,
):
    panel = e0.shape[0]
    columns = c_in.shape[1]
    rows = panel // SIDE
    at_y = where[0]
    later = c_in[0:panel, :]
    crossed = bands(later, c_in[panel : panel + NBAND, :], lambda b: offsets[b])
    gain_wide = wide(gain_in, panel)
    gain_2_wide = wide(gain_2_in, panel)
    turned = dot_t(gain_wide, swap_lanes(later)) - dot_t(gain_2_wide, swap_lanes(crossed))
    filtered = c_in[panel + NBAND : panel + NBAND + 1, :]
    forward = c_in[panel + NBAND + 1 : panel + NBAND + 2, :]
    moved = vector_times(filtered, gain_wide) - vector_times(forward, gain_2_wide)
    inside = where[2] == 1
    shift_out[...] = shift[...] + jnp.where(inside, moved, 0.0)
    mine = jnp.concatenate([first_in[i, :, columns + panel :] for i in range(SIDE)], axis=0)
    turned = jnp.where(inside, turned, 0.0) - mine
    place_tall((e0, e1, e2, e3), STEPS, at_y, tall)
    for i in range(SIDE):
        part_out[i] = dot_t(tall[i * panel : (i + 1) * panel, :], turned)


def join_spread(parts, first_in, shift, out):
    panel = parts.shape[1]
    columns = first_in.shape[2] - 2 * panel
    total = (parts[0] + parts[1]) + (parts[2] + parts[3])
    mine = jnp.concatenate(
        [first_in[i, :, columns : columns + panel] for i in range(SIDE)], axis=0
    )
    out[0:panel, :] = mine + total.T
    out[panel:, :] = shift[...]


def four_times(block, p1, p2, p3, out):
    for i in range(SIDE):
        out[i] = block[...]


def second_spread(
    where, gain_2, gain_2_in, spread, y_in, a0, a1, a2, a3, x_out, shift_out, tall, later_tall,
):
    panel = gain_2.shape[0]
    rows = panel // SIDE
    columns = SIDE * panel
    at_y = where[0]
    inside = where[3] == 1
    gain_2_wide = wide(gain_2_in, panel)
    for i in range(SIDE):
        for b in range(SIDE):
            tall[b * panel + i * rows : b * panel + (i + 1) * rows, :] = y_in[
                i, b * rows : (b + 1) * rows, :
            ]
    turned = jnp.where(inside, dot(gain_2_wide, tall[...]), 0.0)
    shifts = jnp.concatenate([y_in[i, panel : panel + 8, :] for i in range(SIDE)], axis=1)
    moved = vector_times(swap_lanes(shifts)[0:1], gain_2_wide)
    shift_out[...] = spread[panel:, :] + jnp.where(inside, moved, 0.0)
    place_tall((a0, a1, a2, a3), STEPS, at_y, later_tall, panel)
    gain_4 = jnp.where(inside, dot(gain_2_wide, later_tall[...]), gain_2[...])
    for i in range(SIDE):
        x_out[i, :, columns : columns + panel] = gain_4[i * rows : (i + 1) * rows]
        x_out[i, :, columns + panel :] = spread[i * rows : (i + 1) * rows, :]
    for piece, step in zip((a0, a1, a2, a3), STEPS):
        source = lax.rem(at_y + SIDE - step, SIDE)
        tall[pl.ds(pl.multiple_of(source * panel, panel), panel), :] = piece[0:panel, :]
    part = dot_t(turned, tall[...])
    for i in range(SIDE):
        x_out[i, :, 0:columns] = part[i * rows : (i + 1) * rows]


def finish(x_in, gain_out, spread_out):
    rows, columns = gain_out.shape
    panel = SIDE * rows
    gain_out[...] = swap_lanes(
        jnp.concatenate([x_in[i, :, columns : columns + panel] for i in range(SIDE)], axis=1)
    )
    kept = swap_lanes(jnp.concatenate([x_in[i, :, columns + panel :] for i in range(SIDE)], axis=1))
    total = (x_in[0, :, 0:columns] + x_in[1, :, 0:columns]) + (
        x_in[2, :, 0:columns] + x_in[3, :, 0:columns]
    )
    spread_out[...] = total + kept


WHOLE = pl.BlockSpec()
UNREAD = pl.BlockSpec(memory_space=pl.ANY)
SMEM = pl.BlockSpec(memory_space=pltpu.SMEM)


def far(*arrays):
    return [pltpu.with_memory_space_constraint(a, pltpu.HBM) for a in arrays]


def call(kernel, scalars, arrays, outs, scratch=(), flops=0, unread=()):
    shapes = [pltpu.HBM(s, F32) if len(s) == 3 else jax.ShapeDtypeStruct(s, F32) for s in outs]
    size = sum(a.size for a in arrays) + sum(math.prod(s) for s in outs)
    return pl.pallas_call(
        kernel,
        out_shape=shapes,
        in_specs=[SMEM] * len(scalars) + [WHOLE] * len(arrays) + [UNREAD] * len(unread),
        out_specs=[WHOLE] * len(outs),
        scratch_shapes=[pltpu.VMEM(s, F32) for s in scratch],
        compiler_params=pltpu.CompilerParams(vmem_limit_bytes=24 * 2**20),
        cost_estimate=pl.CostEstimate(flops=flops, bytes_accessed=4 * size, transcendentals=0),
    )(*scalars, *arrays, *unread)


def shifted(block, distance):
    count = lax.axis_size("tm")
    return lax.ppermute(block, "tm", [(i + distance, i) for i in range(count - distance)])


def swap(message, axis):
    return lax.all_to_all(message, axis, 0, 0)


def ring(block, axis):
    pieces = [block]
    for step in STEPS[1:]:
        pieces.append(lax.ppermute(block, axis, [(i, (i + step) % SIDE) for i in range(SIDE)]))
    return pieces


def ring_shifted(block, distance):
    count = lax.axis_size("tm")
    pieces = []
    for step in STEPS:
        route = [
            ((i + distance) * SIDE + j, i * SIDE + (j + step) % SIDE)
            for i in range(count - distance)
            for j in range(SIDE)
        ]
        pieces.append(lax.ppermute(block, ("tm", "y"), route))
    return pieces


def body(covariance, precision, band_weight, band_offset, prior_mean, innovation, seen_sites):
    own = covariance[0]
    inverse = precision[0]
    weights = band_weight[0]
    rows, columns = own.shape
    panel = SIDE * rows
    at_t = lax.axis_index("tm")
    count_t = lax.axis_size("tm")
    at_x = lax.axis_index("x")
    where = jnp.stack(
        [
            lax.axis_index("y").astype(jnp.int32),
            at_x.astype(jnp.int32),
            (at_t + 1 < count_t).astype(jnp.int32),
            (at_t + 2 < count_t).astype(jnp.int32),
        ]
    )
    unit = 2 * panel * panel * columns

    x_message, y_message = call(
        prepare,
        (band_offset,),
        far(own, inverse, weights, prior_mean, innovation, seen_sites),
        ((SIDE, rows, columns + 2 * panel), (rows + 8, columns)),
    )
    first_in = swap(x_message, "x")
    inverse_pieces = ring(y_message, "y")
    own_panel = lax.all_gather(own, "y", axis=0, tiled=True)
    gain, x_message = call(
        first_gain,
        (where,),
        (first_in, *inverse_pieces),
        ((panel, panel), (SIDE, panel + 8, panel)),
        ((panel + 32, columns),),
        unit,
    )
    gain_in = swap(x_message, "x")
    later_pieces = ring_shifted(gain, 1)
    gain_2, x_message, shift, c_message = call(
        second_gain,
        (where, band_offset),
        (*far(weights), gain, gain_in, *far(*later_pieces, own_panel)),
        ((panel, panel), (SIDE, panel, panel), (8, panel), (panel + 8, columns)),
        ((columns, panel),),
        unit,
    )
    gain_2_in = swap(x_message, "x")
    gain_pieces = ring(gain, "y")
    gain_2_later = shifted(gain_2, 2)
    c_in = shifted(c_message, 1)
    next_offsets = c_in[panel + NBAND + 2, 0:8].astype(jnp.int32)
    part, shift_2 = call(
        first_spread,
        (where, next_offsets),
        (c_in, gain_in, gain_2_in, first_in, gain, *far(*gain_pieces[1:]), shift),
        ((SIDE, panel, panel), (8, panel)),
        ((columns, panel),),
        3 * unit,
    )
    parts = swap(part, "x")
    gain_2_pieces = ring(jnp.concatenate([gain_2, gain_2_later], axis=0), "y")
    (spread_2,) = call(join_spread, (), (parts, first_in, shift_2), ((panel + 8, panel),))
    later = shifted(spread_2, 2)
    (y_message,) = call(
        four_times, (), (later,), ((SIDE, panel + 8, panel),), unread=gain_2_pieces[1:]
    )
    y_in = swap(y_message, "y")
    x_message, shift_4 = call(
        second_spread,
        (where,),
        (gain_2, gain_2_in, spread_2, y_in, *gain_2_pieces),
        ((SIDE, rows, columns + 2 * panel), (8, panel)),
        ((columns, panel), (columns, panel)),
        3 * unit,
    )
    last_in = swap(x_message, "x")
    final_gain, final_spread = call(finish, (), (last_in,), ((rows, columns), (rows, columns)))
    final_shift = lax.dynamic_slice_in_dim(shift_4[0], at_x * rows, rows, 0)
    return final_gain[None], final_shift[None], final_spread[None]


def solution(mesh):
    count = mesh.devices.shape[0]
    grid = Mesh(mesh.devices.reshape(count, SIDE, SIDE), ("tm", "y", "x"))
    row = ("y", "x")
    in_specs = (
        P("tm", row, None),
        P("tm", row, None),
        P("tm", None, None),
        P("tm", None),
        P("tm", row),
        P("tm", None),
        P("tm", None),
    )
    out_specs = (P("tm", row, None), P("tm", row), P("tm", row, None))
    return jax.shard_map(body, mesh=grid, in_specs=in_specs, out_specs=out_specs, check_vma=False)
```

```python
import math

import jax
import jax.numpy as jnp
from jax import lax
from jax.experimental import pallas as pl
from jax.experimental.pallas import tpu as pltpu
from jax.sharding import Mesh, PartitionSpec as P

NBAND = 5
SIDE = 4

HIGHEST = lax.Precision.HIGHEST
F32 = jnp.float32


def halves(array):
    high = array.astype(jnp.bfloat16)
    return high, (array - high.astype(F32)).astype(jnp.bfloat16)


def three(left, right, contract):
    def one(first, second):
        return lax.dot_general(first, second, (contract, ((), ())), preferred_element_type=F32)

    left_high, left_low = left
    right_high, right_low = right
    return one(left_high, right_high) + (one(left_high, right_low) + one(left_low, right_high))


def dot_t(left, right):
    return three(halves(left), halves(right), ((1,), (1,)))


def exact_dot_t(left, right):
    return lax.dot_general(
        left, right, (((1,), (1,)), ((), ())), precision=HIGHEST, preferred_element_type=F32
    )


def vector_times(row, matrix):
    return exact_dot_t(jnp.broadcast_to(row, (8, row.shape[1])), matrix)[0:1]


def row_times(row, matrix_halves):
    whole = jnp.broadcast_to(row, (8, row.shape[1]))
    return three(halves(whole), matrix_halves, ((1,), (1,)))[0:1]


LANES = 128


def tiles(array):
    return [array[:, i : i + LANES] for i in range(0, array.shape[1], LANES)]


def low_lanes(rows, width):
    return lax.broadcasted_iota(jnp.int32, (rows, LANES), 1) < width


def swap_tiles(blocks):
    width = LANES // 2
    low = low_lanes(blocks[0].shape[0], width)
    rolled = [pltpu.roll(block, width, 1) for block in blocks]
    out = []
    for b in range(SIDE):
        for half in range(SIDE // 2):
            ends = []
            for side in range(2):
                at = (2 * half + side) * SIDE + b
                ends.append((blocks if at % 2 == side else rolled)[at // 2])
            out.append(jnp.where(low, ends[0], ends[1]))
    return out


def swap_lanes(array):
    return jnp.concatenate(swap_tiles(tiles(array)), axis=1)


def band_tiles(blocks, weights, offset_at):
    rows = blocks[0].shape[0]
    width = LANES // 2
    low = low_lanes(rows, width)
    zero = jnp.zeros((rows, LANES), F32)
    turned = [zero] + [pltpu.roll(block, width, 1) for block in blocks] + [zero]
    moved = [jnp.where(low, turned[i], turned[i + 1]) for i in range(len(blocks) + 1)]
    totals = [zero] * len(blocks)
    for b in range(NBAND):
        distance = offset_at(b) + width
        near = low_lanes(rows, LANES - distance)
        back = lax.rem(LANES - distance, LANES)
        rolled = [pltpu.roll(block, back, 1) for block in moved]
        for i in range(len(blocks)):
            weight = weights[b : b + 1, i * LANES : (i + 1) * LANES]
            totals[i] = totals[i] + weight * jnp.where(near, rolled[i], rolled[i + 1])
    return totals


def bands(array, weights, offset_at):
    return jnp.concatenate(band_tiles(tiles(array), weights, offset_at), axis=1)


def wide(ref, rows):
    return jnp.concatenate([ref[i, 0:rows, :] for i in range(SIDE)], axis=1)


STEPS = (0, 1, 3, 2)


def sources(pieces, at):
    return [(piece, lax.rem(at + SIDE - step, SIDE)) for piece, step in zip(pieces, STEPS)]


def place_tall(pieces, at_y, out_ref, row0=0):
    panel = out_ref.shape[0] // SIDE
    chunk = panel // SIDE
    for piece, source in sources(pieces, at_y):
        for b in range(SIDE):
            out_ref[pl.ds(pl.multiple_of(b * panel + source * chunk, chunk), chunk), :] = piece[
                row0 + b * chunk : row0 + (b + 1) * chunk, :
            ]


def prepare(offsets, own, inverse, weights, prior, innovation, sites, crossed_out, y_out):
    rows, columns = own.shape
    matrix = own[...]
    crossed_out[...] = bands(matrix, weights[...], lambda b: offsets[0, b])
    state = lax.broadcasted_iota(jnp.int32, (columns, sites.shape[1]), 0)
    matches = (state == sites[...]).astype(F32)
    pulled = vector_times(innovation[...], matches)
    filtered = prior[...] + vector_times(pulled, matrix)
    for i in range(SIDE):
        y_out[i, 0:rows, :] = inverse[...]
        y_out[i, rows : 2 * rows, :] = matrix
        y_out[i, 2 * rows :, :] = jnp.zeros((8, columns), F32)
        y_out[i, 2 * rows : 2 * rows + 1, 0:rows] = filtered


def place_rows(pieces, at, out):
    rows = pieces[0].shape[0]
    for piece, source in sources(pieces, at):
        out[pl.ds(pl.multiple_of(source * rows, rows), rows), :] = piece[...]


def first_gain(where, y_in, x0, x1, x2, x3, gain_out, x_out, crossed):
    rows = x0.shape[0]
    panel = SIDE * rows
    place_rows((x0, x1, x2, x3), where[1], crossed)
    inverse = jnp.concatenate([y_in[i, 0:rows, :] for i in range(SIDE)], axis=0)
    gain = dot_t(crossed[...], inverse)
    gain_out[...] = gain
    tail = jnp.concatenate(
        [y_in[i, 2 * rows : 2 * rows + 1, 0:rows] for i in range(SIDE)], axis=1
    )
    tail = jnp.broadcast_to(tail, (8, panel))
    for i in range(SIDE):
        x_out[i, 0:panel, :] = gain
        x_out[i, panel:, :] = tail


def cut_blocks(where, y_in, x0, x1, x2, x3, out, crossed):
    rows = x0.shape[0]
    panel = SIDE * rows
    place_rows((x0, x1, x2, x3), where[1], crossed)
    at_y = pl.multiple_of(where[0] * panel, panel)
    own = jnp.concatenate(
        [y_in[i, rows : 2 * rows, pl.ds(at_y, panel)] for i in range(SIDE)], axis=0
    )
    out[0:panel, :] = own.T
    odd = lax.rem(where[1], 2)
    at_x = lax.div(where[1], 2) * LANES
    low = low_lanes(panel, rows)
    parts = []
    for i in range(SIDE):
        part = crossed[:, pl.ds(pl.multiple_of(i * panel + at_x, LANES), LANES)]
        turn = odd if i % 2 == 0 else 1 - odd
        parts.append(pltpu.roll(part, turn * rows, 1))
    out[panel:, 0:LANES] = jnp.where(low, parts[0], parts[1])
    out[panel:, LANES:] = jnp.where(low, parts[2], parts[3])


def second_gain(
    where, offsets, weights, gain, x_in, e0, e1, e2, e3, y_in,
    gain_out, x_out, shift_out, c_out, high_out, low_out, tall,
):
    panel = gain.shape[0]
    rows = panel // SIDE
    at_y = where[0]
    gain_wide = halves(wide(x_in, panel))
    high_out[...] = gain_wide[0]
    low_out[...] = gain_wide[1]
    place_tall((e0, e1, e2, e3), at_y, tall)
    product = three(gain_wide, halves(tall[...]), ((1,), (0,)))
    gain_2 = jnp.where(where[2] == 1, product, gain[...])
    gain_out[...] = gain_2
    for i in range(SIDE):
        x_out[i] = gain_2
    filtered = jnp.concatenate([x_in[i, panel : panel + 8, :] for i in range(SIDE)], axis=1)
    natural = swap_lanes(filtered)
    forward = swap_lanes(bands(natural, weights[...], lambda b: offsets[0, b]))
    mine = jnp.zeros((1, panel), F32)
    for i in range(SIDE):
        mine = mine + jnp.where(at_y == i, natural[0:1, i * panel : (i + 1) * panel], 0.0)
    shift_out[...] = jnp.broadcast_to(mine - row_times(forward[0:1], gain_wide), (8, panel))
    for i in range(SIDE):
        c_out[i * rows : (i + 1) * rows, :] = y_in[i, rows : 2 * rows, :]
    c_out[panel : panel + NBAND, :] = weights[...]
    c_out[panel + NBAND : panel + NBAND + 1, :] = filtered[0:1]
    c_out[panel + NBAND + 1 : panel + NBAND + 2, :] = forward[0:1]
    lane = lax.broadcasted_iota(jnp.int32, (1, c_out.shape[1]), 1)
    held = jnp.zeros((1, c_out.shape[1]), jnp.int32)
    for b in range(NBAND):
        held = jnp.where(lane == b, offsets[0, b], held)
    c_out[panel + NBAND + 2 : panel + NBAND + 3, :] = held.astype(F32)


def later_inputs(offsets, c_in, rows_out, own_high, own_low, crossed_high, crossed_low):
    panel = own_high.shape[0]
    step = 16
    weights = c_in[panel : panel + NBAND, :]

    def put(at, blocks, high_out, low_out):
        for i, block in enumerate(swap_tiles(blocks)):
            high, low = halves(block)
            high_out[pl.ds(at, step), i * LANES : (i + 1) * LANES] = high
            low_out[pl.ds(at, step), i * LANES : (i + 1) * LANES] = low

    def one(index, carry):
        at = pl.multiple_of(index * step, step)
        blocks = tiles(c_in[pl.ds(at, step), :])
        put(at, blocks, own_high, own_low)
        put(at, band_tiles(blocks, weights, lambda b: offsets[b]), crossed_high, crossed_low)
        return carry

    lax.fori_loop(0, panel // step, one, 0)
    rows_out[...] = c_in[panel:, :]


def first_spread(
    where, wide_high, wide_low, gain_2_in, own_high, own_low, crossed_high, crossed_low,
    later_rows, blocks, e0, e1, e2, e3, shift, gain_2, gain_2_later,
    part_out, shift_out, pair_out, high_out, low_out, tall,
):
    panel = e0.shape[0]
    at_y = where[0]
    pair_out[0:panel, :] = gain_2[...]
    pair_out[panel:, :] = gain_2_later[...]
    gain_wide = (wide_high[...], wide_low[...])
    gain_2_wide = halves(wide(gain_2_in, panel))
    high_out[...] = gain_2_wide[0]
    low_out[...] = gain_2_wide[1]
    across = ((1,), (1,))
    turned = three(gain_wide, (own_high[...], own_low[...]), across) - three(
        gain_2_wide, (crossed_high[...], crossed_low[...]), across
    )
    moved = row_times(later_rows[NBAND : NBAND + 1, :], gain_wide) - row_times(
        later_rows[NBAND + 1 : NBAND + 2, :], gain_2_wide
    )
    inside = where[2] == 1
    shift_out[...] = shift[...] + jnp.where(inside, moved, 0.0)
    turned = halves(jnp.where(inside, turned, 0.0) - blocks[panel:, :])
    place_tall((e0, e1, e2, e3), at_y, tall)
    for i in range(SIDE):
        part_out[i] = three(halves(tall[i * panel : (i + 1) * panel, :]), turned, across)


def join_spread(parts, blocks, shift, out):
    panel = parts.shape[1]
    total = (parts[0] + parts[1]) + (parts[2] + parts[3])
    out[0:panel, :] = blocks[0:panel, :] + total.T
    out[panel:, :] = shift[...]


def four_times(block, p1, p2, p3, out):
    for i in range(SIDE):
        out[i] = block[...]


def second_spread(
    where, gain_2, wide_high, wide_low, spread, y_in, a0, a1, a2, a3,
    x_out, shift_out, tall, later_tall,
):
    panel = gain_2.shape[0]
    rows = panel // SIDE
    columns = SIDE * panel
    at_y = where[0]
    inside = where[3] == 1
    gain_2_wide = (wide_high[...], wide_low[...])
    for i in range(SIDE):
        for b in range(SIDE):
            tall[b * panel + i * rows : b * panel + (i + 1) * rows, :] = y_in[
                i, b * rows : (b + 1) * rows, :
            ]
    along = ((1,), (0,))
    turned = halves(jnp.where(inside, three(gain_2_wide, halves(tall[...]), along), 0.0))
    shifts = jnp.concatenate([y_in[i, panel : panel + 8, :] for i in range(SIDE)], axis=1)
    moved = row_times(swap_lanes(shifts)[0:1], gain_2_wide)
    shift_out[...] = spread[panel:, :] + jnp.where(inside, moved, 0.0)
    pieces = (a0, a1, a2, a3)
    place_tall(pieces, at_y, later_tall, panel)
    gain_4 = jnp.where(inside, three(gain_2_wide, halves(later_tall[...]), along), gain_2[...])
    for i in range(SIDE):
        x_out[i, :, columns : columns + panel] = gain_4[i * rows : (i + 1) * rows]
        x_out[i, :, columns + panel :] = spread[i * rows : (i + 1) * rows, :]
    for piece, source in sources(pieces, at_y):
        tall[pl.ds(pl.multiple_of(source * panel, panel), panel), :] = piece[0:panel, :]
    part = three(turned, halves(tall[...]), ((1,), (1,)))
    for i in range(SIDE):
        x_out[i, :, 0:columns] = part[i * rows : (i + 1) * rows]


def finish(x_in, gain_out, spread_out):
    rows, columns = gain_out.shape
    panel = SIDE * rows
    gain_out[...] = swap_lanes(
        jnp.concatenate([x_in[i, :, columns : columns + panel] for i in range(SIDE)], axis=1)
    )
    kept = swap_lanes(jnp.concatenate([x_in[i, :, columns + panel :] for i in range(SIDE)], axis=1))
    total = (x_in[0, :, 0:columns] + x_in[1, :, 0:columns]) + (
        x_in[2, :, 0:columns] + x_in[3, :, 0:columns]
    )
    spread_out[...] = total + kept


WHOLE = pl.BlockSpec()
UNREAD = pl.BlockSpec(memory_space=pl.ANY)
SMEM = pl.BlockSpec(memory_space=pltpu.SMEM)


def far(*arrays):
    return [pltpu.with_memory_space_constraint(a, pltpu.HBM) for a in arrays]


def call(kernel, scalars, arrays, outs, scratch=(), flops=0, unread=(), coarse=()):
    shapes = [pltpu.HBM(s, F32) for s in outs] + [pltpu.HBM(s, jnp.bfloat16) for s in coarse]
    size = sum(a.size for a in arrays) + sum(math.prod(s) for s in outs)
    return pl.pallas_call(
        kernel,
        out_shape=shapes,
        in_specs=[SMEM] * len(scalars) + [WHOLE] * len(arrays) + [UNREAD] * len(unread),
        out_specs=[WHOLE] * len(shapes),
        scratch_shapes=[pltpu.VMEM(s, F32) for s in scratch],
        compiler_params=pltpu.CompilerParams(vmem_limit_bytes=24 * 2**20),
        cost_estimate=pl.CostEstimate(flops=flops, bytes_accessed=4 * size, transcendentals=0),
    )(*scalars, *arrays, *unread)


def shifted(block, distance):
    count = lax.axis_size("tm")
    return lax.ppermute(block, "tm", [(i + distance, i) for i in range(count - distance)])


def swap(message, axis):
    return lax.all_to_all(message, axis, 0, 0)


def ring(block, axis):
    pieces = [block]
    for step in STEPS[1:]:
        pieces.append(lax.ppermute(block, axis, [(i, (i + step) % SIDE) for i in range(SIDE)]))
    return pieces


def ring_shifted(block, distance):
    count = lax.axis_size("tm")
    pieces = []
    for step in STEPS:
        route = [
            ((i + distance) * SIDE + j, i * SIDE + (j + step) % SIDE)
            for i in range(count - distance)
            for j in range(SIDE)
        ]
        pieces.append(lax.ppermute(block, ("tm", "y"), route))
    return pieces


def body(covariance, precision, band_weight, band_offset, prior_mean, innovation, seen_sites):
    own = covariance[0]
    inverse = precision[0]
    weights = band_weight[0]
    rows, columns = own.shape
    panel = SIDE * rows
    at_t = lax.axis_index("tm")
    count_t = lax.axis_size("tm")
    at_x = lax.axis_index("x")
    where = jnp.stack(
        [
            lax.axis_index("y").astype(jnp.int32),
            at_x.astype(jnp.int32),
            (at_t + 1 < count_t).astype(jnp.int32),
            (at_t + 2 < count_t).astype(jnp.int32),
        ]
    )
    unit = 2 * panel * panel * columns

    crossed, y_message = call(
        prepare,
        (band_offset,),
        far(own, inverse, weights, prior_mean, innovation, seen_sites),
        ((rows, columns), (SIDE, 2 * rows + 8, columns)),
    )
    y_in = swap(y_message, "y")
    crossed_pieces = ring(crossed, "x")
    gain, x_message = call(
        first_gain,
        (where,),
        (y_in, *far(*crossed_pieces)),
        ((panel, panel), (SIDE, panel + 8, panel)),
        ((panel, columns),),
        unit,
    )
    gain_in = swap(x_message, "x")
    later_pieces = ring_shifted(gain, 1)
    (blocks,) = call(
        cut_blocks, (where,), (y_in, *far(*crossed_pieces)), ((2 * panel, panel),), ((panel, columns),)
    )
    gain_2, x_message, shift, c_message, wide_high, wide_low = call(
        second_gain,
        (where, band_offset),
        (*far(weights, gain), gain_in, *far(*later_pieces), y_in),
        ((panel, panel), (SIDE, panel, panel), (8, panel), (panel + 8, columns)),
        ((columns, panel),),
        unit,
        coarse=((panel, columns),) * 2,
    )
    gain_2_in = swap(x_message, "x")
    gain_pieces = ring(gain, "y")
    gain_2_later = shifted(gain_2, 2)
    c_in = shifted(c_message, 1)
    next_offsets = c_in[panel + NBAND + 2, 0:8].astype(jnp.int32)
    later_rows, *later_halves = call(
        later_inputs, (next_offsets,), far(c_in), ((8, columns),), coarse=((panel, columns),) * 4
    )
    part, shift_2, gain_2_pair, wide_high, wide_low = call(
        first_spread,
        (where,),
        (
            *far(wide_high, wide_low), gain_2_in, *far(*later_halves, later_rows, blocks),
            *far(gain, *gain_pieces[1:], shift, gain_2, gain_2_later),
        ),
        ((SIDE, panel, panel), (8, panel), (2 * panel, panel)),
        ((columns, panel),),
        3 * unit,
        coarse=((panel, columns),) * 2,
    )
    parts = swap(part, "x")
    gain_2_pieces = ring(gain_2_pair, "y")
    (spread_2,) = call(join_spread, (), (parts, *far(blocks, shift_2)), ((panel + 8, panel),))
    later = shifted(spread_2, 2)
    (y_message,) = call(
        four_times, (), (later,), ((SIDE, panel + 8, panel),), unread=gain_2_pieces[1:]
    )
    y_in = swap(y_message, "y")
    x_message, shift_4 = call(
        second_spread,
        (where,),
        (*far(gain_2, wide_high, wide_low, spread_2), y_in, *far(*gain_2_pieces)),
        ((SIDE, rows, columns + 2 * panel), (8, panel)),
        ((columns, panel), (columns, panel)),
        3 * unit,
    )
    last_in = swap(x_message, "x")
    final_gain, final_spread = call(finish, (), (last_in,), ((rows, columns), (rows, columns)))
    final_shift = lax.dynamic_slice_in_dim(shift_4[0], at_x * rows, rows, 0)
    return final_gain[None], final_shift[None], final_spread[None]


def solution(mesh):
    count = mesh.devices.shape[0]
    grid = Mesh(mesh.devices.reshape(count, SIDE, SIDE), ("tm", "y", "x"))
    row = ("y", "x")
    in_specs = (
        P("tm", row, None),
        P("tm", row, None),
        P("tm", None, None),
        P("tm", None),
        P("tm", row),
        P("tm", None),
        P("tm", None),
    )
    out_specs = (P("tm", row, None), P("tm", row), P("tm", row, None))
    return jax.shard_map(body, mesh=grid, in_specs=in_specs, out_specs=out_specs, check_vma=False)
```

```python
import math

import jax
import jax.numpy as jnp
from jax import lax
from jax.experimental import pallas as pl
from jax.experimental.pallas import tpu as pltpu
from jax.sharding import Mesh, PartitionSpec as P

NBAND = 5
SIDE = 4

HIGHEST = lax.Precision.HIGHEST
F32 = jnp.float32


def halves(array):
    high = array.astype(jnp.bfloat16)
    return high, (array - high.astype(F32)).astype(jnp.bfloat16)


def three(left, right, contract):
    def one(first, second):
        return lax.dot_general(first, second, (contract, ((), ())), preferred_element_type=F32)

    left_high, left_low = left
    right_high, right_low = right
    return one(left_high, right_high) + (one(left_high, right_low) + one(left_low, right_high))


def dot_t(left, right):
    return three(halves(left), halves(right), ((1,), (1,)))


def exact_dot_t(left, right):
    return lax.dot_general(
        left, right, (((1,), (1,)), ((), ())), precision=HIGHEST, preferred_element_type=F32
    )


def vector_times(row, matrix):
    return exact_dot_t(jnp.broadcast_to(row, (8, row.shape[1])), matrix)[0:1]


def row_times(row, matrix_halves):
    whole = jnp.broadcast_to(row, (8, row.shape[1]))
    return three(halves(whole), matrix_halves, ((1,), (1,)))[0:1]


LANES = 128


def tiles(array):
    return [array[:, i : i + LANES] for i in range(0, array.shape[1], LANES)]


def low_lanes(rows, width):
    return lax.broadcasted_iota(jnp.int32, (rows, LANES), 1) < width


def swap_tiles(blocks):
    width = LANES // 2
    low = low_lanes(blocks[0].shape[0], width)
    rolled = [pltpu.roll(block, width, 1) for block in blocks]
    out = []
    for b in range(SIDE):
        for half in range(SIDE // 2):
            ends = []
            for side in range(2):
                at = (2 * half + side) * SIDE + b
                ends.append((blocks if at % 2 == side else rolled)[at // 2])
            out.append(jnp.where(low, ends[0], ends[1]))
    return out


def swap_lanes(array):
    return jnp.concatenate(swap_tiles(tiles(array)), axis=1)


def band_tiles(blocks, weights, offset_at):
    rows = blocks[0].shape[0]
    width = LANES // 2
    low = low_lanes(rows, width)
    zero = jnp.zeros((rows, LANES), F32)
    turned = [zero] + [pltpu.roll(block, width, 1) for block in blocks] + [zero]
    moved = [jnp.where(low, turned[i], turned[i + 1]) for i in range(len(blocks) + 1)]
    totals = [zero] * len(blocks)
    for b in range(NBAND):
        distance = offset_at(b) + width
        near = low_lanes(rows, LANES - distance)
        back = lax.rem(LANES - distance, LANES)
        rolled = [pltpu.roll(block, back, 1) for block in moved]
        for i in range(len(blocks)):
            weight = weights[b : b + 1, i * LANES : (i + 1) * LANES]
            totals[i] = totals[i] + weight * jnp.where(near, rolled[i], rolled[i + 1])
    return totals


def bands(array, weights, offset_at):
    return jnp.concatenate(band_tiles(tiles(array), weights, offset_at), axis=1)


def wide(ref, rows):
    return jnp.concatenate([ref[i, 0:rows, :] for i in range(SIDE)], axis=1)


STEPS = (0, 1, 3, 2)


def sources(pieces, at):
    return [(piece, lax.rem(at + SIDE - step, SIDE)) for piece, step in zip(pieces, STEPS)]


def place_tall(pieces, at_y, out_ref, row0=0):
    panel = out_ref.shape[0] // SIDE
    chunk = panel // SIDE
    for piece, source in sources(pieces, at_y):
        for b in range(SIDE):
            out_ref[pl.ds(pl.multiple_of(b * panel + source * chunk, chunk), chunk), :] = piece[
                row0 + b * chunk : row0 + (b + 1) * chunk, :
            ]


def first_message(offsets, own, inverse, weights, prior, innovation, sites, y_out, c_out):
    rows, columns = own.shape
    matrix = own[...]
    state = lax.broadcasted_iota(jnp.int32, (columns, sites.shape[1]), 0)
    matches = (state == sites[...]).astype(F32)
    pulled = vector_times(innovation[...], matches)
    filtered = prior[...] + vector_times(pulled, matrix)
    for i in range(SIDE):
        y_out[i, 0:rows, :] = inverse[...]
        y_out[i, rows:, :] = jnp.zeros((8, columns), F32)
        y_out[i, rows : rows + 1, 0:rows] = filtered
    c_out[0:rows, :] = matrix
    c_out[rows:, :] = jnp.zeros((8, columns), F32)
    c_out[rows : rows + NBAND, :] = weights[...]
    lane = lax.broadcasted_iota(jnp.int32, (1, columns), 1)
    held = jnp.zeros((1, columns), jnp.int32)
    for b in range(NBAND):
        held = jnp.where(lane == b, offsets[0, b], held)
    c_out[rows + NBAND : rows + NBAND + 1, :] = held.astype(F32)


def cross(offsets, own, weights, crossed_out):
    crossed_out[...] = bands(own[...], weights[...], lambda b: offsets[0, b])


def place_rows(pieces, at, out):
    rows = pieces[0].shape[0]
    for piece, source in sources(pieces, at):
        out[pl.ds(pl.multiple_of(source * rows, rows), rows), :] = piece[...]


def pick_chunks(ref, at_x):
    panel = ref.shape[0]
    odd = lax.rem(at_x, 2)
    base = lax.div(at_x, 2) * LANES
    low = low_lanes(panel, LANES // 2)
    parts = []
    for i in range(SIDE):
        part = ref[:, pl.ds(pl.multiple_of(i * panel + base, LANES), LANES)]
        turn = odd if i % 2 == 0 else 1 - odd
        parts.append(pltpu.roll(part, turn * (LANES // 2), 1))
    return jnp.where(low, parts[0], parts[1]), jnp.where(low, parts[2], parts[3])


def first_gain(where, y_in, x0, x1, x2, x3, gain_out, block_out, x_out, crossed):
    rows = x0.shape[0]
    panel = SIDE * rows
    place_rows((x0, x1, x2, x3), where[1], crossed)
    inverse = jnp.concatenate([y_in[i, 0:rows, :] for i in range(SIDE)], axis=0)
    gain = dot_t(crossed[...], inverse)
    gain_out[...] = gain
    tail = jnp.concatenate([y_in[i, rows : rows + 1, 0:rows] for i in range(SIDE)], axis=1)
    tail = jnp.broadcast_to(tail, (8, panel))
    for i in range(SIDE):
        x_out[i, 0:panel, :] = gain
        x_out[i, panel:, :] = tail
    first, second = pick_chunks(crossed, where[1])
    block_out[:, 0:LANES] = first
    block_out[:, LANES:] = second


def second_gain(
    where, offsets, weights, gain, x_in, e0, e1, e2, e3, u1, u2, u3, u4,
    gain_out, x_out, shift_out, rows_out, high_out, low_out, tall,
):
    panel = gain.shape[0]
    at_y = where[0]
    gain_wide = halves(wide(x_in, panel))
    high_out[...] = gain_wide[0]
    low_out[...] = gain_wide[1]
    place_tall((e0, e1, e2, e3), at_y, tall)
    product = three(gain_wide, halves(tall[...]), ((1,), (0,)))
    gain_2 = jnp.where(where[2] == 1, product, gain[...])
    gain_out[...] = gain_2
    for i in range(SIDE):
        x_out[i] = gain_2
    filtered = jnp.concatenate([x_in[i, panel : panel + 8, :] for i in range(SIDE)], axis=1)
    natural = swap_lanes(filtered)
    forward = swap_lanes(bands(natural, weights[...], lambda b: offsets[0, b]))
    mine = jnp.zeros((1, panel), F32)
    for i in range(SIDE):
        mine = mine + jnp.where(at_y == i, natural[0:1, i * panel : (i + 1) * panel], 0.0)
    shift_out[...] = jnp.broadcast_to(mine - row_times(forward[0:1], gain_wide), (8, panel))
    rows_out[0:4, :] = filtered[0:4]
    rows_out[4:, :] = forward[0:4]


def later_inputs(offsets, piece, own_high, own_low, crossed_high, crossed_low):
    rows = own_high.shape[0]
    step = 16
    weights = piece[rows : rows + NBAND, :]

    def put(at, blocks, high_out, low_out):
        for i, block in enumerate(swap_tiles(blocks)):
            high, low = halves(block)
            high_out[at : at + step, i * LANES : (i + 1) * LANES] = high
            low_out[at : at + step, i * LANES : (i + 1) * LANES] = low

    for at in range(0, rows, step):
        blocks = tiles(piece[at : at + step, :])
        put(at, blocks, own_high, own_low)
        put(at, band_tiles(blocks, weights, lambda b: offsets[b]), crossed_high, crossed_low)


def first_spread(
    where, wide_high, wide_low, gain_2_in,
    later_rows, block, own, e0, e1, e2, e3, shift, gain_2, gain_2_later,
    h0, h1, h2, h3, l0, l1, l2, l3, g0, g1, g2, g3, k0, k1, k2, k3,
    part_out, shift_out, pair_out, high_out, low_out,
    tall, own_high, own_low, crossed_high, crossed_low,
):
    place_rows((h0, h1, h2, h3), where[0], own_high)
    place_rows((l0, l1, l2, l3), where[0], own_low)
    place_rows((g0, g1, g2, g3), where[0], crossed_high)
    place_rows((k0, k1, k2, k3), where[0], crossed_low)
    panel = e0.shape[0]
    at_y = where[0]
    pair_out[0:panel, :] = gain_2[...]
    pair_out[panel:, :] = gain_2_later[...]
    gain_wide = (wide_high[...], wide_low[...])
    gain_2_wide = halves(wide(gain_2_in, panel))
    high_out[...] = gain_2_wide[0]
    low_out[...] = gain_2_wide[1]
    across = ((1,), (1,))
    turned = three(gain_wide, (own_high[...], own_low[...]), across) - three(
        gain_2_wide, (crossed_high[...], crossed_low[...]), across
    )
    moved = row_times(later_rows[0:1, :], gain_wide) - row_times(
        later_rows[4:5, :], gain_2_wide
    )
    inside = where[2] == 1
    shift_out[...] = shift[...] + jnp.where(inside, moved, 0.0)
    turned = halves(jnp.where(inside, turned, 0.0) - block[...])
    place_tall((e0, e1, e2, e3), at_y, tall)
    twice = jnp.concatenate(swap_tiles(tiles(jnp.concatenate([own[...]] * 2, axis=0))), axis=1)
    mine = low_lanes(panel, LANES // 2) == (lax.rem(where[1], 2) == 0)
    at_x = pl.multiple_of(lax.div(where[1], 2) * LANES, LANES)
    for i in range(SIDE):
        part_out[i] = three(halves(tall[i * panel : (i + 1) * panel, :]), turned, across)
        turned_own = twice[:, i * panel : (i + 1) * panel].T
        part_out[i, :, pl.ds(at_x, LANES)] += jnp.where(mine, turned_own, 0.0)


def join_spread(parts, shift, out):
    panel = parts.shape[1]
    out[0:panel, :] = ((parts[0] + parts[1]) + (parts[2] + parts[3])).T
    out[panel:, :] = shift[...]


def four_times(block, p1, p2, out):
    for i in range(SIDE):
        out[i] = block[...]


def second_spread(
    where, gain_2, wide_high, wide_low, spread, y_in, a0, a1, a2, a3,
    x_out, shift_out, tall, later_tall,
):
    panel = gain_2.shape[0]
    rows = panel // SIDE
    columns = SIDE * panel
    at_y = where[0]
    inside = where[3] == 1
    gain_2_wide = (wide_high[...], wide_low[...])
    for i in range(SIDE):
        for b in range(SIDE):
            tall[b * panel + i * rows : b * panel + (i + 1) * rows, :] = y_in[
                i, b * rows : (b + 1) * rows, :
            ]
    along = ((1,), (0,))
    turned = halves(jnp.where(inside, three(gain_2_wide, halves(tall[...]), along), 0.0))
    shifts = jnp.concatenate([y_in[i, panel : panel + 8, :] for i in range(SIDE)], axis=1)
    moved = row_times(swap_lanes(shifts)[0:1], gain_2_wide)
    shift_out[...] = spread[panel:, :] + jnp.where(inside, moved, 0.0)
    pieces = (a0, a1, a2, a3)
    place_tall(pieces, at_y, later_tall, panel)
    gain_4 = jnp.where(inside, three(gain_2_wide, halves(later_tall[...]), along), gain_2[...])
    for i in range(SIDE):
        x_out[i, :, columns : columns + panel] = gain_4[i * rows : (i + 1) * rows]
    for piece, source in sources(pieces, at_y):
        tall[pl.ds(pl.multiple_of(source * panel, panel), panel), :] = piece[0:panel, :]
    part = three(turned, halves(tall[...]), ((1,), (1,)))
    for i in range(SIDE):
        x_out[i, :, 0:columns] = part[i * rows : (i + 1) * rows]
    odd = lax.rem(where[1], 2)
    base = lax.div(where[1], 2) * LANES
    mine = low_lanes(panel, LANES // 2) == (odd == 0)
    for c in range(SIDE):
        kept = spread[0:panel, (c // 2) * LANES : (c // 2 + 1) * LANES]
        turn = odd if c % 2 == 0 else 1 - odd
        kept = jnp.where(mine, pltpu.roll(kept, turn * (LANES // 2), 1), 0.0)
        at = pl.multiple_of(c * panel + base, LANES)
        for i in range(SIDE):
            x_out[i, :, pl.ds(at, LANES)] += kept[i * rows : (i + 1) * rows]


def finish(x_in, gain_out, spread_out):
    columns = gain_out.shape[1]
    gain_out[...] = swap_lanes(
        jnp.concatenate([x_in[i, :, columns:] for i in range(SIDE)], axis=1)
    )
    spread_out[...] = (x_in[0, :, 0:columns] + x_in[1, :, 0:columns]) + (
        x_in[2, :, 0:columns] + x_in[3, :, 0:columns]
    )


WHOLE = pl.BlockSpec()
UNREAD = pl.BlockSpec(memory_space=pl.ANY)
SMEM = pl.BlockSpec(memory_space=pltpu.SMEM)


def far(*arrays):
    return [pltpu.with_memory_space_constraint(a, pltpu.HBM) for a in arrays]


def call(kernel, scalars, arrays, outs, scratch=(), flops=0, unread=(), coarse=()):
    shapes = [pltpu.HBM(s, F32) for s in outs] + [pltpu.HBM(s, jnp.bfloat16) for s in coarse]
    size = sum(a.size for a in arrays) + sum(math.prod(s) for s in outs)
    return pl.pallas_call(
        kernel,
        out_shape=shapes,
        in_specs=[SMEM] * len(scalars) + [WHOLE] * len(arrays) + [UNREAD] * len(unread),
        out_specs=[WHOLE] * len(shapes),
        scratch_shapes=[pltpu.VMEM(s[:2], *(s[2:] or (F32,))) for s in scratch],
        compiler_params=pltpu.CompilerParams(vmem_limit_bytes=24 * 2**20),
        cost_estimate=pl.CostEstimate(flops=flops, bytes_accessed=4 * size, transcendentals=0),
    )(*scalars, *arrays, *unread)


def shifted(block, distance):
    count = lax.axis_size("tm")
    return lax.ppermute(block, "tm", [(i + distance, i) for i in range(count - distance)])


def swap(message, axis):
    return lax.all_to_all(message, axis, 0, 0)


def ring(block, axis):
    pieces = [block]
    for step in STEPS[1:]:
        pieces.append(lax.ppermute(block, axis, [(i, (i + step) % SIDE) for i in range(SIDE)]))
    return pieces


def ring_shifted(block, distance):
    count = lax.axis_size("tm")
    pieces = []
    for step in STEPS:
        route = [
            ((i + distance) * SIDE + j, i * SIDE + (j + step) % SIDE)
            for i in range(count - distance)
            for j in range(SIDE)
        ]
        pieces.append(lax.ppermute(block, ("tm", "y"), route))
    return pieces


def body(covariance, precision, band_weight, band_offset, prior_mean, innovation, seen_sites):
    own = covariance[0]
    inverse = precision[0]
    weights = band_weight[0]
    rows, columns = own.shape
    panel = SIDE * rows
    at_t = lax.axis_index("tm")
    count_t = lax.axis_size("tm")
    at_x = lax.axis_index("x")
    where = jnp.stack(
        [
            lax.axis_index("y").astype(jnp.int32),
            at_x.astype(jnp.int32),
            (at_t + 1 < count_t).astype(jnp.int32),
            (at_t + 2 < count_t).astype(jnp.int32),
        ]
    )
    unit = 2 * panel * panel * columns

    y_message, c_message = call(
        first_message,
        (band_offset,),
        far(own, inverse, weights, prior_mean, innovation, seen_sites),
        ((SIDE, rows + 8, columns), (rows + 8, columns)),
    )
    y_in = swap(y_message, "y")
    (crossed,) = call(cross, (band_offset,), far(own, weights), ((rows, columns),))
    crossed_pieces = ring(crossed, "x")
    c_later = shifted(c_message, 1)
    gain, crossed_block, x_message = call(
        first_gain,
        (where,),
        (y_in, *far(*crossed_pieces)),
        ((panel, panel), (panel, panel), (SIDE, panel + 8, panel)),
        ((panel, columns),),
        unit,
    )
    gain_in = swap(x_message, "x")
    later_pieces = ring_shifted(gain, 1)
    gain_pieces = ring(gain, "y")
    c_pieces = ring(c_later, "y")
    next_offsets = c_later[rows + NBAND, 0:8].astype(jnp.int32)
    gain_2, x_message, shift, rows_message, wide_high, wide_low = call(
        second_gain,
        (where, band_offset),
        (*far(weights, gain), gain_in, *far(*later_pieces)),
        ((panel, panel), (SIDE, panel, panel), (8, panel), (8, columns)),
        ((columns, panel),),
        unit,
        unread=(*gain_pieces[1:], c_later),
        coarse=((panel, columns),) * 2,
    )
    gain_2_in = swap(x_message, "x")
    gain_2_later = shifted(gain_2, 2)
    later_rows = shifted(rows_message, 1)
    later_halves = [
        call(later_inputs, (next_offsets,), far(piece), (), coarse=((rows, columns),) * 4)
        for piece in c_pieces
    ]
    later_halves = [half for halves_of in zip(*later_halves) for half in halves_of]
    part, shift_2, gain_2_pair, wide_high, wide_low = call(
        first_spread,
        (where,),
        (
            *far(wide_high, wide_low), gain_2_in, *far(later_rows, crossed_block),
            *far(own, gain, *gain_pieces[1:], shift, gain_2, gain_2_later, *later_halves),
        ),
        ((SIDE, panel, panel), (8, panel), (2 * panel, panel)),
        ((columns, panel),) + ((panel, columns, jnp.bfloat16),) * 4,
        3 * unit,
        coarse=((panel, columns),) * 2,
    )
    parts = swap(part, "x")
    gain_2_pieces = ring(gain_2_pair, "y")
    (spread_2,) = call(join_spread, (), (parts, *far(shift_2)), ((panel + 8, panel),))
    later = shifted(spread_2, 2)
    (y_message,) = call(
        four_times, (), (later,), ((SIDE, panel + 8, panel),), unread=gain_2_pieces[1:3]
    )
    y_in = swap(y_message, "y")
    x_message, shift_4 = call(
        second_spread,
        (where,),
        (*far(gain_2, wide_high, wide_low, spread_2), y_in, *far(*gain_2_pieces)),
        ((SIDE, rows, columns + panel), (8, panel)),
        ((columns, panel), (columns, panel)),
        3 * unit,
    )
    last_in = swap(x_message, "x")
    final_gain, final_spread = call(finish, (), (last_in,), ((rows, columns), (rows, columns)))
    final_shift = lax.dynamic_slice_in_dim(shift_4[0], at_x * rows, rows, 0)
    return final_gain[None], final_shift[None], final_spread[None]


def solution(mesh):
    count = mesh.devices.shape[0]
    grid = Mesh(mesh.devices.reshape(count, SIDE, SIDE), ("tm", "y", "x"))
    row = ("y", "x")
    in_specs = (
        P("tm", row, None),
        P("tm", row, None),
        P("tm", None, None),
        P("tm", None),
        P("tm", row),
        P("tm", None),
        P("tm", None),
    )
    out_specs = (P("tm", row, None), P("tm", row), P("tm", row, None))
    return jax.shard_map(body, mesh=grid, in_specs=in_specs, out_specs=out_specs, check_vma=False)
```

```python
import math

import jax
import jax.numpy as jnp
from jax import lax
from jax.experimental import pallas as pl
from jax.experimental.pallas import tpu as pltpu
from jax.sharding import Mesh, PartitionSpec as P

NBAND = 5
SIDE = 4

HIGHEST = lax.Precision.HIGHEST
F32 = jnp.float32


def halves(array):
    high = array.astype(jnp.bfloat16)
    return high, (array - high.astype(F32)).astype(jnp.bfloat16)


def three(left, right, contract):
    def one(first, second):
        return lax.dot_general(first, second, (contract, ((), ())), preferred_element_type=F32)

    left_high, left_low = left
    right_high, right_low = right
    return one(left_high, right_high) + (one(left_high, right_low) + one(left_low, right_high))


def dot_t(left, right):
    return three(halves(left), halves(right), ((1,), (1,)))


def exact_dot_t(left, right):
    return lax.dot_general(
        left, right, (((1,), (1,)), ((), ())), precision=HIGHEST, preferred_element_type=F32
    )


def vector_times(row, matrix):
    return exact_dot_t(jnp.broadcast_to(row, (8, row.shape[1])), matrix)[0:1]


def row_times(row, matrix_halves):
    whole = jnp.broadcast_to(row, (8, row.shape[1]))
    return three(halves(whole), matrix_halves, ((1,), (1,)))[0:1]


LANES = 128


def tiles(array):
    return [array[:, i : i + LANES] for i in range(0, array.shape[1], LANES)]


def low_lanes(rows, width):
    return lax.broadcasted_iota(jnp.int32, (rows, LANES), 1) < width


def swap_tiles(blocks):
    width = LANES // 2
    low = low_lanes(blocks[0].shape[0], width)
    rolled = [pltpu.roll(block, width, 1) for block in blocks]
    out = []
    for b in range(SIDE):
        for half in range(SIDE // 2):
            ends = []
            for side in range(2):
                at = (2 * half + side) * SIDE + b
                ends.append((blocks if at % 2 == side else rolled)[at // 2])
            out.append(jnp.where(low, ends[0], ends[1]))
    return out


def swap_lanes(array):
    return jnp.concatenate(swap_tiles(tiles(array)), axis=1)


def band_tiles(blocks, weights, offset_at):
    rows = blocks[0].shape[0]
    width = LANES // 2
    low = low_lanes(rows, width)
    zero = jnp.zeros((rows, LANES), F32)
    turned = [zero] + [pltpu.roll(block, width, 1) for block in blocks] + [zero]
    moved = [jnp.where(low, turned[i], turned[i + 1]) for i in range(len(blocks) + 1)]
    totals = [zero] * len(blocks)
    for b in range(NBAND):
        distance = offset_at(b) + width
        near = low_lanes(rows, LANES - distance)
        back = lax.rem(LANES - distance, LANES)
        rolled = [pltpu.roll(block, back, 1) for block in moved]
        for i in range(len(blocks)):
            weight = weights[b : b + 1, i * LANES : (i + 1) * LANES]
            totals[i] = totals[i] + weight * jnp.where(near, rolled[i], rolled[i + 1])
    return totals


def bands(array, weights, offset_at):
    return jnp.concatenate(band_tiles(tiles(array), weights, offset_at), axis=1)


def wide(ref, rows):
    return jnp.concatenate([ref[i, 0:rows, :] for i in range(SIDE)], axis=1)


STEPS = (0, 1, 3, 2)


def sources(pieces, at):
    return [(piece, lax.rem(at + SIDE - step, SIDE)) for piece, step in zip(pieces, STEPS)]


def place_tall(pieces, at_y, out_ref, row0=0):
    panel = out_ref.shape[0] // SIDE
    chunk = panel // SIDE
    for piece, source in sources(pieces, at_y):
        for b in range(SIDE):
            out_ref[pl.ds(pl.multiple_of(b * panel + source * chunk, chunk), chunk), :] = piece[
                row0 + b * chunk : row0 + (b + 1) * chunk, :
            ]


def prepare(offsets, own, inverse, weights, prior, innovation, sites, crossed_out, y_out):
    rows, columns = own.shape
    matrix = own[...]
    crossed_out[...] = bands(matrix, weights[...], lambda b: offsets[0, b])
    state = lax.broadcasted_iota(jnp.int32, (columns, sites.shape[1]), 0)
    matches = (state == sites[...]).astype(F32)
    pulled = vector_times(innovation[...], matches)
    filtered = prior[...] + vector_times(pulled, matrix)
    for i in range(SIDE):
        y_out[i, 0:rows, :] = inverse[...]
        y_out[i, rows : 2 * rows, :] = matrix
        y_out[i, 2 * rows :, :] = jnp.zeros((8, columns), F32)
        y_out[i, 2 * rows : 2 * rows + 1, 0:rows] = filtered


def place_rows(pieces, at, out):
    rows = pieces[0].shape[0]
    for piece, source in sources(pieces, at):
        out[pl.ds(pl.multiple_of(source * rows, rows), rows), :] = piece[...]


def pick_chunks(ref, at_x):
    panel = ref.shape[0]
    odd = lax.rem(at_x, 2)
    base = lax.div(at_x, 2) * LANES
    low = low_lanes(panel, LANES // 2)
    parts = []
    for i in range(SIDE):
        part = ref[:, pl.ds(pl.multiple_of(i * panel + base, LANES), LANES)]
        turn = odd if i % 2 == 0 else 1 - odd
        parts.append(pltpu.roll(part, turn * (LANES // 2), 1))
    return jnp.where(low, parts[0], parts[1]), jnp.where(low, parts[2], parts[3])


def first_gain(
    where, offsets, y_in, x0, x1, x2, x3, weights, gain_out, block_out, c_out, x_out, crossed
):
    rows = x0.shape[0]
    panel = SIDE * rows
    place_rows((x0, x1, x2, x3), where[1], crossed)
    inverse = jnp.concatenate([y_in[i, 0:rows, :] for i in range(SIDE)], axis=0)
    gain = dot_t(crossed[...], inverse)
    gain_out[...] = gain
    tail = jnp.concatenate(
        [y_in[i, 2 * rows : 2 * rows + 1, 0:rows] for i in range(SIDE)], axis=1
    )
    tail = jnp.broadcast_to(tail, (8, panel))
    for i in range(SIDE):
        x_out[i, 0:panel, :] = gain
        x_out[i, panel:, :] = tail
    first, second = pick_chunks(crossed, where[1])
    block_out[:, 0:LANES] = first
    block_out[:, LANES:] = second
    for i in range(SIDE):
        c_out[i * rows : (i + 1) * rows, :] = y_in[i, rows : 2 * rows, :]
    lane = lax.broadcasted_iota(jnp.int32, (1, c_out.shape[1]), 1)
    held = jnp.zeros((1, c_out.shape[1]), jnp.int32)
    for b in range(NBAND):
        held = jnp.where(lane == b, offsets[0, b], held)
    c_out[panel:, :] = jnp.broadcast_to(held.astype(F32), (8, c_out.shape[1]))
    c_out[panel : panel + NBAND, :] = weights[...]


def second_gain(
    where, offsets, weights, gain, x_in, e0, e1, e2, e3, unread,
    gain_out, x_out, shift_out, rows_out, high_out, low_out, tall,
):
    panel = gain.shape[0]
    at_y = where[0]
    gain_wide = halves(wide(x_in, panel))
    high_out[...] = gain_wide[0]
    low_out[...] = gain_wide[1]
    place_tall((e0, e1, e2, e3), at_y, tall)
    product = three(gain_wide, halves(tall[...]), ((1,), (0,)))
    gain_2 = jnp.where(where[2] == 1, product, gain[...])
    gain_out[...] = gain_2
    for i in range(SIDE):
        x_out[i] = gain_2
    filtered = jnp.concatenate([x_in[i, panel : panel + 8, :] for i in range(SIDE)], axis=1)
    natural = swap_lanes(filtered)
    forward = swap_lanes(bands(natural, weights[...], lambda b: offsets[0, b]))
    mine = jnp.zeros((1, panel), F32)
    for i in range(SIDE):
        mine = mine + jnp.where(at_y == i, natural[0:1, i * panel : (i + 1) * panel], 0.0)
    shift_out[...] = jnp.broadcast_to(mine - row_times(forward[0:1], gain_wide), (8, panel))
    rows_out[0:4, :] = filtered[0:4]
    rows_out[4:, :] = forward[0:4]


def later_inputs(offsets, c_in, own_high, own_low, crossed_high, crossed_low):
    panel, columns = own_high.shape
    matrix = c_in[0:panel, :]
    weights = c_in[panel : panel + NBAND, :]
    high, low = halves(matrix)
    reach = 3 * LANES
    ahead = (
        lax.broadcasted_iota(jnp.int32, (reach, LANES), 0)
        - lax.broadcasted_iota(jnp.int32, (reach, LANES), 1)
        - LANES
    )
    count = columns // LANES
    crossed = []
    for i in range(count):
        first = max(i - 1, 0)
        last = min(i + 2, count)
        spread = jnp.zeros((reach, LANES), F32)
        for b in range(NBAND):
            weight = weights[b : b + 1, i * LANES : (i + 1) * LANES]
            spread = spread + jnp.where(ahead == offsets[b], weight, 0.0)
        spread = spread[(first - i + 1) * LANES : (last - i + 1) * LANES]
        lanes = slice(first * LANES, last * LANES)
        crossed.append(three((high[:, lanes], low[:, lanes]), halves(spread), ((1,), (0,))))
    for blocks, high_out, low_out in (
        (tiles(matrix), own_high, own_low),
        (crossed, crossed_high, crossed_low),
    ):
        for i, block in enumerate(swap_tiles(blocks)):
            high, low = halves(block)
            high_out[:, i * LANES : (i + 1) * LANES] = high
            low_out[:, i * LANES : (i + 1) * LANES] = low


def first_spread(
    where, wide_high, wide_low, gain_2_in, own_high, own_low, crossed_high, crossed_low,
    later_rows, block, own, e0, e1, e2, e3, shift, gain_2, gain_2_later,
    part_out, shift_out, pair_out, high_out, low_out, tall,
):
    panel = e0.shape[0]
    at_y = where[0]
    pair_out[0:panel, :] = gain_2[...]
    pair_out[panel:, :] = gain_2_later[...]
    gain_wide = (wide_high[...], wide_low[...])
    gain_2_wide = halves(wide(gain_2_in, panel))
    high_out[...] = gain_2_wide[0]
    low_out[...] = gain_2_wide[1]
    across = ((1,), (1,))
    turned = three(gain_wide, (own_high[...], own_low[...]), across) - three(
        gain_2_wide, (crossed_high[...], crossed_low[...]), across
    )
    moved = row_times(later_rows[0:1, :], gain_wide) - row_times(
        later_rows[4:5, :], gain_2_wide
    )
    inside = where[2] == 1
    shift_out[...] = shift[...] + jnp.where(inside, moved, 0.0)
    turned = halves(jnp.where(inside, turned, 0.0) - block[...])
    place_tall((e0, e1, e2, e3), at_y, tall)
    twice = jnp.concatenate(swap_tiles(tiles(jnp.concatenate([own[...]] * 2, axis=0))), axis=1)
    mine = low_lanes(panel, LANES // 2) == (lax.rem(where[1], 2) == 0)
    at_x = pl.multiple_of(lax.div(where[1], 2) * LANES, LANES)
    for i in range(SIDE):
        part_out[i] = three(halves(tall[i * panel : (i + 1) * panel, :]), turned, across)
        turned_own = twice[:, i * panel : (i + 1) * panel].T
        part_out[i, :, pl.ds(at_x, LANES)] += jnp.where(mine, turned_own, 0.0)


def join_spread(parts, shift, out):
    panel = parts.shape[1]
    out[0:panel, :] = ((parts[0] + parts[1]) + (parts[2] + parts[3])).T
    out[panel:, :] = shift[...]


def four_times(block, p1, p2, p3, out):
    for i in range(SIDE):
        out[i] = block[...]


def second_spread(
    where, gain_2, wide_high, wide_low, spread, y_in, a0, a1, a2, a3,
    x_out, shift_out, tall, later_tall,
):
    panel = gain_2.shape[0]
    rows = panel // SIDE
    columns = SIDE * panel
    at_y = where[0]
    inside = where[3] == 1
    gain_2_wide = (wide_high[...], wide_low[...])
    for i in range(SIDE):
        for b in range(SIDE):
            tall[b * panel + i * rows : b * panel + (i + 1) * rows, :] = y_in[
                i, b * rows : (b + 1) * rows, :
            ]
    along = ((1,), (0,))
    turned = halves(jnp.where(inside, three(gain_2_wide, halves(tall[...]), along), 0.0))
    shifts = jnp.concatenate([y_in[i, panel : panel + 8, :] for i in range(SIDE)], axis=1)
    moved = row_times(swap_lanes(shifts)[0:1], gain_2_wide)
    shift_out[...] = spread[panel:, :] + jnp.where(inside, moved, 0.0)
    pieces = (a0, a1, a2, a3)
    place_tall(pieces, at_y, later_tall, panel)
    gain_4 = jnp.where(inside, three(gain_2_wide, halves(later_tall[...]), along), gain_2[...])
    for i in range(SIDE):
        x_out[i, :, columns : columns + panel] = gain_4[i * rows : (i + 1) * rows]
    for piece, source in sources(pieces, at_y):
        tall[pl.ds(pl.multiple_of(source * panel, panel), panel), :] = piece[0:panel, :]
    part = three(turned, halves(tall[...]), ((1,), (1,)))
    for i in range(SIDE):
        x_out[i, :, 0:columns] = part[i * rows : (i + 1) * rows]
    odd = lax.rem(where[1], 2)
    base = lax.div(where[1], 2) * LANES
    mine = low_lanes(panel, LANES // 2) == (odd == 0)
    for c in range(SIDE):
        kept = spread[0:panel, (c // 2) * LANES : (c // 2 + 1) * LANES]
        turn = odd if c % 2 == 0 else 1 - odd
        kept = jnp.where(mine, pltpu.roll(kept, turn * (LANES // 2), 1), 0.0)
        at = pl.multiple_of(c * panel + base, LANES)
        for i in range(SIDE):
            x_out[i, :, pl.ds(at, LANES)] += kept[i * rows : (i + 1) * rows]


def finish(x_in, gain_out, spread_out):
    columns = gain_out.shape[1]
    gain_out[...] = swap_lanes(
        jnp.concatenate([x_in[i, :, columns:] for i in range(SIDE)], axis=1)
    )
    spread_out[...] = (x_in[0, :, 0:columns] + x_in[1, :, 0:columns]) + (
        x_in[2, :, 0:columns] + x_in[3, :, 0:columns]
    )


WHOLE = pl.BlockSpec()
UNREAD = pl.BlockSpec(memory_space=pl.ANY)
SMEM = pl.BlockSpec(memory_space=pltpu.SMEM)


def far(*arrays):
    return [pltpu.with_memory_space_constraint(a, pltpu.HBM) for a in arrays]


def call(kernel, scalars, arrays, outs, scratch=(), flops=0, unread=(), coarse=()):
    shapes = [pltpu.HBM(s, F32) for s in outs] + [pltpu.HBM(s, jnp.bfloat16) for s in coarse]
    size = sum(a.size for a in arrays) + sum(math.prod(s) for s in outs)
    return pl.pallas_call(
        kernel,
        out_shape=shapes,
        in_specs=[SMEM] * len(scalars) + [WHOLE] * len(arrays) + [UNREAD] * len(unread),
        out_specs=[WHOLE] * len(shapes),
        scratch_shapes=[pltpu.VMEM(s, F32) for s in scratch],
        compiler_params=pltpu.CompilerParams(vmem_limit_bytes=24 * 2**20),
        cost_estimate=pl.CostEstimate(flops=flops, bytes_accessed=4 * size, transcendentals=0),
    )(*scalars, *arrays, *unread)


def shifted(block, distance):
    count = lax.axis_size("tm")
    return lax.ppermute(block, "tm", [(i + distance, i) for i in range(count - distance)])


def swap(message, axis):
    return lax.all_to_all(message, axis, 0, 0)


def ring(block, axis):
    pieces = [block]
    for step in STEPS[1:]:
        pieces.append(lax.ppermute(block, axis, [(i, (i + step) % SIDE) for i in range(SIDE)]))
    return pieces


def ring_shifted(block, distance):
    count = lax.axis_size("tm")
    pieces = []
    for step in STEPS:
        route = [
            ((i + distance) * SIDE + j, i * SIDE + (j + step) % SIDE)
            for i in range(count - distance)
            for j in range(SIDE)
        ]
        pieces.append(lax.ppermute(block, ("tm", "y"), route))
    return pieces


def body(covariance, precision, band_weight, band_offset, prior_mean, innovation, seen_sites):
    own = covariance[0]
    inverse = precision[0]
    weights = band_weight[0]
    rows, columns = own.shape
    panel = SIDE * rows
    at_t = lax.axis_index("tm")
    count_t = lax.axis_size("tm")
    at_x = lax.axis_index("x")
    where = jnp.stack(
        [
            lax.axis_index("y").astype(jnp.int32),
            at_x.astype(jnp.int32),
            (at_t + 1 < count_t).astype(jnp.int32),
            (at_t + 2 < count_t).astype(jnp.int32),
        ]
    )
    unit = 2 * panel * panel * columns

    crossed, y_message = call(
        prepare,
        (band_offset,),
        far(own, inverse, weights, prior_mean, innovation, seen_sites),
        ((rows, columns), (SIDE, 2 * rows + 8, columns)),
    )
    y_in = swap(y_message, "y")
    crossed_pieces = ring(crossed, "x")
    gain, crossed_block, c_message, x_message = call(
        first_gain,
        (where, band_offset),
        (y_in, *far(*crossed_pieces, weights)),
        ((panel, panel), (panel, panel), (panel + 8, columns), (SIDE, panel + 8, panel)),
        ((panel, columns),),
        unit,
    )
    gain_in = swap(x_message, "x")
    later_pieces = ring_shifted(gain, 1)
    c_in = shifted(c_message, 1)
    next_offsets = c_in[panel + NBAND, 0:8].astype(jnp.int32)
    gain_2, x_message, shift, rows_message, wide_high, wide_low = call(
        second_gain,
        (where, band_offset),
        (*far(weights, gain), gain_in, *far(*later_pieces)),
        ((panel, panel), (SIDE, panel, panel), (8, panel), (8, columns)),
        ((columns, panel),),
        unit,
        unread=(c_in,),
        coarse=((panel, columns),) * 2,
    )
    gain_2_in = swap(x_message, "x")
    gain_pieces = ring(gain, "y")
    gain_2_later = shifted(gain_2, 2)
    later_rows = shifted(rows_message, 1)
    later_halves = call(
        later_inputs, (next_offsets,), far(c_in), (), coarse=((panel, columns),) * 4
    )
    part, shift_2, gain_2_pair, wide_high, wide_low = call(
        first_spread,
        (where,),
        (
            *far(wide_high, wide_low), gain_2_in, *far(*later_halves, later_rows, crossed_block),
            *far(own, gain, *gain_pieces[1:], shift, gain_2, gain_2_later),
        ),
        ((SIDE, panel, panel), (8, panel), (2 * panel, panel)),
        ((columns, panel),),
        3 * unit,
        coarse=((panel, columns),) * 2,
    )
    parts = swap(part, "x")
    gain_2_pieces = ring(gain_2_pair, "y")
    (spread_2,) = call(join_spread, (), (parts, *far(shift_2)), ((panel + 8, panel),))
    later = shifted(spread_2, 2)
    (y_message,) = call(
        four_times, (), (later,), ((SIDE, panel + 8, panel),), unread=gain_2_pieces[1:]
    )
    y_in = swap(y_message, "y")
    x_message, shift_4 = call(
        second_spread,
        (where,),
        (*far(gain_2, wide_high, wide_low, spread_2), y_in, *far(*gain_2_pieces)),
        ((SIDE, rows, columns + panel), (8, panel)),
        ((columns, panel), (columns, panel)),
        3 * unit,
    )
    last_in = swap(x_message, "x")
    final_gain, final_spread = call(finish, (), (last_in,), ((rows, columns), (rows, columns)))
    final_shift = lax.dynamic_slice_in_dim(shift_4[0], at_x * rows, rows, 0)
    return final_gain[None], final_shift[None], final_spread[None]


def solution(mesh):
    count = mesh.devices.shape[0]
    grid = Mesh(mesh.devices.reshape(count, SIDE, SIDE), ("tm", "y", "x"))
    row = ("y", "x")
    in_specs = (
        P("tm", row, None),
        P("tm", row, None),
        P("tm", None, None),
        P("tm", None),
        P("tm", row),
        P("tm", None),
        P("tm", None),
    )
    out_specs = (P("tm", row, None), P("tm", row), P("tm", row, None))
    return jax.shard_map(body, mesh=grid, in_specs=in_specs, out_specs=out_specs, check_vma=False)
```

```python
import math

import jax
import jax.numpy as jnp
from jax import lax
from jax.experimental import pallas as pl
from jax.experimental.pallas import tpu as pltpu
from jax.sharding import Mesh, PartitionSpec as P

NBAND = 5
SIDE = 4

HIGHEST = lax.Precision.HIGHEST
F32 = jnp.float32


def halves(array):
    high = array.astype(jnp.bfloat16)
    return high, (array - high.astype(F32)).astype(jnp.bfloat16)


def three(left, right, contract):
    def one(first, second):
        return lax.dot_general(first, second, (contract, ((), ())), preferred_element_type=F32)

    left_high, left_low = left
    right_high, right_low = right
    return one(left_high, right_high) + (one(left_high, right_low) + one(left_low, right_high))


def dot_t(left, right):
    return three(halves(left), halves(right), ((1,), (1,)))


def exact_dot_t(left, right):
    return lax.dot_general(
        left, right, (((1,), (1,)), ((), ())), precision=HIGHEST, preferred_element_type=F32
    )


def vector_times(row, matrix):
    return exact_dot_t(jnp.broadcast_to(row, (8, row.shape[1])), matrix)[0:1]


def row_times(row, matrix_halves):
    whole = jnp.broadcast_to(row, (8, row.shape[1]))
    return three(halves(whole), matrix_halves, ((1,), (1,)))[0:1]


LANES = 128


def tiles(array):
    return [array[:, i : i + LANES] for i in range(0, array.shape[1], LANES)]


def low_lanes(rows, width):
    return lax.broadcasted_iota(jnp.int32, (rows, LANES), 1) < width


def swap_tiles(blocks):
    width = LANES // 2
    low = low_lanes(blocks[0].shape[0], width)
    rolled = [pltpu.roll(block, width, 1) for block in blocks]
    out = []
    for b in range(SIDE):
        for half in range(SIDE // 2):
            ends = []
            for side in range(2):
                at = (2 * half + side) * SIDE + b
                ends.append((blocks if at % 2 == side else rolled)[at // 2])
            out.append(jnp.where(low, ends[0], ends[1]))
    return out


def swap_lanes(array):
    return jnp.concatenate(swap_tiles(tiles(array)), axis=1)


def band_tiles(blocks, weights, offset_at):
    rows = blocks[0].shape[0]
    width = LANES // 2
    low = low_lanes(rows, width)
    zero = jnp.zeros((rows, LANES), F32)
    turned = [zero] + [pltpu.roll(block, width, 1) for block in blocks] + [zero]
    moved = [jnp.where(low, turned[i], turned[i + 1]) for i in range(len(blocks) + 1)]
    totals = [zero] * len(blocks)
    for b in range(NBAND):
        distance = offset_at(b) + width
        near = low_lanes(rows, LANES - distance)
        back = lax.rem(LANES - distance, LANES)
        rolled = [pltpu.roll(block, back, 1) for block in moved]
        for i in range(len(blocks)):
            weight = weights[b : b + 1, i * LANES : (i + 1) * LANES]
            totals[i] = totals[i] + weight * jnp.where(near, rolled[i], rolled[i + 1])
    return totals


def bands(array, weights, offset_at):
    return jnp.concatenate(band_tiles(tiles(array), weights, offset_at), axis=1)


def wide(ref, rows):
    return jnp.concatenate([ref[i, 0:rows, :] for i in range(SIDE)], axis=1)


STEPS = (0, 1, 3, 2)


def sources(pieces, at):
    return [(piece, lax.rem(at + SIDE - step, SIDE)) for piece, step in zip(pieces, STEPS)]


def place_tall(pieces, at_y, out_ref, row0=0):
    panel = out_ref.shape[0] // SIDE
    chunk = panel // SIDE
    for piece, source in sources(pieces, at_y):
        for b in range(SIDE):
            out_ref[pl.ds(pl.multiple_of(b * panel + source * chunk, chunk), chunk), :] = piece[
                row0 + b * chunk : row0 + (b + 1) * chunk, :
            ]


def prepare(offsets, own, inverse, weights, prior, innovation, sites, crossed_out, y_out):
    rows, columns = own.shape
    matrix = own[...]
    crossed_out[...] = bands(matrix, weights[...], lambda b: offsets[0, b])
    state = lax.broadcasted_iota(jnp.int32, (columns, sites.shape[1]), 0)
    matches = (state == sites[...]).astype(F32)
    pulled = vector_times(innovation[...], matches)
    filtered = prior[...] + vector_times(pulled, matrix)
    for i in range(SIDE):
        y_out[i, 0:rows, :] = inverse[...]
        y_out[i, rows : 2 * rows, :] = matrix
        y_out[i, 2 * rows :, :] = jnp.zeros((8, columns), F32)
        y_out[i, 2 * rows : 2 * rows + 1, 0:rows] = filtered


def place_rows(pieces, at, out):
    rows = pieces[0].shape[0]
    for piece, source in sources(pieces, at):
        out[pl.ds(pl.multiple_of(source * rows, rows), rows), :] = piece[...]


def pick_chunks(ref, at_x):
    panel = ref.shape[0]
    odd = lax.rem(at_x, 2)
    base = lax.div(at_x, 2) * LANES
    low = low_lanes(panel, LANES // 2)
    parts = []
    for i in range(SIDE):
        part = ref[:, pl.ds(pl.multiple_of(i * panel + base, LANES), LANES)]
        turn = odd if i % 2 == 0 else 1 - odd
        parts.append(pltpu.roll(part, turn * (LANES // 2), 1))
    return jnp.where(low, parts[0], parts[1]), jnp.where(low, parts[2], parts[3])


def first_gain(
    where, offsets, y_in, x0, x1, x2, x3, weights, gain_out, block_out, c_out, x_out, crossed
):
    rows = x0.shape[0]
    panel = SIDE * rows
    place_rows((x0, x1, x2, x3), where[1], crossed)
    inverse = jnp.concatenate([y_in[i, 0:rows, :] for i in range(SIDE)], axis=0)
    gain = dot_t(crossed[...], inverse)
    gain_out[...] = gain
    tail = jnp.concatenate(
        [y_in[i, 2 * rows : 2 * rows + 1, 0:rows] for i in range(SIDE)], axis=1
    )
    tail = jnp.broadcast_to(tail, (8, panel))
    for i in range(SIDE):
        x_out[i, 0:panel, :] = gain
        x_out[i, panel:, :] = tail
    first, second = pick_chunks(crossed, where[1])
    block_out[:, 0:LANES] = first
    block_out[:, LANES:] = second
    for i in range(SIDE):
        c_out[i * rows : (i + 1) * rows, :] = y_in[i, rows : 2 * rows, :]
    lane = lax.broadcasted_iota(jnp.int32, (1, c_out.shape[1]), 1)
    held = jnp.zeros((1, c_out.shape[1]), jnp.int32)
    for b in range(NBAND):
        held = jnp.where(lane == b, offsets[0, b], held)
    c_out[panel:, :] = jnp.broadcast_to(held.astype(F32), (8, c_out.shape[1]))
    c_out[panel : panel + NBAND, :] = weights[...]


def second_gain(
    where, offsets, weights, gain, x_in, e0, e1, e2, e3, unread,
    gain_out, x_out, shift_out, rows_out, high_out, low_out, tall,
):
    panel = gain.shape[0]
    at_y = where[0]
    gain_wide = halves(wide(x_in, panel))
    high_out[...] = gain_wide[0]
    low_out[...] = gain_wide[1]
    place_tall((e0, e1, e2, e3), at_y, tall)
    product = three(gain_wide, halves(tall[...]), ((1,), (0,)))
    gain_2 = jnp.where(where[2] == 1, product, gain[...])
    gain_out[...] = gain_2
    for i in range(SIDE):
        x_out[i] = gain_2
    filtered = jnp.concatenate([x_in[i, panel : panel + 8, :] for i in range(SIDE)], axis=1)
    natural = swap_lanes(filtered)
    forward = swap_lanes(bands(natural, weights[...], lambda b: offsets[0, b]))
    mine = jnp.zeros((1, panel), F32)
    for i in range(SIDE):
        mine = mine + jnp.where(at_y == i, natural[0:1, i * panel : (i + 1) * panel], 0.0)
    shift_out[...] = jnp.broadcast_to(mine - row_times(forward[0:1], gain_wide), (8, panel))
    rows_out[0:4, :] = filtered[0:4]
    rows_out[4:, :] = forward[0:4]


def later_inputs(offsets, c_in, own_high, own_low, crossed_high, crossed_low):
    panel, columns = own_high.shape
    matrix = c_in[0:panel, :]
    weights = c_in[panel : panel + NBAND, :]
    high, low = halves(matrix)
    reach = 3 * LANES
    ahead = (
        lax.broadcasted_iota(jnp.int32, (reach, LANES), 0)
        - lax.broadcasted_iota(jnp.int32, (reach, LANES), 1)
        - LANES
    )
    count = columns // LANES
    crossed = []
    for i in range(count):
        first = max(i - 1, 0)
        last = min(i + 2, count)
        spread = jnp.zeros((reach, LANES), F32)
        for b in range(NBAND):
            weight = weights[b : b + 1, i * LANES : (i + 1) * LANES]
            spread = spread + jnp.where(ahead == offsets[b], weight, 0.0)
        spread = spread[(first - i + 1) * LANES : (last - i + 1) * LANES]
        lanes = slice(first * LANES, last * LANES)
        crossed.append(three((high[:, lanes], low[:, lanes]), halves(spread), ((1,), (0,))))
    for blocks, high_out, low_out in (
        (tiles(matrix), own_high, own_low),
        (crossed, crossed_high, crossed_low),
    ):
        for i, block in enumerate(swap_tiles(blocks)):
            high, low = halves(block)
            high_out[:, i * LANES : (i + 1) * LANES] = high
            low_out[:, i * LANES : (i + 1) * LANES] = low


def first_spread(
    where, wide_high, wide_low, gain_2_in, own_high, own_low, crossed_high, crossed_low,
    later_rows, block, own, e0, e1, e2, e3, shift, gain_2, gain_2_later,
    part_out, shift_out, pair_out, high_out, low_out, tall,
):
    panel = e0.shape[0]
    at_y = where[0]
    pair_out[0:panel, :] = gain_2[...]
    pair_out[panel:, :] = gain_2_later[...]
    gain_wide = (wide_high[...], wide_low[...])
    gain_2_wide = halves(wide(gain_2_in, panel))
    high_out[...] = gain_2_wide[0]
    low_out[...] = gain_2_wide[1]
    across = ((1,), (1,))
    turned = three(gain_wide, (own_high[...], own_low[...]), across) - three(
        gain_2_wide, (crossed_high[...], crossed_low[...]), across
    )
    moved = row_times(later_rows[0:1, :], gain_wide) - row_times(
        later_rows[4:5, :], gain_2_wide
    )
    inside = where[2] == 1
    shift_out[...] = shift[...] + jnp.where(inside, moved, 0.0)
    turned = halves(jnp.where(inside, turned, 0.0) - block[...])
    place_tall((e0, e1, e2, e3), at_y, tall)
    twice = jnp.concatenate(swap_tiles(tiles(jnp.concatenate([own[...]] * 2, axis=0))), axis=1)
    mine = low_lanes(panel, LANES // 2) == (lax.rem(where[1], 2) == 0)
    at_x = pl.multiple_of(lax.div(where[1], 2) * LANES, LANES)
    for i in range(SIDE):
        part_out[i] = three(halves(tall[i * panel : (i + 1) * panel, :]), turned, across)
        turned_own = twice[:, i * panel : (i + 1) * panel].T
        part_out[i, :, pl.ds(at_x, LANES)] += jnp.where(mine, turned_own, 0.0)


def join_spread(parts, shift, out):
    panel = parts.shape[1]
    out[0:panel, :] = ((parts[0] + parts[1]) + (parts[2] + parts[3])).T
    out[panel:, :] = shift[...]


def four_times(block, p1, p2, p3, out):
    for i in range(SIDE):
        out[i] = block[...]


def second_spread(
    where, gain_2, wide_high, wide_low, spread, y_in, a0, a1, a2, a3,
    x_out, shift_out, tall, later_tall,
):
    panel = gain_2.shape[0]
    rows = panel // SIDE
    columns = SIDE * panel
    at_y = where[0]
    inside = where[3] == 1
    gain_2_wide = (wide_high[...], wide_low[...])
    for i in range(SIDE):
        for b in range(SIDE):
            tall[b * panel + i * rows : b * panel + (i + 1) * rows, :] = y_in[
                i, b * rows : (b + 1) * rows, :
            ]
    along = ((1,), (0,))
    turned = halves(jnp.where(inside, three(gain_2_wide, halves(tall[...]), along), 0.0))
    shifts = jnp.concatenate([y_in[i, panel : panel + 8, :] for i in range(SIDE)], axis=1)
    moved = row_times(swap_lanes(shifts)[0:1], gain_2_wide)
    shift_out[...] = spread[panel:, :] + jnp.where(inside, moved, 0.0)
    pieces = (a0, a1, a2, a3)
    place_tall(pieces, at_y, later_tall, panel)
    gain_4 = jnp.where(inside, three(gain_2_wide, halves(later_tall[...]), along), gain_2[...])
    for i in range(SIDE):
        x_out[i, :, columns : columns + panel] = gain_4[i * rows : (i + 1) * rows]
    for piece, source in sources(pieces, at_y):
        tall[pl.ds(pl.multiple_of(source * panel, panel), panel), :] = piece[0:panel, :]
    part = three(turned, halves(tall[...]), ((1,), (1,)))
    for i in range(SIDE):
        x_out[i, :, 0:columns] = part[i * rows : (i + 1) * rows]
    odd = lax.rem(where[1], 2)
    base = lax.div(where[1], 2) * LANES
    mine = low_lanes(panel, LANES // 2) == (odd == 0)
    for c in range(SIDE):
        kept = spread[0:panel, (c // 2) * LANES : (c // 2 + 1) * LANES]
        turn = odd if c % 2 == 0 else 1 - odd
        kept = jnp.where(mine, pltpu.roll(kept, turn * (LANES // 2), 1), 0.0)
        at = pl.multiple_of(c * panel + base, LANES)
        for i in range(SIDE):
            x_out[i, :, pl.ds(at, LANES)] += kept[i * rows : (i + 1) * rows]


def finish(x_in, gain_out, spread_out):
    columns = gain_out.shape[1]
    gain_out[...] = swap_lanes(
        jnp.concatenate([x_in[i, :, columns:] for i in range(SIDE)], axis=1)
    )
    spread_out[...] = (x_in[0, :, 0:columns] + x_in[1, :, 0:columns]) + (
        x_in[2, :, 0:columns] + x_in[3, :, 0:columns]
    )


WHOLE = pl.BlockSpec()
UNREAD = pl.BlockSpec(memory_space=pl.ANY)
SMEM = pl.BlockSpec(memory_space=pltpu.SMEM)


def far(*arrays):
    return [pltpu.with_memory_space_constraint(a, pltpu.HBM) for a in arrays]


def call(kernel, scalars, arrays, outs, scratch=(), flops=0, unread=(), coarse=()):
    shapes = [pltpu.HBM(s, F32) for s in outs] + [pltpu.HBM(s, jnp.bfloat16) for s in coarse]
    size = sum(a.size for a in arrays) + sum(math.prod(s) for s in outs)
    return pl.pallas_call(
        kernel,
        out_shape=shapes,
        in_specs=[SMEM] * len(scalars) + [WHOLE] * len(arrays) + [UNREAD] * len(unread),
        out_specs=[WHOLE] * len(shapes),
        scratch_shapes=[pltpu.VMEM(s, F32) for s in scratch],
        compiler_params=pltpu.CompilerParams(vmem_limit_bytes=24 * 2**20),
        cost_estimate=pl.CostEstimate(flops=flops, bytes_accessed=4 * size, transcendentals=0),
    )(*scalars, *arrays, *unread)


def shifted(block, distance):
    count = lax.axis_size("tm")
    return lax.ppermute(block, "tm", [(i + distance, i) for i in range(count - distance)])


def swap(message, axis):
    return lax.all_to_all(message, axis, 0, 0)


def ring(block, axis):
    pieces = [block]
    for step in STEPS[1:]:
        pieces.append(lax.ppermute(block, axis, [(i, (i + step) % SIDE) for i in range(SIDE)]))
    return pieces


def body(covariance, precision, band_weight, band_offset, prior_mean, innovation, seen_sites):
    own = covariance[0]
    inverse = precision[0]
    weights = band_weight[0]
    rows, columns = own.shape
    panel = SIDE * rows
    at_t = lax.axis_index("tm")
    count_t = lax.axis_size("tm")
    at_x = lax.axis_index("x")
    where = jnp.stack(
        [
            lax.axis_index("y").astype(jnp.int32),
            at_x.astype(jnp.int32),
            (at_t + 1 < count_t).astype(jnp.int32),
            (at_t + 2 < count_t).astype(jnp.int32),
        ]
    )
    unit = 2 * panel * panel * columns

    crossed, y_message = call(
        prepare,
        (band_offset,),
        far(own, inverse, weights, prior_mean, innovation, seen_sites),
        ((rows, columns), (SIDE, 2 * rows + 8, columns)),
    )
    y_in = swap(y_message, "y")
    crossed_pieces = ring(crossed, "x")
    gain, crossed_block, c_message, x_message = call(
        first_gain,
        (where, band_offset),
        (y_in, *far(*crossed_pieces, weights)),
        ((panel, panel), (panel, panel), (panel + 8, columns), (SIDE, panel + 8, panel)),
        ((panel, columns),),
        unit,
    )
    gain_in = swap(x_message, "x")
    later_pieces = ring(shifted(gain, 1), "y")
    c_in = shifted(c_message, 1)
    next_offsets = c_in[panel + NBAND, 0:8].astype(jnp.int32)
    later_halves = call(
        later_inputs, (next_offsets,), far(c_in), (), coarse=((panel, columns),) * 4
    )
    gain_2, x_message, shift, rows_message, wide_high, wide_low = call(
        second_gain,
        (where, band_offset),
        (*far(weights, gain), gain_in, *far(*later_pieces)),
        ((panel, panel), (SIDE, panel, panel), (8, panel), (8, columns)),
        ((columns, panel),),
        unit,
        unread=(later_halves[0],),
        coarse=((panel, columns),) * 2,
    )
    gain_2_in = swap(x_message, "x")
    gain_pieces = ring(gain, "y")
    gain_2_later = shifted(gain_2, 2)
    later_rows = shifted(rows_message, 1)
    part, shift_2, gain_2_pair, wide_high, wide_low = call(
        first_spread,
        (where,),
        (
            *far(wide_high, wide_low), gain_2_in, *far(*later_halves, later_rows, crossed_block),
            *far(own, gain, *gain_pieces[1:], shift, gain_2, gain_2_later),
        ),
        ((SIDE, panel, panel), (8, panel), (2 * panel, panel)),
        ((columns, panel),),
        3 * unit,
        coarse=((panel, columns),) * 2,
    )
    parts = swap(part, "x")
    gain_2_pieces = ring(gain_2_pair, "y")
    (spread_2,) = call(join_spread, (), (parts, *far(shift_2)), ((panel + 8, panel),))
    later = shifted(spread_2, 2)
    (y_message,) = call(
        four_times, (), (later,), ((SIDE, panel + 8, panel),), unread=gain_2_pieces[1:]
    )
    y_in = swap(y_message, "y")
    x_message, shift_4 = call(
        second_spread,
        (where,),
        (*far(gain_2, wide_high, wide_low, spread_2), y_in, *far(*gain_2_pieces)),
        ((SIDE, rows, columns + panel), (8, panel)),
        ((columns, panel), (columns, panel)),
        3 * unit,
    )
    last_in = swap(x_message, "x")
    final_gain, final_spread = call(finish, (), (last_in,), ((rows, columns), (rows, columns)))
    final_shift = lax.dynamic_slice_in_dim(shift_4[0], at_x * rows, rows, 0)
    return final_gain[None], final_shift[None], final_spread[None]


def solution(mesh):
    count = mesh.devices.shape[0]
    grid = Mesh(mesh.devices.reshape(count, SIDE, SIDE), ("tm", "y", "x"))
    row = ("y", "x")
    in_specs = (
        P("tm", row, None),
        P("tm", row, None),
        P("tm", None, None),
        P("tm", None),
        P("tm", row),
        P("tm", None),
        P("tm", None),
    )
    out_specs = (P("tm", row, None), P("tm", row), P("tm", row, None))
    return jax.shard_map(body, mesh=grid, in_specs=in_specs, out_specs=out_specs, check_vma=False)
```

```python
import math

import jax
import jax.numpy as jnp
from jax import lax
from jax.experimental import pallas as pl
from jax.experimental.pallas import tpu as pltpu
from jax.sharding import Mesh, PartitionSpec as P

NBAND = 5
SIDE = 4

HIGHEST = lax.Precision.HIGHEST
F32 = jnp.float32


def halves(array):
    high = array.astype(jnp.bfloat16)
    return high, (array - high.astype(F32)).astype(jnp.bfloat16)


def three(left, right, contract):
    def one(first, second):
        return lax.dot_general(first, second, (contract, ((), ())), preferred_element_type=F32)

    left_high, left_low = left
    right_high, right_low = right
    return one(left_high, right_high) + (one(left_high, right_low) + one(left_low, right_high))


def dot_t(left, right):
    return three(halves(left), halves(right), ((1,), (1,)))


def exact_dot_t(left, right):
    return lax.dot_general(
        left, right, (((1,), (1,)), ((), ())), precision=HIGHEST, preferred_element_type=F32
    )


def vector_times(row, matrix):
    return exact_dot_t(jnp.broadcast_to(row, (8, row.shape[1])), matrix)[0:1]


def row_times(row, matrix_halves):
    whole = jnp.broadcast_to(row, (8, row.shape[1]))
    return three(halves(whole), matrix_halves, ((1,), (1,)))[0:1]


LANES = 128


def tiles(array):
    return [array[:, i : i + LANES] for i in range(0, array.shape[1], LANES)]


def low_lanes(rows, width):
    return lax.broadcasted_iota(jnp.int32, (rows, LANES), 1) < width


def swap_tiles(blocks):
    width = LANES // 2
    low = low_lanes(blocks[0].shape[0], width)
    rolled = [pltpu.roll(block, width, 1) for block in blocks]
    out = []
    for b in range(SIDE):
        for half in range(SIDE // 2):
            ends = []
            for side in range(2):
                at = (2 * half + side) * SIDE + b
                ends.append((blocks if at % 2 == side else rolled)[at // 2])
            out.append(jnp.where(low, ends[0], ends[1]))
    return out


def swap_lanes(array):
    return jnp.concatenate(swap_tiles(tiles(array)), axis=1)


def band_tiles(blocks, weights, offset_at):
    rows = blocks[0].shape[0]
    width = LANES // 2
    low = low_lanes(rows, width)
    zero = jnp.zeros((rows, LANES), F32)
    turned = [zero] + [pltpu.roll(block, width, 1) for block in blocks] + [zero]
    moved = [jnp.where(low, turned[i], turned[i + 1]) for i in range(len(blocks) + 1)]
    totals = [zero] * len(blocks)
    for b in range(NBAND):
        distance = offset_at(b) + width
        near = low_lanes(rows, LANES - distance)
        back = lax.rem(LANES - distance, LANES)
        rolled = [pltpu.roll(block, back, 1) for block in moved]
        for i in range(len(blocks)):
            weight = weights[b : b + 1, i * LANES : (i + 1) * LANES]
            totals[i] = totals[i] + weight * jnp.where(near, rolled[i], rolled[i + 1])
    return totals


def bands(array, weights, offset_at):
    return jnp.concatenate(band_tiles(tiles(array), weights, offset_at), axis=1)


def wide(ref, rows):
    return jnp.concatenate([ref[i, 0:rows, :] for i in range(SIDE)], axis=1)


STEPS = (0, 1, 3, 2)


def sources(pieces, at):
    return [(piece, lax.rem(at + SIDE - step, SIDE)) for piece, step in zip(pieces, STEPS)]


def place_tall(pieces, at_y, out_ref, row0=0):
    panel = out_ref.shape[0] // SIDE
    chunk = panel // SIDE
    for piece, source in sources(pieces, at_y):
        for b in range(SIDE):
            out_ref[pl.ds(pl.multiple_of(b * panel + source * chunk, chunk), chunk), :] = piece[
                row0 + b * chunk : row0 + (b + 1) * chunk, :
            ]


def prepare(offsets, own, inverse, weights, prior, innovation, sites, crossed_out, y_out):
    rows, columns = own.shape
    matrix = own[...]
    crossed_out[...] = bands(matrix, weights[...], lambda b: offsets[0, b])
    state = lax.broadcasted_iota(jnp.int32, (columns, sites.shape[1]), 0)
    matches = (state == sites[...]).astype(F32)
    pulled = vector_times(innovation[...], matches)
    filtered = prior[...] + vector_times(pulled, matrix)
    for i in range(SIDE):
        y_out[i, 0:rows, :] = inverse[...]
        y_out[i, rows : 2 * rows, :] = matrix
        y_out[i, 2 * rows :, :] = jnp.zeros((8, columns), F32)
        y_out[i, 2 * rows : 2 * rows + 1, 0:rows] = filtered


def place_rows(pieces, at, out):
    rows = pieces[0].shape[0]
    for piece, source in sources(pieces, at):
        out[pl.ds(pl.multiple_of(source * rows, rows), rows), :] = piece[...]


def pick_chunks(ref, at_x):
    panel = ref.shape[0]
    odd = lax.rem(at_x, 2)
    base = lax.div(at_x, 2) * LANES
    low = low_lanes(panel, LANES // 2)
    parts = []
    for i in range(SIDE):
        part = ref[:, pl.ds(pl.multiple_of(i * panel + base, LANES), LANES)]
        turn = odd if i % 2 == 0 else 1 - odd
        parts.append(pltpu.roll(part, turn * (LANES // 2), 1))
    return jnp.where(low, parts[0], parts[1]), jnp.where(low, parts[2], parts[3])


def first_gain(where, y_in, x0, x1, x2, x3, gain_out, block_out, x_out, crossed):
    rows = x0.shape[0]
    panel = SIDE * rows
    place_rows((x0, x1, x2, x3), where[1], crossed)
    inverse = jnp.concatenate([y_in[i, 0:rows, :] for i in range(SIDE)], axis=0)
    gain = dot_t(crossed[...], inverse)
    gain_out[...] = gain
    tail = jnp.concatenate(
        [y_in[i, 2 * rows : 2 * rows + 1, 0:rows] for i in range(SIDE)], axis=1
    )
    tail = jnp.broadcast_to(tail, (8, panel))
    for i in range(SIDE):
        x_out[i, 0:panel, :] = gain
        x_out[i, panel:, :] = tail
    first, second = pick_chunks(crossed, where[1])
    block_out[:, 0:LANES] = first
    block_out[:, LANES:] = second


def second_gain(
    where, offsets, weights, gain, x_in, e0, e1, e2, e3, y_in,
    gain_out, x_out, shift_out, c_out, high_out, low_out, tall,
):
    panel = gain.shape[0]
    at_y = where[0]
    gain_wide = halves(wide(x_in, panel))
    high_out[...] = gain_wide[0]
    low_out[...] = gain_wide[1]
    place_tall((e0, e1, e2, e3), at_y, tall)
    product = three(gain_wide, halves(tall[...]), ((1,), (0,)))
    gain_2 = jnp.where(where[2] == 1, product, gain[...])
    gain_out[...] = gain_2
    for i in range(SIDE):
        x_out[i] = gain_2
    filtered = jnp.concatenate([x_in[i, panel : panel + 8, :] for i in range(SIDE)], axis=1)
    natural = swap_lanes(filtered)
    forward = swap_lanes(bands(natural, weights[...], lambda b: offsets[0, b]))
    mine = jnp.zeros((1, panel), F32)
    for i in range(SIDE):
        mine = mine + jnp.where(at_y == i, natural[0:1, i * panel : (i + 1) * panel], 0.0)
    shift_out[...] = jnp.broadcast_to(mine - row_times(forward[0:1], gain_wide), (8, panel))
    rows = panel // SIDE
    for i in range(SIDE):
        c_out[i * rows : (i + 1) * rows, :] = y_in[i, rows : 2 * rows, :]
    c_out[panel : panel + NBAND, :] = weights[...]
    c_out[panel + NBAND : panel + NBAND + 1, :] = filtered[0:1]
    c_out[panel + NBAND + 1 : panel + NBAND + 2, :] = forward[0:1]
    lane = lax.broadcasted_iota(jnp.int32, (1, c_out.shape[1]), 1)
    held = jnp.zeros((1, c_out.shape[1]), jnp.int32)
    for b in range(NBAND):
        held = jnp.where(lane == b, offsets[0, b], held)
    c_out[panel + NBAND + 2 : panel + NBAND + 3, :] = held.astype(F32)


def later_inputs(offsets, c_in, rows_out, own_high, own_low, crossed_high, crossed_low):
    panel, columns = own_high.shape
    matrix = c_in[0:panel, :]
    weights = c_in[panel : panel + NBAND, :]
    rows_out[...] = c_in[panel:, :]
    high, low = halves(matrix)
    reach = 3 * LANES
    ahead = (
        lax.broadcasted_iota(jnp.int32, (reach, LANES), 0)
        - lax.broadcasted_iota(jnp.int32, (reach, LANES), 1)
        - LANES
    )
    count = columns // LANES
    crossed = []
    for i in range(count):
        first = max(i - 1, 0)
        last = min(i + 2, count)
        spread = jnp.zeros((reach, LANES), F32)
        for b in range(NBAND):
            weight = weights[b : b + 1, i * LANES : (i + 1) * LANES]
            spread = spread + jnp.where(ahead == offsets[b], weight, 0.0)
        spread = spread[(first - i + 1) * LANES : (last - i + 1) * LANES]
        lanes = slice(first * LANES, last * LANES)
        crossed.append(three((high[:, lanes], low[:, lanes]), halves(spread), ((1,), (0,))))
    for blocks, high_out, low_out in (
        (tiles(matrix), own_high, own_low),
        (crossed, crossed_high, crossed_low),
    ):
        for i, block in enumerate(swap_tiles(blocks)):
            high, low = halves(block)
            high_out[:, i * LANES : (i + 1) * LANES] = high
            low_out[:, i * LANES : (i + 1) * LANES] = low


def first_spread(
    where, wide_high, wide_low, gain_2_in, own_high, own_low, crossed_high, crossed_low,
    block, own, e0, e1, e2, e3, gain_2, gain_2_later,
    part_out, pair_out, high_out, low_out, tall,
):
    panel = e0.shape[0]
    at_y = where[0]
    pair_out[0:panel, :] = gain_2[...]
    pair_out[panel:, :] = gain_2_later[...]
    gain_wide = (wide_high[...], wide_low[...])
    gain_2_wide = halves(wide(gain_2_in, panel))
    high_out[...] = gain_2_wide[0]
    low_out[...] = gain_2_wide[1]
    across = ((1,), (1,))
    turned = three(gain_wide, (own_high[...], own_low[...]), across) - three(
        gain_2_wide, (crossed_high[...], crossed_low[...]), across
    )
    inside = where[2] == 1
    turned = halves(jnp.where(inside, turned, 0.0) - block[...])
    place_tall((e0, e1, e2, e3), at_y, tall)
    twice = jnp.concatenate(swap_tiles(tiles(jnp.concatenate([own[...]] * 2, axis=0))), axis=1)
    mine = low_lanes(panel, LANES // 2) == (lax.rem(where[1], 2) == 0)
    at_x = pl.multiple_of(lax.div(where[1], 2) * LANES, LANES)
    for i in range(SIDE):
        part_out[i] = three(halves(tall[i * panel : (i + 1) * panel, :]), turned, across)
        turned_own = twice[:, i * panel : (i + 1) * panel].T
        part_out[i, :, pl.ds(at_x, LANES)] += jnp.where(mine, turned_own, 0.0)


def later_shift(where, high, low, high_2, low_2, later_rows, shift, out):
    moved = row_times(later_rows[NBAND : NBAND + 1, :], (high[...], low[...])) - row_times(
        later_rows[NBAND + 1 : NBAND + 2, :], (high_2[...], low_2[...])
    )
    out[...] = shift[...] + jnp.where(where[2] == 1, moved, 0.0)


def join_spread(parts, shift, out):
    panel = parts.shape[1]
    out[0:panel, :] = ((parts[0] + parts[1]) + (parts[2] + parts[3])).T
    out[panel:, :] = shift[...]


def four_times(block, p1, p2, p3, out):
    for i in range(SIDE):
        out[i] = block[...]


def second_spread(
    where, gain_2, wide_high, wide_low, spread, y_in, a0, a1, a2, a3,
    x_out, shift_out, tall, later_tall,
):
    panel = gain_2.shape[0]
    rows = panel // SIDE
    columns = SIDE * panel
    at_y = where[0]
    inside = where[3] == 1
    gain_2_wide = (wide_high[...], wide_low[...])
    for i in range(SIDE):
        for b in range(SIDE):
            tall[b * panel + i * rows : b * panel + (i + 1) * rows, :] = y_in[
                i, b * rows : (b + 1) * rows, :
            ]
    along = ((1,), (0,))
    turned = halves(jnp.where(inside, three(gain_2_wide, halves(tall[...]), along), 0.0))
    shifts = jnp.concatenate([y_in[i, panel : panel + 8, :] for i in range(SIDE)], axis=1)
    moved = row_times(swap_lanes(shifts)[0:1], gain_2_wide)
    shift_out[...] = spread[panel:, :] + jnp.where(inside, moved, 0.0)
    pieces = (a0, a1, a2, a3)
    place_tall(pieces, at_y, later_tall, panel)
    gain_4 = jnp.where(inside, three(gain_2_wide, halves(later_tall[...]), along), gain_2[...])
    for i in range(SIDE):
        x_out[i, :, columns : columns + panel] = gain_4[i * rows : (i + 1) * rows]
    for piece, source in sources(pieces, at_y):
        tall[pl.ds(pl.multiple_of(source * panel, panel), panel), :] = piece[0:panel, :]
    part = three(turned, halves(tall[...]), ((1,), (1,)))
    for i in range(SIDE):
        x_out[i, :, 0:columns] = part[i * rows : (i + 1) * rows]
    odd = lax.rem(where[1], 2)
    base = lax.div(where[1], 2) * LANES
    mine = low_lanes(panel, LANES // 2) == (odd == 0)
    for c in range(SIDE):
        kept = spread[0:panel, (c // 2) * LANES : (c // 2 + 1) * LANES]
        turn = odd if c % 2 == 0 else 1 - odd
        kept = jnp.where(mine, pltpu.roll(kept, turn * (LANES // 2), 1), 0.0)
        at = pl.multiple_of(c * panel + base, LANES)
        for i in range(SIDE):
            x_out[i, :, pl.ds(at, LANES)] += kept[i * rows : (i + 1) * rows]


def finish(x_in, gain_out, spread_out):
    columns = gain_out.shape[1]
    gain_out[...] = swap_lanes(
        jnp.concatenate([x_in[i, :, columns:] for i in range(SIDE)], axis=1)
    )
    spread_out[...] = (x_in[0, :, 0:columns] + x_in[1, :, 0:columns]) + (
        x_in[2, :, 0:columns] + x_in[3, :, 0:columns]
    )


WHOLE = pl.BlockSpec()
UNREAD = pl.BlockSpec(memory_space=pl.ANY)
SMEM = pl.BlockSpec(memory_space=pltpu.SMEM)


def far(*arrays):
    return [pltpu.with_memory_space_constraint(a, pltpu.HBM) for a in arrays]


def call(kernel, scalars, arrays, outs, scratch=(), flops=0, unread=(), coarse=()):
    shapes = [pltpu.HBM(s, F32) for s in outs] + [pltpu.HBM(s, jnp.bfloat16) for s in coarse]
    size = sum(a.size for a in arrays) + sum(math.prod(s) for s in outs)
    return pl.pallas_call(
        kernel,
        out_shape=shapes,
        in_specs=[SMEM] * len(scalars) + [WHOLE] * len(arrays) + [UNREAD] * len(unread),
        out_specs=[WHOLE] * len(shapes),
        scratch_shapes=[pltpu.VMEM(s, F32) for s in scratch],
        compiler_params=pltpu.CompilerParams(vmem_limit_bytes=24 * 2**20),
        cost_estimate=pl.CostEstimate(flops=flops, bytes_accessed=4 * size, transcendentals=0),
    )(*scalars, *arrays, *unread)


def shifted(block, distance):
    count = lax.axis_size("tm")
    return lax.ppermute(block, "tm", [(i + distance, i) for i in range(count - distance)])


def swap(message, axis):
    return lax.all_to_all(message, axis, 0, 0)


def ring(block, axis):
    pieces = [block]
    for step in STEPS[1:]:
        pieces.append(lax.ppermute(block, axis, [(i, (i + step) % SIDE) for i in range(SIDE)]))
    return pieces


def ring_shifted(block, distance):
    count = lax.axis_size("tm")
    pieces = []
    for step in STEPS:
        route = [
            ((i + distance) * SIDE + j, i * SIDE + (j + step) % SIDE)
            for i in range(count - distance)
            for j in range(SIDE)
        ]
        pieces.append(lax.ppermute(block, ("tm", "y"), route))
    return pieces


def body(covariance, precision, band_weight, band_offset, prior_mean, innovation, seen_sites):
    own = covariance[0]
    inverse = precision[0]
    weights = band_weight[0]
    rows, columns = own.shape
    panel = SIDE * rows
    at_t = lax.axis_index("tm")
    count_t = lax.axis_size("tm")
    at_x = lax.axis_index("x")
    where = jnp.stack(
        [
            lax.axis_index("y").astype(jnp.int32),
            at_x.astype(jnp.int32),
            (at_t + 1 < count_t).astype(jnp.int32),
            (at_t + 2 < count_t).astype(jnp.int32),
        ]
    )
    unit = 2 * panel * panel * columns

    crossed, y_message = call(
        prepare,
        (band_offset,),
        far(own, inverse, weights, prior_mean, innovation, seen_sites),
        ((rows, columns), (SIDE, 2 * rows + 8, columns)),
    )
    y_in = swap(y_message, "y")
    crossed_pieces = ring(crossed, "x")
    gain, crossed_block, x_message = call(
        first_gain,
        (where,),
        (y_in, *far(*crossed_pieces)),
        ((panel, panel), (panel, panel), (SIDE, panel + 8, panel)),
        ((panel, columns),),
        unit,
    )
    gain_in = swap(x_message, "x")
    later_pieces = ring_shifted(gain, 1)
    gain_2, x_message, shift, c_message, wide_high, wide_low = call(
        second_gain,
        (where, band_offset),
        (*far(weights, gain), gain_in, *far(*later_pieces), y_in),
        ((panel, panel), (SIDE, panel, panel), (8, panel), (panel + 8, columns)),
        ((columns, panel),),
        unit,
        coarse=((panel, columns),) * 2,
    )
    gain_2_in = swap(x_message, "x")
    gain_pieces = ring(gain, "y")
    gain_2_later = shifted(gain_2, 2)
    c_in = shifted(c_message, 1)
    next_offsets = c_in[panel + NBAND + 2, 0:8].astype(jnp.int32)
    later_rows, *later_halves = call(
        later_inputs, (next_offsets,), far(c_in), ((8, columns),), coarse=((panel, columns),) * 4
    )
    part, gain_2_pair, wide_2_high, wide_2_low = call(
        first_spread,
        (where,),
        (
            *far(wide_high, wide_low), gain_2_in, *far(*later_halves, crossed_block),
            *far(own, gain, *gain_pieces[1:], gain_2, gain_2_later),
        ),
        ((SIDE, panel, panel), (2 * panel, panel)),
        ((columns, panel),),
        3 * unit,
        coarse=((panel, columns),) * 2,
    )
    (shift_2,) = call(
        later_shift,
        (where,),
        far(wide_high, wide_low, wide_2_high, wide_2_low, later_rows, shift),
        ((8, panel),),
    )
    wide_high, wide_low = wide_2_high, wide_2_low
    parts = swap(part, "x")
    gain_2_pieces = ring(gain_2_pair, "y")
    (spread_2,) = call(join_spread, (), (parts, *far(shift_2)), ((panel + 8, panel),))
    later = shifted(spread_2, 2)
    (y_message,) = call(
        four_times, (), (later,), ((SIDE, panel + 8, panel),), unread=gain_2_pieces[1:]
    )
    y_in = swap(y_message, "y")
    x_message, shift_4 = call(
        second_spread,
        (where,),
        (*far(gain_2, wide_high, wide_low, spread_2), y_in, *far(*gain_2_pieces)),
        ((SIDE, rows, columns + panel), (8, panel)),
        ((columns, panel), (columns, panel)),
        3 * unit,
    )
    last_in = swap(x_message, "x")
    final_gain, final_spread = call(finish, (), (last_in,), ((rows, columns), (rows, columns)))
    final_shift = lax.dynamic_slice_in_dim(shift_4[0], at_x * rows, rows, 0)
    return final_gain[None], final_shift[None], final_spread[None]


def solution(mesh):
    count = mesh.devices.shape[0]
    grid = Mesh(mesh.devices.reshape(count, SIDE, SIDE), ("tm", "y", "x"))
    row = ("y", "x")
    in_specs = (
        P("tm", row, None),
        P("tm", row, None),
        P("tm", None, None),
        P("tm", None),
        P("tm", row),
        P("tm", None),
        P("tm", None),
    )
    out_specs = (P("tm", row, None), P("tm", row), P("tm", row, None))
    return jax.shard_map(body, mesh=grid, in_specs=in_specs, out_specs=out_specs, check_vma=False)
```

```python
import math

import jax
import jax.numpy as jnp
from jax import lax
from jax.experimental import pallas as pl
from jax.experimental.pallas import tpu as pltpu
from jax.sharding import Mesh, PartitionSpec as P

NBAND = 5
SIDE = 4

HIGHEST = lax.Precision.HIGHEST
F32 = jnp.float32


def halves(array):
    high = array.astype(jnp.bfloat16)
    return high, (array - high.astype(F32)).astype(jnp.bfloat16)


def three(left, right, contract):
    def one(first, second):
        return lax.dot_general(first, second, (contract, ((), ())), preferred_element_type=F32)

    left_high, left_low = left
    right_high, right_low = right
    return one(left_high, right_high) + (one(left_high, right_low) + one(left_low, right_high))


def dot_t(left, right):
    return three(halves(left), halves(right), ((1,), (1,)))


def exact_dot_t(left, right):
    return lax.dot_general(
        left, right, (((1,), (1,)), ((), ())), precision=HIGHEST, preferred_element_type=F32
    )


def vector_times(row, matrix):
    return exact_dot_t(jnp.broadcast_to(row, (8, row.shape[1])), matrix)[0:1]


def row_times(row, matrix_halves):
    whole = jnp.broadcast_to(row, (8, row.shape[1]))
    return three(halves(whole), matrix_halves, ((1,), (1,)))[0:1]


LANES = 128


def tiles(array):
    return [array[:, i : i + LANES] for i in range(0, array.shape[1], LANES)]


def low_lanes(rows, width):
    return lax.broadcasted_iota(jnp.int32, (rows, LANES), 1) < width


def swap_tiles(blocks):
    width = LANES // 2
    low = low_lanes(blocks[0].shape[0], width)
    rolled = [pltpu.roll(block, width, 1) for block in blocks]
    out = []
    for b in range(SIDE):
        for half in range(SIDE // 2):
            ends = []
            for side in range(2):
                at = (2 * half + side) * SIDE + b
                ends.append((blocks if at % 2 == side else rolled)[at // 2])
            out.append(jnp.where(low, ends[0], ends[1]))
    return out


def swap_lanes(array):
    return jnp.concatenate(swap_tiles(tiles(array)), axis=1)


def band_tiles(blocks, weights, offset_at):
    rows = blocks[0].shape[0]
    width = LANES // 2
    low = low_lanes(rows, width)
    zero = jnp.zeros((rows, LANES), F32)
    turned = [zero] + [pltpu.roll(block, width, 1) for block in blocks] + [zero]
    moved = [jnp.where(low, turned[i], turned[i + 1]) for i in range(len(blocks) + 1)]
    totals = [zero] * len(blocks)
    for b in range(NBAND):
        distance = offset_at(b) + width
        near = low_lanes(rows, LANES - distance)
        back = lax.rem(LANES - distance, LANES)
        rolled = [pltpu.roll(block, back, 1) for block in moved]
        for i in range(len(blocks)):
            weight = weights[b : b + 1, i * LANES : (i + 1) * LANES]
            totals[i] = totals[i] + weight * jnp.where(near, rolled[i], rolled[i + 1])
    return totals


def bands(array, weights, offset_at):
    return jnp.concatenate(band_tiles(tiles(array), weights, offset_at), axis=1)


def wide(ref, rows):
    return jnp.concatenate([ref[i, 0:rows, :] for i in range(SIDE)], axis=1)


STEPS = (0, 1, 3, 2)


def sources(pieces, at):
    return [(piece, lax.rem(at + SIDE - step, SIDE)) for piece, step in zip(pieces, STEPS)]


def place_tall(pieces, at_y, out_ref, row0=0):
    panel = out_ref.shape[0] // SIDE
    chunk = panel // SIDE
    for piece, source in sources(pieces, at_y):
        for b in range(SIDE):
            out_ref[pl.ds(pl.multiple_of(b * panel + source * chunk, chunk), chunk), :] = piece[
                row0 + b * chunk : row0 + (b + 1) * chunk, :
            ]


def first_message(own, inverse, prior, innovation, sites, y_out):
    rows, columns = own.shape
    matrix = own[...]
    state = lax.broadcasted_iota(jnp.int32, (columns, sites.shape[1]), 0)
    matches = (state == sites[...]).astype(F32)
    pulled = vector_times(innovation[...], matches)
    filtered = prior[...] + vector_times(pulled, matrix)
    for i in range(SIDE):
        y_out[i, 0:rows, :] = inverse[...]
        y_out[i, rows : 2 * rows, :] = matrix
        y_out[i, 2 * rows :, :] = jnp.zeros((8, columns), F32)
        y_out[i, 2 * rows : 2 * rows + 1, 0:rows] = filtered


def cross(offsets, own, weights, crossed_out):
    crossed_out[...] = bands(own[...], weights[...], lambda b: offsets[0, b])


def place_rows(pieces, at, out):
    rows = pieces[0].shape[0]
    for piece, source in sources(pieces, at):
        out[pl.ds(pl.multiple_of(source * rows, rows), rows), :] = piece[...]


def pick_chunks(ref, at_x):
    panel = ref.shape[0]
    odd = lax.rem(at_x, 2)
    base = lax.div(at_x, 2) * LANES
    low = low_lanes(panel, LANES // 2)
    parts = []
    for i in range(SIDE):
        part = ref[:, pl.ds(pl.multiple_of(i * panel + base, LANES), LANES)]
        turn = odd if i % 2 == 0 else 1 - odd
        parts.append(pltpu.roll(part, turn * (LANES // 2), 1))
    return jnp.where(low, parts[0], parts[1]), jnp.where(low, parts[2], parts[3])


def first_gain(where, y_in, x0, x1, x2, x3, gain_out, block_out, x_out, crossed):
    rows = x0.shape[0]
    panel = SIDE * rows
    place_rows((x0, x1, x2, x3), where[1], crossed)
    inverse = jnp.concatenate([y_in[i, 0:rows, :] for i in range(SIDE)], axis=0)
    gain = dot_t(crossed[...], inverse)
    gain_out[...] = gain
    tail = jnp.concatenate(
        [y_in[i, 2 * rows : 2 * rows + 1, 0:rows] for i in range(SIDE)], axis=1
    )
    tail = jnp.broadcast_to(tail, (8, panel))
    for i in range(SIDE):
        x_out[i, 0:panel, :] = gain
        x_out[i, panel:, :] = tail
    first, second = pick_chunks(crossed, where[1])
    block_out[:, 0:LANES] = first
    block_out[:, LANES:] = second


def second_gain(
    where, offsets, weights, gain, x_in, e0, e1, e2, e3, y_in,
    gain_out, x_out, shift_out, c_out, high_out, low_out, tall,
):
    panel = gain.shape[0]
    at_y = where[0]
    gain_wide = halves(wide(x_in, panel))
    high_out[...] = gain_wide[0]
    low_out[...] = gain_wide[1]
    place_tall((e0, e1, e2, e3), at_y, tall)
    product = three(gain_wide, halves(tall[...]), ((1,), (0,)))
    gain_2 = jnp.where(where[2] == 1, product, gain[...])
    gain_out[...] = gain_2
    for i in range(SIDE):
        x_out[i] = gain_2
    filtered = jnp.concatenate([x_in[i, panel : panel + 8, :] for i in range(SIDE)], axis=1)
    natural = swap_lanes(filtered)
    forward = swap_lanes(bands(natural, weights[...], lambda b: offsets[0, b]))
    mine = jnp.zeros((1, panel), F32)
    for i in range(SIDE):
        mine = mine + jnp.where(at_y == i, natural[0:1, i * panel : (i + 1) * panel], 0.0)
    shift_out[...] = jnp.broadcast_to(mine - row_times(forward[0:1], gain_wide), (8, panel))
    rows = panel // SIDE
    for i in range(SIDE):
        c_out[i * rows : (i + 1) * rows, :] = y_in[i, rows : 2 * rows, :]
    c_out[panel : panel + NBAND, :] = weights[...]
    c_out[panel + NBAND : panel + NBAND + 1, :] = filtered[0:1]
    c_out[panel + NBAND + 1 : panel + NBAND + 2, :] = forward[0:1]
    lane = lax.broadcasted_iota(jnp.int32, (1, c_out.shape[1]), 1)
    held = jnp.zeros((1, c_out.shape[1]), jnp.int32)
    for b in range(NBAND):
        held = jnp.where(lane == b, offsets[0, b], held)
    c_out[panel + NBAND + 2 : panel + NBAND + 3, :] = held.astype(F32)


def later_inputs(offsets, c_in, rows_out, own_high, own_low, crossed_high, crossed_low):
    panel, columns = own_high.shape
    matrix = c_in[0:panel, :]
    weights = c_in[panel : panel + NBAND, :]
    rows_out[...] = c_in[panel:, :]
    high, low = halves(matrix)
    reach = 3 * LANES
    ahead = (
        lax.broadcasted_iota(jnp.int32, (reach, LANES), 0)
        - lax.broadcasted_iota(jnp.int32, (reach, LANES), 1)
        - LANES
    )
    count = columns // LANES
    crossed = []
    for i in range(count):
        first = max(i - 1, 0)
        last = min(i + 2, count)
        spread = jnp.zeros((reach, LANES), F32)
        for b in range(NBAND):
            weight = weights[b : b + 1, i * LANES : (i + 1) * LANES]
            spread = spread + jnp.where(ahead == offsets[b], weight, 0.0)
        spread = spread[(first - i + 1) * LANES : (last - i + 1) * LANES]
        lanes = slice(first * LANES, last * LANES)
        crossed.append(three((high[:, lanes], low[:, lanes]), halves(spread), ((1,), (0,))))
    for blocks, high_out, low_out in (
        (tiles(matrix), own_high, own_low),
        (crossed, crossed_high, crossed_low),
    ):
        for i, block in enumerate(swap_tiles(blocks)):
            high, low = halves(block)
            high_out[:, i * LANES : (i + 1) * LANES] = high
            low_out[:, i * LANES : (i + 1) * LANES] = low


def first_spread(
    where, wide_high, wide_low, gain_2_in, own_high, own_low, crossed_high, crossed_low,
    block, own, e0, e1, e2, e3, gain_2, gain_2_later,
    part_out, pair_out, high_out, low_out, tall,
):
    panel = e0.shape[0]
    at_y = where[0]
    pair_out[0:panel, :] = gain_2[...]
    pair_out[panel:, :] = gain_2_later[...]
    gain_wide = (wide_high[...], wide_low[...])
    gain_2_wide = halves(wide(gain_2_in, panel))
    high_out[...] = gain_2_wide[0]
    low_out[...] = gain_2_wide[1]
    across = ((1,), (1,))
    turned = three(gain_wide, (own_high[...], own_low[...]), across) - three(
        gain_2_wide, (crossed_high[...], crossed_low[...]), across
    )
    inside = where[2] == 1
    turned = halves(jnp.where(inside, turned, 0.0) - block[...])
    place_tall((e0, e1, e2, e3), at_y, tall)
    twice = jnp.concatenate(swap_tiles(tiles(jnp.concatenate([own[...]] * 2, axis=0))), axis=1)
    mine = low_lanes(panel, LANES // 2) == (lax.rem(where[1], 2) == 0)
    at_x = pl.multiple_of(lax.div(where[1], 2) * LANES, LANES)
    for i in range(SIDE):
        part_out[i] = three(halves(tall[i * panel : (i + 1) * panel, :]), turned, across)
        turned_own = twice[:, i * panel : (i + 1) * panel].T
        part_out[i, :, pl.ds(at_x, LANES)] += jnp.where(mine, turned_own, 0.0)


def later_shift(where, high, low, high_2, low_2, later_rows, shift, out):
    moved = row_times(later_rows[NBAND : NBAND + 1, :], (high[...], low[...])) - row_times(
        later_rows[NBAND + 1 : NBAND + 2, :], (high_2[...], low_2[...])
    )
    out[...] = shift[...] + jnp.where(where[2] == 1, moved, 0.0)


def join_spread(parts, shift, out):
    panel = parts.shape[1]
    out[0:panel, :] = ((parts[0] + parts[1]) + (parts[2] + parts[3])).T
    out[panel:, :] = shift[...]


def four_times(block, p1, p2, p3, out):
    for i in range(SIDE):
        out[i] = block[...]


def second_spread(
    where, gain_2, wide_high, wide_low, spread, y_in, a0, a1, a2, a3,
    x_out, shift_out, tall, later_tall,
):
    panel = gain_2.shape[0]
    rows = panel // SIDE
    columns = SIDE * panel
    at_y = where[0]
    inside = where[3] == 1
    gain_2_wide = (wide_high[...], wide_low[...])
    for i in range(SIDE):
        for b in range(SIDE):
            tall[b * panel + i * rows : b * panel + (i + 1) * rows, :] = y_in[
                i, b * rows : (b + 1) * rows, :
            ]
    along = ((1,), (0,))
    turned = halves(jnp.where(inside, three(gain_2_wide, halves(tall[...]), along), 0.0))
    shifts = jnp.concatenate([y_in[i, panel : panel + 8, :] for i in range(SIDE)], axis=1)
    moved = row_times(swap_lanes(shifts)[0:1], gain_2_wide)
    shift_out[...] = spread[panel:, :] + jnp.where(inside, moved, 0.0)
    pieces = (a0, a1, a2, a3)
    place_tall(pieces, at_y, later_tall, panel)
    gain_4 = jnp.where(inside, three(gain_2_wide, halves(later_tall[...]), along), gain_2[...])
    for i in range(SIDE):
        x_out[i, :, columns : columns + panel] = gain_4[i * rows : (i + 1) * rows]
    for piece, source in sources(pieces, at_y):
        tall[pl.ds(pl.multiple_of(source * panel, panel), panel), :] = piece[0:panel, :]
    part = three(turned, halves(tall[...]), ((1,), (1,)))
    for i in range(SIDE):
        x_out[i, :, 0:columns] = part[i * rows : (i + 1) * rows]
    odd = lax.rem(where[1], 2)
    base = lax.div(where[1], 2) * LANES
    mine = low_lanes(panel, LANES // 2) == (odd == 0)
    for c in range(SIDE):
        kept = spread[0:panel, (c // 2) * LANES : (c // 2 + 1) * LANES]
        turn = odd if c % 2 == 0 else 1 - odd
        kept = jnp.where(mine, pltpu.roll(kept, turn * (LANES // 2), 1), 0.0)
        at = pl.multiple_of(c * panel + base, LANES)
        for i in range(SIDE):
            x_out[i, :, pl.ds(at, LANES)] += kept[i * rows : (i + 1) * rows]


def finish(x_in, gain_out, spread_out):
    columns = gain_out.shape[1]
    gain_out[...] = swap_lanes(
        jnp.concatenate([x_in[i, :, columns:] for i in range(SIDE)], axis=1)
    )
    spread_out[...] = (x_in[0, :, 0:columns] + x_in[1, :, 0:columns]) + (
        x_in[2, :, 0:columns] + x_in[3, :, 0:columns]
    )


WHOLE = pl.BlockSpec()
UNREAD = pl.BlockSpec(memory_space=pl.ANY)
SMEM = pl.BlockSpec(memory_space=pltpu.SMEM)


def far(*arrays):
    return [pltpu.with_memory_space_constraint(a, pltpu.HBM) for a in arrays]


def call(kernel, scalars, arrays, outs, scratch=(), flops=0, unread=(), coarse=()):
    shapes = [pltpu.HBM(s, F32) for s in outs] + [pltpu.HBM(s, jnp.bfloat16) for s in coarse]
    size = sum(a.size for a in arrays) + sum(math.prod(s) for s in outs)
    return pl.pallas_call(
        kernel,
        out_shape=shapes,
        in_specs=[SMEM] * len(scalars) + [WHOLE] * len(arrays) + [UNREAD] * len(unread),
        out_specs=[WHOLE] * len(shapes),
        scratch_shapes=[pltpu.VMEM(s, F32) for s in scratch],
        compiler_params=pltpu.CompilerParams(vmem_limit_bytes=24 * 2**20),
        cost_estimate=pl.CostEstimate(flops=flops, bytes_accessed=4 * size, transcendentals=0),
    )(*scalars, *arrays, *unread)


def shifted(block, distance):
    count = lax.axis_size("tm")
    return lax.ppermute(block, "tm", [(i + distance, i) for i in range(count - distance)])


def swap(message, axis):
    return lax.all_to_all(message, axis, 0, 0)


def ring(block, axis):
    pieces = [block]
    for step in STEPS[1:]:
        pieces.append(lax.ppermute(block, axis, [(i, (i + step) % SIDE) for i in range(SIDE)]))
    return pieces


def ring_shifted(block, distance):
    count = lax.axis_size("tm")
    pieces = []
    for step in STEPS:
        route = [
            ((i + distance) * SIDE + j, i * SIDE + (j + step) % SIDE)
            for i in range(count - distance)
            for j in range(SIDE)
        ]
        pieces.append(lax.ppermute(block, ("tm", "y"), route))
    return pieces


def body(covariance, precision, band_weight, band_offset, prior_mean, innovation, seen_sites):
    own = covariance[0]
    inverse = precision[0]
    weights = band_weight[0]
    rows, columns = own.shape
    panel = SIDE * rows
    at_t = lax.axis_index("tm")
    count_t = lax.axis_size("tm")
    at_x = lax.axis_index("x")
    where = jnp.stack(
        [
            lax.axis_index("y").astype(jnp.int32),
            at_x.astype(jnp.int32),
            (at_t + 1 < count_t).astype(jnp.int32),
            (at_t + 2 < count_t).astype(jnp.int32),
        ]
    )
    unit = 2 * panel * panel * columns

    (y_message,) = call(
        first_message,
        (),
        far(own, inverse, prior_mean, innovation, seen_sites),
        ((SIDE, 2 * rows + 8, columns),),
    )
    y_in = swap(y_message, "y")
    (crossed,) = call(cross, (band_offset,), far(own, weights), ((rows, columns),))
    crossed_pieces = ring(crossed, "x")
    gain, crossed_block, x_message = call(
        first_gain,
        (where,),
        (y_in, *far(*crossed_pieces)),
        ((panel, panel), (panel, panel), (SIDE, panel + 8, panel)),
        ((panel, columns),),
        unit,
    )
    gain_in = swap(x_message, "x")
    later_pieces = ring_shifted(gain, 1)
    gain_2, x_message, shift, c_message, wide_high, wide_low = call(
        second_gain,
        (where, band_offset),
        (*far(weights, gain), gain_in, *far(*later_pieces), y_in),
        ((panel, panel), (SIDE, panel, panel), (8, panel), (panel + 8, columns)),
        ((columns, panel),),
        unit,
        coarse=((panel, columns),) * 2,
    )
    gain_2_in = swap(x_message, "x")
    gain_pieces = ring(gain, "y")
    gain_2_later = shifted(gain_2, 2)
    c_in = shifted(c_message, 1)
    next_offsets = c_in[panel + NBAND + 2, 0:8].astype(jnp.int32)
    later_rows, *later_halves = call(
        later_inputs, (next_offsets,), far(c_in), ((8, columns),), coarse=((panel, columns),) * 4
    )
    part, gain_2_pair, wide_2_high, wide_2_low = call(
        first_spread,
        (where,),
        (
            *far(wide_high, wide_low), gain_2_in, *far(*later_halves, crossed_block),
            *far(own, gain, *gain_pieces[1:], gain_2, gain_2_later),
        ),
        ((SIDE, panel, panel), (2 * panel, panel)),
        ((columns, panel),),
        3 * unit,
        coarse=((panel, columns),) * 2,
    )
    (shift_2,) = call(
        later_shift,
        (where,),
        far(wide_high, wide_low, wide_2_high, wide_2_low, later_rows, shift),
        ((8, panel),),
    )
    wide_high, wide_low = wide_2_high, wide_2_low
    parts = swap(part, "x")
    gain_2_pieces = ring(gain_2_pair, "y")
    (spread_2,) = call(join_spread, (), (parts, *far(shift_2)), ((panel + 8, panel),))
    later = shifted(spread_2, 2)
    (y_message,) = call(
        four_times, (), (later,), ((SIDE, panel + 8, panel),), unread=gain_2_pieces[1:]
    )
    y_in = swap(y_message, "y")
    x_message, shift_4 = call(
        second_spread,
        (where,),
        (*far(gain_2, wide_high, wide_low, spread_2), y_in, *far(*gain_2_pieces)),
        ((SIDE, rows, columns + panel), (8, panel)),
        ((columns, panel), (columns, panel)),
        3 * unit,
    )
    last_in = swap(x_message, "x")
    final_gain, final_spread = call(finish, (), (last_in,), ((rows, columns), (rows, columns)))
    final_shift = lax.dynamic_slice_in_dim(shift_4[0], at_x * rows, rows, 0)
    return final_gain[None], final_shift[None], final_spread[None]


def solution(mesh):
    count = mesh.devices.shape[0]
    grid = Mesh(mesh.devices.reshape(count, SIDE, SIDE), ("tm", "y", "x"))
    row = ("y", "x")
    in_specs = (
        P("tm", row, None),
        P("tm", row, None),
        P("tm", None, None),
        P("tm", None),
        P("tm", row),
        P("tm", None),
        P("tm", None),
    )
    out_specs = (P("tm", row, None), P("tm", row), P("tm", row, None))
    return jax.shard_map(body, mesh=grid, in_specs=in_specs, out_specs=out_specs, check_vma=False)
```

```python
import math

import jax
import jax.numpy as jnp
from jax import lax
from jax.experimental import pallas as pl
from jax.experimental.pallas import tpu as pltpu
from jax.sharding import Mesh, PartitionSpec as P

NBAND = 5
SIDE = 4

HIGHEST = lax.Precision.HIGHEST
F32 = jnp.float32


def halves(array):
    high = array.astype(jnp.bfloat16)
    return high, (array - high.astype(F32)).astype(jnp.bfloat16)


def three(left, right, contract):
    def one(first, second):
        return lax.dot_general(first, second, (contract, ((), ())), preferred_element_type=F32)

    left_high, left_low = left
    right_high, right_low = right
    return one(left_high, right_high) + (one(left_high, right_low) + one(left_low, right_high))


def dot_t(left, right):
    return three(halves(left), halves(right), ((1,), (1,)))


def exact_dot_t(left, right):
    return lax.dot_general(
        left, right, (((1,), (1,)), ((), ())), precision=HIGHEST, preferred_element_type=F32
    )


def vector_times(row, matrix):
    return exact_dot_t(jnp.broadcast_to(row, (8, row.shape[1])), matrix)[0:1]


def row_times(row, matrix_halves):
    whole = jnp.broadcast_to(row, (8, row.shape[1]))
    return three(halves(whole), matrix_halves, ((1,), (1,)))[0:1]


LANES = 128


def tiles(array):
    return [array[:, i : i + LANES] for i in range(0, array.shape[1], LANES)]


def low_lanes(rows, width):
    return lax.broadcasted_iota(jnp.int32, (rows, LANES), 1) < width


def swap_tiles(blocks):
    width = LANES // 2
    low = low_lanes(blocks[0].shape[0], width)
    rolled = [pltpu.roll(block, width, 1) for block in blocks]
    out = []
    for b in range(SIDE):
        for half in range(SIDE // 2):
            ends = []
            for side in range(2):
                at = (2 * half + side) * SIDE + b
                ends.append((blocks if at % 2 == side else rolled)[at // 2])
            out.append(jnp.where(low, ends[0], ends[1]))
    return out


def swap_lanes(array):
    return jnp.concatenate(swap_tiles(tiles(array)), axis=1)


def band_tiles(blocks, weights, offset_at):
    rows = blocks[0].shape[0]
    width = LANES // 2
    low = low_lanes(rows, width)
    zero = jnp.zeros((rows, LANES), F32)
    turned = [zero] + [pltpu.roll(block, width, 1) for block in blocks] + [zero]
    moved = [jnp.where(low, turned[i], turned[i + 1]) for i in range(len(blocks) + 1)]
    totals = [zero] * len(blocks)
    for b in range(NBAND):
        distance = offset_at(b) + width
        near = low_lanes(rows, LANES - distance)
        back = lax.rem(LANES - distance, LANES)
        rolled = [pltpu.roll(block, back, 1) for block in moved]
        for i in range(len(blocks)):
            weight = weights[b : b + 1, i * LANES : (i + 1) * LANES]
            totals[i] = totals[i] + weight * jnp.where(near, rolled[i], rolled[i + 1])
    return totals


def bands(array, weights, offset_at):
    return jnp.concatenate(band_tiles(tiles(array), weights, offset_at), axis=1)


def wide(ref, rows):
    return jnp.concatenate([ref[i, 0:rows, :] for i in range(SIDE)], axis=1)


STEPS = (0, 1, 3, 2)


def sources(pieces, at):
    return [(piece, lax.rem(at + SIDE - step, SIDE)) for piece, step in zip(pieces, STEPS)]


def place_tall(pieces, at_y, out_ref, row0=0):
    panel = out_ref.shape[0] // SIDE
    chunk = panel // SIDE
    for piece, source in sources(pieces, at_y):
        for b in range(SIDE):
            out_ref[pl.ds(pl.multiple_of(b * panel + source * chunk, chunk), chunk), :] = piece[
                row0 + b * chunk : row0 + (b + 1) * chunk, :
            ]


def first_message(own, inverse, prior, innovation, sites, y_out):
    rows, columns = own.shape
    matrix = own[...]
    state = lax.broadcasted_iota(jnp.int32, (columns, sites.shape[1]), 0)
    matches = (state == sites[...]).astype(F32)
    pulled = vector_times(innovation[...], matches)
    filtered = prior[...] + vector_times(pulled, matrix)
    for i in range(SIDE):
        y_out[i, 0:rows, :] = inverse[...]
        y_out[i, rows : 2 * rows, :] = matrix
        y_out[i, 2 * rows :, :] = jnp.zeros((8, columns), F32)
        y_out[i, 2 * rows : 2 * rows + 1, 0:rows] = filtered


def cross(offsets, own, weights, crossed_out):
    crossed_out[...] = bands(own[...], weights[...], lambda b: offsets[0, b])


def place_rows(pieces, at, out):
    rows = pieces[0].shape[0]
    for piece, source in sources(pieces, at):
        out[pl.ds(pl.multiple_of(source * rows, rows), rows), :] = piece[...]


def pick_chunks(ref, at_x):
    panel = ref.shape[0]
    odd = lax.rem(at_x, 2)
    base = lax.div(at_x, 2) * LANES
    low = low_lanes(panel, LANES // 2)
    parts = []
    for i in range(SIDE):
        part = ref[:, pl.ds(pl.multiple_of(i * panel + base, LANES), LANES)]
        turn = odd if i % 2 == 0 else 1 - odd
        parts.append(pltpu.roll(part, turn * (LANES // 2), 1))
    return jnp.where(low, parts[0], parts[1]), jnp.where(low, parts[2], parts[3])


def first_gain(where, y_in, x0, x1, x2, x3, gain_out, block_out, x_out, crossed):
    rows = x0.shape[0]
    panel = SIDE * rows
    place_rows((x0, x1, x2, x3), where[1], crossed)
    inverse = jnp.concatenate([y_in[i, 0:rows, :] for i in range(SIDE)], axis=0)
    gain = dot_t(crossed[...], inverse)
    gain_out[...] = gain
    tail = jnp.concatenate(
        [y_in[i, 2 * rows : 2 * rows + 1, 0:rows] for i in range(SIDE)], axis=1
    )
    tail = jnp.broadcast_to(tail, (8, panel))
    for i in range(SIDE):
        x_out[i, 0:panel, :] = gain
        x_out[i, panel:, :] = tail
    first, second = pick_chunks(crossed, where[1])
    block_out[:, 0:LANES] = first
    block_out[:, LANES:] = second


def second_gain(
    where, offsets, weights, gain, x_in, e0, e1, e2, e3, y_in,
    gain_out, x_out, shift_out, c_out, high_out, low_out, tall,
):
    panel = gain.shape[0]
    at_y = where[0]
    gain_wide = halves(wide(x_in, panel))
    high_out[...] = gain_wide[0]
    low_out[...] = gain_wide[1]
    place_tall((e0, e1, e2, e3), at_y, tall)
    product = three(gain_wide, halves(tall[...]), ((1,), (0,)))
    gain_2 = jnp.where(where[2] == 1, product, gain[...])
    gain_out[...] = gain_2
    for i in range(SIDE):
        x_out[i] = gain_2
    filtered = jnp.concatenate([x_in[i, panel : panel + 8, :] for i in range(SIDE)], axis=1)
    natural = swap_lanes(filtered)
    forward = swap_lanes(bands(natural, weights[...], lambda b: offsets[0, b]))
    mine = jnp.zeros((1, panel), F32)
    for i in range(SIDE):
        mine = mine + jnp.where(at_y == i, natural[0:1, i * panel : (i + 1) * panel], 0.0)
    shift_out[...] = jnp.broadcast_to(mine - row_times(forward[0:1], gain_wide), (8, panel))
    rows = panel // SIDE
    for i in range(SIDE):
        c_out[i * rows : (i + 1) * rows, :] = y_in[i, rows : 2 * rows, :]
    c_out[panel : panel + NBAND, :] = weights[...]
    c_out[panel + NBAND : panel + NBAND + 1, :] = filtered[0:1]
    c_out[panel + NBAND + 1 : panel + NBAND + 2, :] = forward[0:1]
    lane = lax.broadcasted_iota(jnp.int32, (1, c_out.shape[1]), 1)
    held = jnp.zeros((1, c_out.shape[1]), jnp.int32)
    for b in range(NBAND):
        held = jnp.where(lane == b, offsets[0, b], held)
    c_out[panel + NBAND + 2 : panel + NBAND + 3, :] = held.astype(F32)


def later_inputs(offsets, c_in, rows_out, own_high, own_low, crossed_high, crossed_low):
    panel, columns = own_high.shape
    matrix = c_in[0:panel, :]
    weights = c_in[panel : panel + NBAND, :]
    rows_out[...] = c_in[panel:, :]
    high, low = halves(matrix)
    reach = 3 * LANES
    ahead = (
        lax.broadcasted_iota(jnp.int32, (reach, LANES), 0)
        - lax.broadcasted_iota(jnp.int32, (reach, LANES), 1)
        - LANES
    )
    count = columns // LANES
    crossed = []
    for i in range(count):
        first = max(i - 1, 0)
        last = min(i + 2, count)
        spread = jnp.zeros((reach, LANES), F32)
        for b in range(NBAND):
            weight = weights[b : b + 1, i * LANES : (i + 1) * LANES]
            spread = spread + jnp.where(ahead == offsets[b], weight, 0.0)
        spread = spread[(first - i + 1) * LANES : (last - i + 1) * LANES]
        lanes = slice(first * LANES, last * LANES)
        crossed.append(three((high[:, lanes], low[:, lanes]), halves(spread), ((1,), (0,))))
    for blocks, high_out, low_out in (
        (tiles(matrix), own_high, own_low),
        (crossed, crossed_high, crossed_low),
    ):
        for i, block in enumerate(swap_tiles(blocks)):
            high, low = halves(block)
            high_out[:, i * LANES : (i + 1) * LANES] = high
            low_out[:, i * LANES : (i + 1) * LANES] = low


def first_spread(
    where, wide_high, wide_low, gain_2_in, own_high, own_low, crossed_high, crossed_low,
    block, own, e0, e1, e2, e3, gain_2, gain_2_later,
    part_out, pair_out, high_out, low_out, tall,
):
    panel = e0.shape[0]
    at_y = where[0]
    pair_out[0:panel, :] = gain_2[...]
    pair_out[panel:, :] = gain_2_later[...]
    gain_wide = (wide_high[...], wide_low[...])
    gain_2_wide = halves(wide(gain_2_in, panel))
    high_out[...] = gain_2_wide[0]
    low_out[...] = gain_2_wide[1]
    across = ((1,), (1,))
    turned = three(gain_wide, (own_high[...], own_low[...]), across) - three(
        gain_2_wide, (crossed_high[...], crossed_low[...]), across
    )
    inside = where[2] == 1
    turned = halves(jnp.where(inside, turned, 0.0) - block[...])
    place_tall((e0, e1, e2, e3), at_y, tall)
    twice = jnp.concatenate(swap_tiles(tiles(jnp.concatenate([own[...]] * 2, axis=0))), axis=1)
    mine = low_lanes(panel, LANES // 2) == (lax.rem(where[1], 2) == 0)
    at_x = pl.multiple_of(lax.div(where[1], 2) * LANES, LANES)
    for i in range(SIDE):
        part_out[i] = three(halves(tall[i * panel : (i + 1) * panel, :]), turned, across)
        turned_own = twice[:, i * panel : (i + 1) * panel].T
        part_out[i, :, pl.ds(at_x, LANES)] += jnp.where(mine, turned_own, 0.0)


def later_shift(where, high, low, high_2, low_2, later_rows, shift, out):
    moved = row_times(later_rows[NBAND : NBAND + 1, :], (high[...], low[...])) - row_times(
        later_rows[NBAND + 1 : NBAND + 2, :], (high_2[...], low_2[...])
    )
    out[...] = shift[...] + jnp.where(where[2] == 1, moved, 0.0)


def join_spread(parts, shift, out):
    panel = parts.shape[1]
    out[0:panel, :] = ((parts[0] + parts[1]) + (parts[2] + parts[3])).T
    out[panel:, :] = shift[...]


def four_times(block, p1, p2, p3, out):
    for i in range(SIDE):
        out[i] = block[...]


def third_gain(where, gain_2, wide_high, wide_low, a0, a1, a2, a3, gain_out, high_out, low_out, tall):
    panel = gain_2.shape[0]
    at_y = where[0]
    pieces = (a0, a1, a2, a3)
    place_tall(pieces, at_y, tall, panel)
    product = three((wide_high[...], wide_low[...]), halves(tall[...]), ((1,), (0,)))
    gain_out[...] = jnp.where(where[3] == 1, product, gain_2[...])
    for piece, source in sources(pieces, at_y):
        at = pl.ds(pl.multiple_of(source * panel, panel), panel)
        high_out[at, :], low_out[at, :] = halves(piece[0:panel, :])


def second_spread(
    where, gain_4, wide_high, wide_low, tall_high, tall_low, spread, y_in, x_out, shift_out, tall
):
    panel = gain_4.shape[0]
    rows = panel // SIDE
    columns = SIDE * panel
    inside = where[3] == 1
    gain_2_wide = (wide_high[...], wide_low[...])
    for i in range(SIDE):
        for b in range(SIDE):
            tall[b * panel + i * rows : b * panel + (i + 1) * rows, :] = y_in[
                i, b * rows : (b + 1) * rows, :
            ]
    turned = three(gain_2_wide, halves(tall[...]), ((1,), (0,)))
    turned = halves(jnp.where(inside, turned, 0.0))
    shifts = jnp.concatenate([y_in[i, panel : panel + 8, :] for i in range(SIDE)], axis=1)
    moved = row_times(swap_lanes(shifts)[0:1], gain_2_wide)
    shift_out[...] = spread[panel:, :] + jnp.where(inside, moved, 0.0)
    for i in range(SIDE):
        x_out[i, :, columns : columns + panel] = gain_4[i * rows : (i + 1) * rows, :]
    part = three(turned, (tall_high[...], tall_low[...]), ((1,), (1,)))
    for i in range(SIDE):
        x_out[i, :, 0:columns] = part[i * rows : (i + 1) * rows]
    odd = lax.rem(where[1], 2)
    base = lax.div(where[1], 2) * LANES
    mine = low_lanes(panel, LANES // 2) == (odd == 0)
    for c in range(SIDE):
        kept = spread[0:panel, (c // 2) * LANES : (c // 2 + 1) * LANES]
        turn = odd if c % 2 == 0 else 1 - odd
        kept = jnp.where(mine, pltpu.roll(kept, turn * (LANES // 2), 1), 0.0)
        at = pl.multiple_of(c * panel + base, LANES)
        for i in range(SIDE):
            x_out[i, :, pl.ds(at, LANES)] += kept[i * rows : (i + 1) * rows]


def finish(x_in, gain_out, spread_out):
    columns = gain_out.shape[1]
    gain_out[...] = swap_lanes(
        jnp.concatenate([x_in[i, :, columns:] for i in range(SIDE)], axis=1)
    )
    spread_out[...] = (x_in[0, :, 0:columns] + x_in[1, :, 0:columns]) + (
        x_in[2, :, 0:columns] + x_in[3, :, 0:columns]
    )


WHOLE = pl.BlockSpec()
UNREAD = pl.BlockSpec(memory_space=pl.ANY)
SMEM = pl.BlockSpec(memory_space=pltpu.SMEM)


def far(*arrays):
    return [pltpu.with_memory_space_constraint(a, pltpu.HBM) for a in arrays]


def call(kernel, scalars, arrays, outs, scratch=(), flops=0, unread=(), coarse=()):
    shapes = [pltpu.HBM(s, F32) for s in outs] + [pltpu.HBM(s, jnp.bfloat16) for s in coarse]
    size = sum(a.size for a in arrays) + sum(math.prod(s) for s in outs)
    return pl.pallas_call(
        kernel,
        out_shape=shapes,
        in_specs=[SMEM] * len(scalars) + [WHOLE] * len(arrays) + [UNREAD] * len(unread),
        out_specs=[WHOLE] * len(shapes),
        scratch_shapes=[pltpu.VMEM(s, F32) for s in scratch],
        compiler_params=pltpu.CompilerParams(vmem_limit_bytes=24 * 2**20),
        cost_estimate=pl.CostEstimate(flops=flops, bytes_accessed=4 * size, transcendentals=0),
    )(*scalars, *arrays, *unread)


def shifted(block, distance):
    count = lax.axis_size("tm")
    return lax.ppermute(block, "tm", [(i + distance, i) for i in range(count - distance)])


def swap(message, axis):
    return lax.all_to_all(message, axis, 0, 0)


def ring(block, axis):
    pieces = [block]
    for step in STEPS[1:]:
        pieces.append(lax.ppermute(block, axis, [(i, (i + step) % SIDE) for i in range(SIDE)]))
    return pieces


def ring_shifted(block, distance):
    count = lax.axis_size("tm")
    pieces = []
    for step in STEPS:
        route = [
            ((i + distance) * SIDE + j, i * SIDE + (j + step) % SIDE)
            for i in range(count - distance)
            for j in range(SIDE)
        ]
        pieces.append(lax.ppermute(block, ("tm", "y"), route))
    return pieces


def body(covariance, precision, band_weight, band_offset, prior_mean, innovation, seen_sites):
    own = covariance[0]
    inverse = precision[0]
    weights = band_weight[0]
    rows, columns = own.shape
    panel = SIDE * rows
    at_t = lax.axis_index("tm")
    count_t = lax.axis_size("tm")
    at_x = lax.axis_index("x")
    where = jnp.stack(
        [
            lax.axis_index("y").astype(jnp.int32),
            at_x.astype(jnp.int32),
            (at_t + 1 < count_t).astype(jnp.int32),
            (at_t + 2 < count_t).astype(jnp.int32),
        ]
    )
    unit = 2 * panel * panel * columns

    (y_message,) = call(
        first_message,
        (),
        far(own, inverse, prior_mean, innovation, seen_sites),
        ((SIDE, 2 * rows + 8, columns),),
    )
    y_in = swap(y_message, "y")
    (crossed,) = call(cross, (band_offset,), far(own, weights), ((rows, columns),))
    crossed_pieces = ring(crossed, "x")
    gain, crossed_block, x_message = call(
        first_gain,
        (where,),
        (y_in, *far(*crossed_pieces)),
        ((panel, panel), (panel, panel), (SIDE, panel + 8, panel)),
        ((panel, columns),),
        unit,
    )
    gain_in = swap(x_message, "x")
    later_pieces = ring_shifted(gain, 1)
    gain_2, x_message, shift, c_message, wide_high, wide_low = call(
        second_gain,
        (where, band_offset),
        (*far(weights, gain), gain_in, *far(*later_pieces), y_in),
        ((panel, panel), (SIDE, panel, panel), (8, panel), (panel + 8, columns)),
        ((columns, panel),),
        unit,
        coarse=((panel, columns),) * 2,
    )
    gain_2_in = swap(x_message, "x")
    gain_pieces = ring(gain, "y")
    gain_2_later = shifted(gain_2, 2)
    c_in = shifted(c_message, 1)
    next_offsets = c_in[panel + NBAND + 2, 0:8].astype(jnp.int32)
    later_rows, *later_halves = call(
        later_inputs, (next_offsets,), far(c_in), ((8, columns),), coarse=((panel, columns),) * 4
    )
    part, gain_2_pair, wide_2_high, wide_2_low = call(
        first_spread,
        (where,),
        (
            *far(wide_high, wide_low), gain_2_in, *far(*later_halves, crossed_block),
            *far(own, gain, *gain_pieces[1:], gain_2, gain_2_later),
        ),
        ((SIDE, panel, panel), (2 * panel, panel)),
        ((columns, panel),),
        3 * unit,
        coarse=((panel, columns),) * 2,
    )
    (shift_2,) = call(
        later_shift,
        (where,),
        far(wide_high, wide_low, wide_2_high, wide_2_low, later_rows, shift),
        ((8, panel),),
    )
    wide_high, wide_low = wide_2_high, wide_2_low
    parts = swap(part, "x")
    gain_2_pieces = ring(gain_2_pair, "y")
    (spread_2,) = call(join_spread, (), (parts, *far(shift_2)), ((panel + 8, panel),))
    later = shifted(spread_2, 2)
    (y_message,) = call(
        four_times, (), (later,), ((SIDE, panel + 8, panel),), unread=gain_2_pieces[1:]
    )
    y_in = swap(y_message, "y")
    gain_4, tall_high, tall_low = call(
        third_gain,
        (where,),
        far(gain_2, wide_high, wide_low, *gain_2_pieces),
        ((panel, panel),),
        ((columns, panel),),
        unit,
        coarse=((columns, panel),) * 2,
    )
    x_message, shift_4 = call(
        second_spread,
        (where,),
        (*far(gain_4, wide_high, wide_low, tall_high, tall_low, spread_2), y_in),
        ((SIDE, rows, columns + panel), (8, panel)),
        ((columns, panel),),
        2 * unit,
    )
    last_in = swap(x_message, "x")
    final_gain, final_spread = call(finish, (), (last_in,), ((rows, columns), (rows, columns)))
    final_shift = lax.dynamic_slice_in_dim(shift_4[0], at_x * rows, rows, 0)
    return final_gain[None], final_shift[None], final_spread[None]


def solution(mesh):
    count = mesh.devices.shape[0]
    grid = Mesh(mesh.devices.reshape(count, SIDE, SIDE), ("tm", "y", "x"))
    row = ("y", "x")
    in_specs = (
        P("tm", row, None),
        P("tm", row, None),
        P("tm", None, None),
        P("tm", None),
        P("tm", row),
        P("tm", None),
        P("tm", None),
    )
    out_specs = (P("tm", row, None), P("tm", row), P("tm", row, None))
    return jax.shard_map(body, mesh=grid, in_specs=in_specs, out_specs=out_specs, check_vma=False)
```

```python
import math

import jax
import jax.numpy as jnp
from jax import lax
from jax.experimental import pallas as pl
from jax.experimental.pallas import tpu as pltpu
from jax.sharding import Mesh, PartitionSpec as P

NBAND = 5
SIDE = 4

HIGHEST = lax.Precision.HIGHEST
F32 = jnp.float32


def halves(array):
    high = array.astype(jnp.bfloat16)
    return high, (array - high.astype(F32)).astype(jnp.bfloat16)


def three(left, right, contract):
    def one(first, second):
        return lax.dot_general(first, second, (contract, ((), ())), preferred_element_type=F32)

    left_high, left_low = left
    right_high, right_low = right
    return one(left_high, right_high) + (one(left_high, right_low) + one(left_low, right_high))


def dot_t(left, right):
    return three(halves(left), halves(right), ((1,), (1,)))


def exact_dot_t(left, right):
    return lax.dot_general(
        left, right, (((1,), (1,)), ((), ())), precision=HIGHEST, preferred_element_type=F32
    )


def vector_times(row, matrix):
    return exact_dot_t(jnp.broadcast_to(row, (8, row.shape[1])), matrix)[0:1]


def row_times(row, matrix_halves):
    whole = jnp.broadcast_to(row, (8, row.shape[1]))
    return three(halves(whole), matrix_halves, ((1,), (1,)))[0:1]


LANES = 128


def tiles(array):
    return [array[:, i : i + LANES] for i in range(0, array.shape[1], LANES)]


def low_lanes(rows, width):
    return lax.broadcasted_iota(jnp.int32, (rows, LANES), 1) < width


def swap_tiles(blocks):
    width = LANES // 2
    low = low_lanes(blocks[0].shape[0], width)
    rolled = [pltpu.roll(block, width, 1) for block in blocks]
    out = []
    for b in range(SIDE):
        for half in range(SIDE // 2):
            ends = []
            for side in range(2):
                at = (2 * half + side) * SIDE + b
                ends.append((blocks if at % 2 == side else rolled)[at // 2])
            out.append(jnp.where(low, ends[0], ends[1]))
    return out


def swap_lanes(array):
    return jnp.concatenate(swap_tiles(tiles(array)), axis=1)


def band_tiles(blocks, weights, offset_at):
    rows = blocks[0].shape[0]
    width = LANES // 2
    low = low_lanes(rows, width)
    zero = jnp.zeros((rows, LANES), F32)
    turned = [zero] + [pltpu.roll(block, width, 1) for block in blocks] + [zero]
    moved = [jnp.where(low, turned[i], turned[i + 1]) for i in range(len(blocks) + 1)]
    totals = [zero] * len(blocks)
    for b in range(NBAND):
        distance = offset_at(b) + width
        near = low_lanes(rows, LANES - distance)
        back = lax.rem(LANES - distance, LANES)
        rolled = [pltpu.roll(block, back, 1) for block in moved]
        for i in range(len(blocks)):
            weight = weights[b : b + 1, i * LANES : (i + 1) * LANES]
            totals[i] = totals[i] + weight * jnp.where(near, rolled[i], rolled[i + 1])
    return totals


def bands(array, weights, offset_at):
    return jnp.concatenate(band_tiles(tiles(array), weights, offset_at), axis=1)


def wide(ref, rows):
    return jnp.concatenate([ref[i, 0:rows, :] for i in range(SIDE)], axis=1)


STEPS = (0, 1, 3, 2)


def sources(pieces, at):
    return [(piece, lax.rem(at + SIDE - step, SIDE)) for piece, step in zip(pieces, STEPS)]


def place_tall(pieces, at_y, out_ref, row0=0):
    panel = out_ref.shape[0] // SIDE
    chunk = panel // SIDE
    for piece, source in sources(pieces, at_y):
        for b in range(SIDE):
            out_ref[pl.ds(pl.multiple_of(b * panel + source * chunk, chunk), chunk), :] = piece[
                row0 + b * chunk : row0 + (b + 1) * chunk, :
            ]


def first_message(own, inverse, prior, innovation, sites, y_out):
    rows, columns = own.shape
    matrix = own[...]
    state = lax.broadcasted_iota(jnp.int32, (columns, sites.shape[1]), 0)
    matches = (state == sites[...]).astype(F32)
    pulled = vector_times(innovation[...], matches)
    filtered = prior[...] + vector_times(pulled, matrix)
    for i in range(SIDE):
        y_out[i, 0:rows, :] = inverse[...]
        y_out[i, rows : 2 * rows, :] = matrix
        y_out[i, 2 * rows :, :] = jnp.zeros((8, columns), F32)
        y_out[i, 2 * rows : 2 * rows + 1, 0:rows] = filtered


def cross(offsets, own, weights, crossed_out):
    crossed_out[...] = bands(own[...], weights[...], lambda b: offsets[0, b])


def place_rows(pieces, at, out):
    rows = pieces[0].shape[0]
    for piece, source in sources(pieces, at):
        out[pl.ds(pl.multiple_of(source * rows, rows), rows), :] = piece[...]


def pick_chunks(ref, at_x):
    panel = ref.shape[0]
    odd = lax.rem(at_x, 2)
    base = lax.div(at_x, 2) * LANES
    low = low_lanes(panel, LANES // 2)
    parts = []
    for i in range(SIDE):
        part = ref[:, pl.ds(pl.multiple_of(i * panel + base, LANES), LANES)]
        turn = odd if i % 2 == 0 else 1 - odd
        parts.append(pltpu.roll(part, turn * (LANES // 2), 1))
    return jnp.where(low, parts[0], parts[1]), jnp.where(low, parts[2], parts[3])


def first_gain(where, y_in, x0, x1, x2, x3, gain_out, block_out, x_out, crossed):
    rows = x0.shape[0]
    panel = SIDE * rows
    place_rows((x0, x1, x2, x3), where[1], crossed)
    inverse = jnp.concatenate([y_in[i, 0:rows, :] for i in range(SIDE)], axis=0)
    gain = dot_t(crossed[...], inverse)
    gain_out[...] = gain
    tail = jnp.concatenate(
        [y_in[i, 2 * rows : 2 * rows + 1, 0:rows] for i in range(SIDE)], axis=1
    )
    tail = jnp.broadcast_to(tail, (8, panel))
    for i in range(SIDE):
        x_out[i, 0:panel, :] = gain
        x_out[i, panel:, :] = tail
    first, second = pick_chunks(crossed, where[1])
    block_out[:, 0:LANES] = first
    block_out[:, LANES:] = second


def second_gain(
    where, offsets, weights, gain, x_in, e0, e1, e2, e3, y_in,
    gain_out, x_out, shift_out, c_out, high_out, low_out, tall,
):
    panel = gain.shape[0]
    at_y = where[0]
    gain_wide = halves(wide(x_in, panel))
    high_out[...] = gain_wide[0]
    low_out[...] = gain_wide[1]
    place_tall((e0, e1, e2, e3), at_y, tall)
    product = three(gain_wide, halves(tall[...]), ((1,), (0,)))
    gain_2 = jnp.where(where[2] == 1, product, gain[...])
    gain_out[...] = gain_2
    for i in range(SIDE):
        x_out[i] = gain_2
    filtered = jnp.concatenate([x_in[i, panel : panel + 8, :] for i in range(SIDE)], axis=1)
    natural = swap_lanes(filtered)
    forward = swap_lanes(bands(natural, weights[...], lambda b: offsets[0, b]))
    mine = jnp.zeros((1, panel), F32)
    for i in range(SIDE):
        mine = mine + jnp.where(at_y == i, natural[0:1, i * panel : (i + 1) * panel], 0.0)
    shift_out[...] = jnp.broadcast_to(mine - row_times(forward[0:1], gain_wide), (8, panel))
    rows = panel // SIDE
    for i in range(SIDE):
        c_out[i * rows : (i + 1) * rows, :] = y_in[i, rows : 2 * rows, :]
    c_out[panel : panel + NBAND, :] = weights[...]
    c_out[panel + NBAND : panel + NBAND + 1, :] = filtered[0:1]
    c_out[panel + NBAND + 1 : panel + NBAND + 2, :] = forward[0:1]
    lane = lax.broadcasted_iota(jnp.int32, (1, c_out.shape[1]), 1)
    held = jnp.zeros((1, c_out.shape[1]), jnp.int32)
    for b in range(NBAND):
        held = jnp.where(lane == b, offsets[0, b], held)
    c_out[panel + NBAND + 2 : panel + NBAND + 3, :] = held.astype(F32)


def later_inputs(offsets, c_in, rows_out, own_high, own_low, crossed_high, crossed_low):
    panel, columns = own_high.shape
    matrix = c_in[0:panel, :]
    weights = c_in[panel : panel + NBAND, :]
    rows_out[...] = c_in[panel:, :]
    high, low = halves(matrix)
    reach = 3 * LANES
    ahead = (
        lax.broadcasted_iota(jnp.int32, (reach, LANES), 0)
        - lax.broadcasted_iota(jnp.int32, (reach, LANES), 1)
        - LANES
    )
    count = columns // LANES
    crossed = []
    for i in range(count):
        first = max(i - 1, 0)
        last = min(i + 2, count)
        spread = jnp.zeros((reach, LANES), F32)
        for b in range(NBAND):
            weight = weights[b : b + 1, i * LANES : (i + 1) * LANES]
            spread = spread + jnp.where(ahead == offsets[b], weight, 0.0)
        spread = spread[(first - i + 1) * LANES : (last - i + 1) * LANES]
        lanes = slice(first * LANES, last * LANES)
        crossed.append(three((high[:, lanes], low[:, lanes]), halves(spread), ((1,), (0,))))
    for blocks, high_out, low_out in (
        (tiles(matrix), own_high, own_low),
        (crossed, crossed_high, crossed_low),
    ):
        for i, block in enumerate(swap_tiles(blocks)):
            high, low = halves(block)
            high_out[:, i * LANES : (i + 1) * LANES] = high
            low_out[:, i * LANES : (i + 1) * LANES] = low


def first_spread(
    where, wide_high, wide_low, gain_2_in, own_high, own_low, crossed_high, crossed_low,
    block, own, e0, e1, e2, e3, gain_2, gain_2_later,
    part_out, pair_out, high_out, low_out, tall,
):
    panel = e0.shape[0]
    at_y = where[0]
    pair_out[0:panel, :] = gain_2[...]
    pair_out[panel:, :] = gain_2_later[...]
    gain_wide = (wide_high[...], wide_low[...])
    gain_2_wide = halves(wide(gain_2_in, panel))
    high_out[...] = gain_2_wide[0]
    low_out[...] = gain_2_wide[1]
    across = ((1,), (1,))
    turned = three(gain_wide, (own_high[...], own_low[...]), across) - three(
        gain_2_wide, (crossed_high[...], crossed_low[...]), across
    )
    inside = where[2] == 1
    turned = halves(jnp.where(inside, turned, 0.0) - block[...])
    place_tall((e0, e1, e2, e3), at_y, tall)
    twice = jnp.concatenate(swap_tiles(tiles(jnp.concatenate([own[...]] * 2, axis=0))), axis=1)
    mine = low_lanes(panel, LANES // 2) == (lax.rem(where[1], 2) == 0)
    at_x = pl.multiple_of(lax.div(where[1], 2) * LANES, LANES)
    for i in range(SIDE):
        part_out[i] = three(halves(tall[i * panel : (i + 1) * panel, :]), turned, across)
        turned_own = twice[:, i * panel : (i + 1) * panel].T
        part_out[i, :, pl.ds(at_x, LANES)] += jnp.where(mine, turned_own, 0.0)


def later_shift(where, high, low, high_2, low_2, later_rows, shift, out):
    moved = row_times(later_rows[NBAND : NBAND + 1, :], (high[...], low[...])) - row_times(
        later_rows[NBAND + 1 : NBAND + 2, :], (high_2[...], low_2[...])
    )
    out[...] = shift[...] + jnp.where(where[2] == 1, moved, 0.0)


def join_spread(parts, shift, out):
    panel = parts.shape[1]
    out[0:panel, :] = ((parts[0] + parts[1]) + (parts[2] + parts[3])).T
    out[panel:, :] = shift[...]


def four_times(block, p1, p2, p3, out):
    for i in range(SIDE):
        out[i] = block[...]


def third_gain(where, gain_2, wide_high, wide_low, a0, a1, a2, a3, gain_out, high_out, low_out, tall):
    panel = gain_2.shape[0]
    at_y = where[0]
    pieces = (a0, a1, a2, a3)
    place_tall(pieces, at_y, tall, panel)
    product = three((wide_high[...], wide_low[...]), halves(tall[...]), ((1,), (0,)))
    gain_out[...] = jnp.where(where[3] == 1, product, gain_2[...])
    for piece, source in sources(pieces, at_y):
        at = pl.ds(pl.multiple_of(source * panel, panel), panel)
        high_out[at, :], low_out[at, :] = halves(piece[0:panel, :])


def second_spread(
    where, gain_4, wide_high, wide_low, tall_high, tall_low, spread, y_in, x_out, shift_out, tall
):
    panel = gain_4.shape[0]
    rows = panel // SIDE
    columns = SIDE * panel
    inside = where[3] == 1
    gain_2_wide = (wide_high[...], wide_low[...])
    for i in range(SIDE):
        for b in range(SIDE):
            tall[b * panel + i * rows : b * panel + (i + 1) * rows, :] = y_in[
                i, b * rows : (b + 1) * rows, :
            ]
    turned = three(gain_2_wide, halves(tall[...]), ((1,), (0,)))
    turned = halves(jnp.where(inside, turned, 0.0))
    shifts = jnp.concatenate([y_in[i, panel : panel + 8, :] for i in range(SIDE)], axis=1)
    moved = row_times(swap_lanes(shifts)[0:1], gain_2_wide)
    shift_out[...] = spread[panel:, :] + jnp.where(inside, moved, 0.0)
    for i in range(SIDE):
        x_out[i, :, columns : columns + panel] = gain_4[i * rows : (i + 1) * rows, :]
    part = three(turned, (tall_high[...], tall_low[...]), ((1,), (1,)))
    for i in range(SIDE):
        x_out[i, :, 0:columns] = part[i * rows : (i + 1) * rows]
    odd = lax.rem(where[1], 2)
    base = lax.div(where[1], 2) * LANES
    mine = low_lanes(panel, LANES // 2) == (odd == 0)
    for c in range(SIDE):
        kept = spread[0:panel, (c // 2) * LANES : (c // 2 + 1) * LANES]
        turn = odd if c % 2 == 0 else 1 - odd
        kept = jnp.where(mine, pltpu.roll(kept, turn * (LANES // 2), 1), 0.0)
        at = pl.multiple_of(c * panel + base, LANES)
        for i in range(SIDE):
            x_out[i, :, pl.ds(at, LANES)] += kept[i * rows : (i + 1) * rows]


def finish(x_in, gain_out, spread_out):
    columns = gain_out.shape[1]
    gain_out[...] = swap_lanes(
        jnp.concatenate([x_in[i, :, columns:] for i in range(SIDE)], axis=1)
    )
    spread_out[...] = (x_in[0, :, 0:columns] + x_in[1, :, 0:columns]) + (
        x_in[2, :, 0:columns] + x_in[3, :, 0:columns]
    )


WHOLE = pl.BlockSpec()
UNREAD = pl.BlockSpec(memory_space=pl.ANY)
SMEM = pl.BlockSpec(memory_space=pltpu.SMEM)


def far(*arrays):
    return [pltpu.with_memory_space_constraint(a, pltpu.HBM) for a in arrays]


def call(kernel, scalars, arrays, outs, scratch=(), flops=0, unread=(), coarse=()):
    shapes = [pltpu.HBM(s, F32) for s in outs] + [pltpu.HBM(s, jnp.bfloat16) for s in coarse]
    size = sum(a.size for a in arrays) + sum(math.prod(s) for s in outs)
    return pl.pallas_call(
        kernel,
        out_shape=shapes,
        in_specs=[SMEM] * len(scalars) + [WHOLE] * len(arrays) + [UNREAD] * len(unread),
        out_specs=[WHOLE] * len(shapes),
        scratch_shapes=[pltpu.VMEM(s, F32) for s in scratch],
        compiler_params=pltpu.CompilerParams(vmem_limit_bytes=24 * 2**20),
        cost_estimate=pl.CostEstimate(flops=flops, bytes_accessed=4 * size, transcendentals=0),
    )(*scalars, *arrays, *unread)


def shifted(block, distance):
    count = lax.axis_size("tm")
    return lax.ppermute(block, "tm", [(i + distance, i) for i in range(count - distance)])


def swap(message, axis):
    return lax.all_to_all(message, axis, 0, 0)


def ring(block, axis):
    pieces = [block]
    for step in STEPS[1:]:
        pieces.append(lax.ppermute(block, axis, [(i, (i + step) % SIDE) for i in range(SIDE)]))
    return pieces


def ring_shifted(block, distance):
    count = lax.axis_size("tm")
    pieces = []
    for step in STEPS:
        route = [
            ((i + distance) * SIDE + j, i * SIDE + (j + step) % SIDE)
            for i in range(count - distance)
            for j in range(SIDE)
        ]
        pieces.append(lax.ppermute(block, ("tm", "y"), route))
    return pieces


def body(covariance, precision, band_weight, band_offset, prior_mean, innovation, seen_sites):
    own = covariance[0]
    inverse = precision[0]
    weights = band_weight[0]
    rows, columns = own.shape
    panel = SIDE * rows
    at_t = lax.axis_index("tm")
    count_t = lax.axis_size("tm")
    at_x = lax.axis_index("x")
    where = jnp.stack(
        [
            lax.axis_index("y").astype(jnp.int32),
            at_x.astype(jnp.int32),
            (at_t + 1 < count_t).astype(jnp.int32),
            (at_t + 2 < count_t).astype(jnp.int32),
        ]
    )
    unit = 2 * panel * panel * columns

    (y_message,) = call(
        first_message,
        (),
        far(own, inverse, prior_mean, innovation, seen_sites),
        ((SIDE, 2 * rows + 8, columns),),
    )
    y_in = swap(y_message, "y")
    (crossed,) = call(cross, (band_offset,), far(own, weights), ((rows, columns),))
    crossed_pieces = ring(crossed, "x")
    gain, crossed_block, x_message = call(
        first_gain,
        (where,),
        (y_in, *far(*crossed_pieces)),
        ((panel, panel), (panel, panel), (SIDE, panel + 8, panel)),
        ((panel, columns),),
        unit,
    )
    gain_in = swap(x_message, "x")
    later_pieces = ring_shifted(gain, 1)
    gain_2, x_message, shift, c_message, wide_high, wide_low = call(
        second_gain,
        (where, band_offset),
        (*far(weights, gain), gain_in, *far(*later_pieces), y_in),
        ((panel, panel), (SIDE, panel, panel), (8, panel), (panel + 8, columns)),
        ((columns, panel),),
        unit,
        coarse=((panel, columns),) * 2,
    )
    gain_2_in = swap(x_message, "x")
    gain_pieces = ring(gain, "y")
    gain_2_later = shifted(gain_2, 2)
    c_in = shifted(c_message, 1)
    next_offsets = c_in[panel + NBAND + 2, 0:8].astype(jnp.int32)
    later_rows, *later_halves = call(
        later_inputs, (next_offsets,), (c_in,), ((8, columns),), coarse=((panel, columns),) * 4
    )
    part, gain_2_pair, wide_2_high, wide_2_low = call(
        first_spread,
        (where,),
        (
            *far(wide_high, wide_low), gain_2_in, *far(*later_halves, crossed_block),
            *far(own, gain, *gain_pieces[1:], gain_2, gain_2_later),
        ),
        ((SIDE, panel, panel), (2 * panel, panel)),
        ((columns, panel),),
        3 * unit,
        coarse=((panel, columns),) * 2,
    )
    (shift_2,) = call(
        later_shift,
        (where,),
        far(wide_high, wide_low, wide_2_high, wide_2_low, later_rows, shift),
        ((8, panel),),
    )
    wide_high, wide_low = wide_2_high, wide_2_low
    parts = swap(part, "x")
    gain_2_pieces = ring(gain_2_pair, "y")
    (spread_2,) = call(join_spread, (), (parts, *far(shift_2)), ((panel + 8, panel),))
    later = shifted(spread_2, 2)
    (y_message,) = call(
        four_times, (), (later,), ((SIDE, panel + 8, panel),), unread=gain_2_pieces[1:]
    )
    y_in = swap(y_message, "y")
    gain_4, tall_high, tall_low = call(
        third_gain,
        (where,),
        far(gain_2, wide_high, wide_low, *gain_2_pieces),
        ((panel, panel),),
        ((columns, panel),),
        unit,
        coarse=((columns, panel),) * 2,
    )
    x_message, shift_4 = call(
        second_spread,
        (where,),
        (*far(gain_4, wide_high, wide_low, tall_high, tall_low, spread_2), y_in),
        ((SIDE, rows, columns + panel), (8, panel)),
        ((columns, panel),),
        2 * unit,
    )
    last_in = swap(x_message, "x")
    final_gain, final_spread = call(finish, (), (last_in,), ((rows, columns), (rows, columns)))
    final_shift = lax.dynamic_slice_in_dim(shift_4[0], at_x * rows, rows, 0)
    return final_gain[None], final_shift[None], final_spread[None]


def solution(mesh):
    count = mesh.devices.shape[0]
    grid = Mesh(mesh.devices.reshape(count, SIDE, SIDE), ("tm", "y", "x"))
    row = ("y", "x")
    in_specs = (
        P("tm", row, None),
        P("tm", row, None),
        P("tm", None, None),
        P("tm", None),
        P("tm", row),
        P("tm", None),
        P("tm", None),
    )
    out_specs = (P("tm", row, None), P("tm", row), P("tm", row, None))
    return jax.shard_map(body, mesh=grid, in_specs=in_specs, out_specs=out_specs, check_vma=False)
```
